512 devices in a mesh: member: 16 (over y, x), space: 32 (over z, core).
Axes of the slice: x: 4, y: 4, z: 16, core: 2. Of those that a mesh axis runs over, the one named last changes fastest.
Arguments:
- air_ensemble: bfloat16 [16, 128, 360, 384], P('member', 'space'), may hold values from -12 to 12
- sea_indicator: int32 [128, 360], P('space'), may hold values 0 or 1
- layernorm_scaling: float32 [384], replicated, may hold values from 0.5 to 1.5
- harmonic_damping_factor: float32 [128, 384], replicated, may hold values from -4 to 4
- bypass_factor: bfloat16 [384, 384], replicated, may hold values from -0.3125 to 0.3125
- core_exit_factor: bfloat16 [384, 384], replicated, may hold values from -0.3125 to 0.3125
- air_to_exchange_factor: bfloat16 [384, 8], replicated, may hold values from -0.3125 to 0.3125
- sea_heat_imprint: float32 [384], replicated, may hold values from -4 to 4
- sea_ensemble_arrays: bfloat16 [16, 512, 76, 128], P('member', 'space'), may hold values from -6 to 6
- input_to_hidden_kernel: bfloat16 [9, 200, 84], replicated, may hold values from -0.21875 to 0.21875
- hidden_to_change_kernel: bfloat16 [9, 200], replicated, may hold values from -0.125 to 0.125
- patch_exchange_pick: int32 [448, 128], P('space'), may hold values from 0 to 1439
- node_sea_pick: int32 [128, 360], P('space'), may hold values from 0 to 1791
- patch_holder_shift: int32 [448, 1], P('space'), may hold values from 0 to 7; in each aligned block of 14 rows (0 to 13, 14 to 27, ...) at most 2 rows name the same one
- wet_depth_layers: int32 [448], P('space'), may hold values from 1 to 19
Outputs:
- atmos_out: bfloat16 [16, 128, 360, 384], P('member', 'space')
- sst_mean: float32 [128, 360], P('space')
The draws below stay inside these ranges and needn't reach their ends.
Inputs may be any that keep to these rules, and one draw needn't show every extreme that they name: `patch_holder_shift`: among the 14 tiles of one band (aligned blocks of rows), no offset is named more than 2 times, a bound that some block reaches. Slots of sea_ensemble_arrays that no tile maps to are never read.
All inputs are finite; a program needn't handle non-finite values. No bound on the sum of `sea_indicator` on one device may be relied on, other than what follows from the above.
Results may differ from the reference program's by a relative error of at most 0.0075.
Values may be sent and summed in bfloat16 or wider, within the bound.
No kernel may reach another device: no remote copies, remote signals or barrier semaphores. Data moves between devices by JAX's collectives and lax.ppermute only.
A program may use at most 64 MiB of HBM per device.

```python
import math
import jax
import jax.numpy as jnp
import numpy as np
from jax import lax

HARMONIC_CHANS = 384
MERIDIAN_TOTAL = 360
MMAX = 128
LMAX = 128
FC = 8
LEV = 19
HID = 200
CAP = 2
NEAR = 8
HOME_DEV = 14
LAT_DEV = 4
BANDS = 32
MEMBERS = 16
PARALLEL_TOTAL = 128
OCH = 76
NTILES = 448
OWN_SLOTS = 16
SLOTS = 512


def draw_air_ensemble(key, part):
    key = jax.random.fold_in(key, 11)
    keys = jax.random.split(key, 2)
    channel_scale = jnp.exp(jax.random.uniform(keys[0], (HARMONIC_CHANS,), jnp.float32, math.log(0.3), math.log(3.0)))
    base = jnp.clip(jax.random.normal(keys[1], (MEMBERS, PARALLEL_TOTAL, MERIDIAN_TOTAL, HARMONIC_CHANS), jnp.float32), -4.0, 4.0)
    return (base * channel_scale).astype(jnp.bfloat16)


def touch_ends(array, own_key, least, top_value):
    longest = array.shape.index(max(array.shape))
    spots = []
    for shift in (0, 1):
        where = [jax.random.randint(jax.random.fold_in(own_key, axis), (), 0, length) for axis, length in enumerate(array.shape)]
        where[longest] = (where[longest] + shift) % array.shape[longest]
        spots.append(tuple(where))
    return array.at[spots[0]].set(least).at[spots[1]].set(top_value)


def block_levels(rng, extent, cuts, low, high):
    def one(axis_at, blocks):
        steps = jax.random.uniform(jax.random.fold_in(jax.random.fold_in(rng, 6), axis_at), (blocks,), jnp.float32, low / len(cuts), high / len(cuts))
        return jnp.repeat(jnp.exp(steps), extent[axis_at] // blocks).reshape((-1,) + (1,) * (len(extent) - axis_at - 1))

    loudness = one(*cuts[0])
    for cut in cuts[1:]:
        loudness = loudness * one(*cut)
    return loudness


def shared_out(own_key, own, number, rows, number_of, top, bound, lean):
    sequence = jax.random.permutation(own_key, number_of)
    packed, usual = shares(number_of, rows * top, bound, lean, True), shares(number_of, rows * top, bound, lean, False)
    places = jnp.arange(number_of)

    def named(sizes, turn):
        used = int((sizes > 0).sum())
        fixed = max(1, used // 4)
        passed = fixed + (places - fixed + turn * (used - fixed)) % max(1, number_of - fixed)
        return jnp.zeros((number_of,), jnp.int32).at[sequence[jnp.where(places < fixed, places, passed)]].set(jnp.asarray(sizes, jnp.int32))

    sizes = jnp.where(number % 4 == 0, named(packed, number // 4), named(usual, number - number // 4 - 1))
    mixed = jax.random.permutation(jax.random.fold_in(own, 3), number_of)
    source_of, sink = mixed[0:number_of // 2 * 2:2], mixed[1:number_of // 2 * 2:2]
    slack = jnp.minimum(sizes[source_of] - 1, bound - sizes[sink]) // 2
    slack = jnp.where((source_of == sequence[0]) | (sink == sequence[0]) | (sizes[sink] == 0), 0, jnp.maximum(slack, 0))
    passed = jax.random.randint(jax.random.fold_in(own, 4), (number_of // 2,), 0, 1 << 20) % (slack + 1)
    sizes = sizes.at[source_of].add(-passed).at[sink].add(passed)
    items = jnp.searchsorted(jnp.cumsum(sizes), jnp.arange(rows * top), side="right").astype(jnp.int32)
    listing = items.reshape(top, rows).T
    listing = listing[jax.random.permutation(jax.random.fold_in(own, 1), rows)]
    turn = jax.random.randint(jax.random.fold_in(own, 2), (rows, 1), 0, top)
    return jnp.take_along_axis(listing, (jnp.arange(top)[None, :] + turn) % top, axis=1)


def shares(count, total, limit, skew, full):
    portions = [(1 << 20) // math.isqrt(standing ** skew) + 1 for standing in range(1, count + 1)]
    largest = limit if full else min(limit, max(-(-total // count), total * portions[0] // sum(portions)))
    least = 1 if total - largest >= count - 1 else 0
    counts, rest = [largest] + [least] * (count - 1), total - largest - least * (count - 1)
    while rest > 0:
        candidates = [i for i in range(1, count) if counts[i] < largest] or [i for i in range(1, count) if counts[i] < limit]
        pool, left = sum([portions[i] for i in candidates]), rest
        for i in candidates:
            more = min(limit - counts[i], max(1, left * portions[i] // pool), rest)
            counts[i] = counts[i] + more
            rest = rest - more
    return np.array(counts)


def scatter_about(own_key, dims, scale, limit, pieces=(), kind=jnp.bfloat16):
    loudness = block_levels(own_key, dims, pieces, -0.22, 0.18) if pieces else 1.0
    drawn = jax.random.normal(own_key, dims, jnp.float32) * scale * loudness
    return jnp.minimum(jnp.maximum(drawn, -limit), limit).astype(kind)


def setup_inputs(seed: int = 0) -> dict:
    arg_keys = jax.random.split(jax.random.key(seed), 16)
    air_ensemble = draw_air_ensemble(jax.random.fold_in(arg_keys[15], 71), 0)
    sea_indicator = touch_ends((jax.random.randint(arg_keys[1], (PARALLEL_TOTAL, MERIDIAN_TOTAL), 0, 3) < 2).astype(jnp.int32), jax.random.fold_in(arg_keys[1], 1), 0, 1)
    layernorm_scaling = jnp.clip(1.0 + 0.1 * jax.random.normal(arg_keys[2], (HARMONIC_CHANS,), jnp.float32), 0.5, 1.5)
    harmonic_damping_factor = scatter_about(arg_keys[3], (LMAX, HARMONIC_CHANS), 1.0, 4.0, (), jnp.float32)
    bypass_factor = scatter_about(arg_keys[4], (HARMONIC_CHANS, HARMONIC_CHANS), HARMONIC_CHANS ** -0.5, 0.3125)
    core_exit_factor = scatter_about(arg_keys[5], (HARMONIC_CHANS, HARMONIC_CHANS), HARMONIC_CHANS ** -0.5, 0.3125)
    air_to_exchange_factor = scatter_about(arg_keys[6], (HARMONIC_CHANS, FC), HARMONIC_CHANS ** -0.5, 0.3125)
    sea_heat_imprint = scatter_about(arg_keys[7], (HARMONIC_CHANS,), 1.0, 4.0, (), jnp.float32)
    sea_ensemble_arrays = scatter_about(arg_keys[8], (MEMBERS, SLOTS, OCH, 128), 1.0, 6.0, ((0, 16), (1, 32)))
    input_to_hidden_kernel = scatter_about(arg_keys[9], (9, HID, OCH + FC), (9 * (OCH + FC)) ** -0.5, 0.21875)
    hidden_to_change_kernel = scatter_about(arg_keys[10], (9, HID), (9 * HID) ** -0.5, 0.125)
    patch_exchange_pick = touch_ends(jax.random.randint(arg_keys[11], (NTILES, 128), 0, LAT_DEV * MERIDIAN_TOTAL), jax.random.fold_in(arg_keys[11], 1), 0, (LAT_DEV * MERIDIAN_TOTAL) - 1).astype(jnp.int32)
    node_sea_pick = touch_ends(jax.random.randint(arg_keys[12], (PARALLEL_TOTAL, MERIDIAN_TOTAL), 0, HOME_DEV * 128), jax.random.fold_in(arg_keys[12], 1), 0, (HOME_DEV * 128) - 1).astype(jnp.int32)
    patch_holder_shift_keys = jax.random.split(jax.random.fold_in(arg_keys[13], 1), NTILES // HOME_DEV)
    patch_holder_shift_turns = jax.random.permutation(jax.random.fold_in(arg_keys[13], 3), NTILES // HOME_DEV)
    patch_holder_shift = jax.vmap(lambda own, number: shared_out(jax.random.fold_in(arg_keys[13], 2), own, number, HOME_DEV, NEAR, 1, CAP, 2))(patch_holder_shift_keys, patch_holder_shift_turns).reshape((NTILES, 1))
    wet_depth_layers = touch_ends(jax.random.randint(arg_keys[14], (NTILES,), 1, LEV + 1), jax.random.fold_in(arg_keys[14], 1), 1, LEV).astype(jnp.int32)
    return dict(air_ensemble=air_ensemble, sea_indicator=sea_indicator, layernorm_scaling=layernorm_scaling, harmonic_damping_factor=harmonic_damping_factor, bypass_factor=bypass_factor, core_exit_factor=core_exit_factor, air_to_exchange_factor=air_to_exchange_factor, sea_heat_imprint=sea_heat_imprint, sea_ensemble_arrays=sea_ensemble_arrays, input_to_hidden_kernel=input_to_hidden_kernel, hidden_to_change_kernel=hidden_to_change_kernel, patch_exchange_pick=patch_exchange_pick, node_sea_pick=node_sea_pick, patch_holder_shift=patch_holder_shift, wet_depth_layers=wet_depth_layers)


def analysis_table(orders, mesh_nodes):
    wavenumbers = jnp.arange(orders, dtype=jnp.int32)[:, None]
    columns = jnp.arange(mesh_nodes, dtype=jnp.int32)[None, :]
    angles = 2.0 * math.pi / mesh_nodes * (wavenumbers * columns % mesh_nodes).astype(jnp.float32)
    entries = jnp.stack([jnp.cos(angles), -jnp.sin(angles)], axis=1) / mesh_nodes
    return entries.reshape(2 * orders, mesh_nodes).astype(jnp.bfloat16)

def synthesis_table(orders, mesh_nodes):
    wavenumbers = jnp.arange(orders, dtype=jnp.int32)[:, None]
    columns = jnp.arange(mesh_nodes, dtype=jnp.int32)[None, :]
    angles = 2.0 * math.pi / mesh_nodes * (wavenumbers * columns % mesh_nodes).astype(jnp.float32)
    weights = jnp.where(wavenumbers == 0, 1.0, 2.0).astype(jnp.float32)
    entries = jnp.stack([weights * jnp.cos(angles), -weights * jnp.sin(angles)], axis=1)
    return jnp.transpose(entries.reshape(2 * orders, mesh_nodes)).astype(jnp.bfloat16)

def legendre_basis(orders, latitudes, degrees, highest):
    colatitude = math.pi / latitudes * (jnp.arange(latitudes, dtype=jnp.int32).astype(jnp.float32) + 0.5)
    cosine = jnp.cos(colatitude)[None, :]
    sine_values = jnp.sin(colatitude)
    counter = jnp.arange(1, highest, dtype=jnp.int32).astype(jnp.float32)
    log_terms = jnp.log((2.0 * counter - 1.0) / (2.0 * counter))
    totals = jnp.concatenate([jnp.zeros((1,), jnp.float32), jnp.cumsum(log_terms)])
    order_col = orders.astype(jnp.float32)[:, None]
    picked = jnp.take(totals, orders)[:, None]
    diagonal = jnp.exp(0.5 * (jnp.log((2.0 * order_col + 1.0) / (4.0 * math.pi)) + picked) + order_col * jnp.log(sine_values)[None, :])

    def advance(previous, degree):
        latest, before = previous
        square = degree * degree - order_col * order_col
        lowered = (degree - 1.0) * (degree - 1.0)
        upward = jnp.sqrt(jnp.maximum(4.0 * degree * degree - 1.0, 0.0) / jnp.maximum(square, 1.0))
        damping = jnp.sqrt(jnp.maximum(lowered - order_col * order_col, 0.0) / jnp.maximum(4.0 * lowered - 1.0, 1.0))
        current = upward * (cosine * latest - damping * before)
        current = jnp.where(degree == order_col, diagonal, current)
        current = jnp.where(degree < order_col, 0.0, current)
        return ((current, latest), current)
    empty_rows = jnp.zeros((orders.shape[0], latitudes), jnp.float32)
    degree_values = jnp.arange(degrees, dtype=jnp.int32).astype(jnp.float32)
    _, stacked = lax.scan(advance, (empty_rows, empty_rows), degree_values)
    return jnp.transpose(stacked, (1, 0, 2))

def transform_tables(polynomials, latitudes):
    colatitude = math.pi / latitudes * (jnp.arange(latitudes, dtype=jnp.int32).astype(jnp.float32) + 0.5)
    quadrature = 2.0 * math.pi * math.pi / latitudes * jnp.sin(colatitude)
    forward = (polynomials * quadrature[None, None, :]).astype(jnp.bfloat16)
    return (forward, polynomials.astype(jnp.bfloat16))

def layer_norm(values, scales):
    widened = values.astype(jnp.float32)
    centered = widened - lax.optimization_barrier(jnp.mean(widened, axis=-1, keepdims=True))
    spread = lax.optimization_barrier(jnp.mean(centered * centered, axis=-1, keepdims=True))
    return (centered * lax.rsqrt(spread + 1e-05) * scales).astype(jnp.bfloat16)

def patches(inputs):
    number, channels = (inputs.shape[0], inputs.shape[1])
    patch_grid = inputs.reshape(number, channels, 8, 16)
    padded = jnp.pad(patch_grid, ((0, 0), (0, 0), (1, 1), (1, 1)))
    shifted = [padded[:, :, rowshift:rowshift + 8, colshift:colshift + 16] for rowshift in range(3) for colshift in range(3)]
    return jnp.stack(shifted, axis=1).reshape(number, 9 * channels, 128)

def decode_surface(hidden, hidden_to_change_kernel):
    number = hidden.shape[0]
    partial_maps = jnp.einsum('qh,shc->sqc', hidden_to_change_kernel.astype(jnp.float32), hidden.astype(jnp.float32), precision=lax.Precision.HIGHEST)
    planes = jnp.pad(partial_maps.reshape(number, 9, 8, 16), ((0, 0), (0, 0), (1, 1), (1, 1)))
    coupled_step_return = jnp.zeros((number, 8, 16), jnp.float32)
    for rowshift in range(3):
        for colshift in range(3):
            coupled_step_return = coupled_step_return + planes[:, rowshift * 3 + colshift, rowshift:rowshift + 8, colshift:colshift + 16]
    return coupled_step_return.reshape(number, 128)

def marine_increment(current, boundary_driving, depth, input_to_hidden_kernel, hidden_to_change_kernel):
    channels = current.shape[1]
    level_index = jnp.arange(channels, dtype=jnp.int32) % LEV
    active = level_index[None, :] < depth[:, None]
    masked = jnp.where(active[:, :, None], current, jnp.zeros((), jnp.bfloat16))
    inputs = jnp.concatenate([masked, boundary_driving], axis=1)
    columns = patches(inputs)
    kernel = jnp.transpose(input_to_hidden_kernel, (1, 0, 2)).reshape(input_to_hidden_kernel.shape[1], -1)
    hidden = jax.nn.gelu(jnp.einsum('hk,skc->shc', kernel.astype(jnp.float32), columns.astype(jnp.float32), precision=lax.Precision.HIGHEST)).astype(jnp.bfloat16)
    increment = decode_surface(hidden, hidden_to_change_kernel)
    return (current[:, 0, :].astype(jnp.float32) + increment).astype(jnp.bfloat16)

def reference(air_ensemble, sea_indicator, layernorm_scaling, harmonic_damping_factor, bypass_factor, core_exit_factor, air_to_exchange_factor, sea_heat_imprint, sea_ensemble_arrays, input_to_hidden_kernel, hidden_to_change_kernel, patch_exchange_pick, node_sea_pick, patch_holder_shift, wet_depth_layers):
    highest = lax.Precision.HIGHEST
    polynomials = legendre_basis(jnp.arange(MMAX, dtype=jnp.int32), PARALLEL_TOTAL, LMAX, MMAX)
    forward, inverse = transform_tables(polynomials, PARALLEL_TOTAL)
    analysis = analysis_table(MMAX, MERIDIAN_TOTAL).astype(jnp.float32)
    synthesis = synthesis_table(MMAX, MERIDIAN_TOTAL).astype(jnp.float32)
    offsets = patch_holder_shift[:, 0].reshape(BANDS, HOME_DEV)
    earlier = jnp.tril(jnp.ones((HOME_DEV, HOME_DEV), jnp.int32), -1)
    matches = (offsets[:, :, None] == offsets[:, None, :]).astype(jnp.int32)
    positions = lax.optimization_barrier(jnp.sum(matches * earlier[None], axis=2))
    band_ids = jnp.arange(BANDS, dtype=jnp.int32)[:, None]
    owners = (band_ids + offsets) % BANDS
    holder_places = (owners * OWN_SLOTS + offsets * CAP + positions).reshape(-1)
    tile_band = jnp.arange(NTILES, dtype=jnp.int32) // HOME_DEV
    sources = (patch_exchange_pick + tile_band[:, None] * (LAT_DEV * MERIDIAN_TOTAL)).reshape(-1)
    point_band = jnp.arange(PARALLEL_TOTAL, dtype=jnp.int32) // LAT_DEV
    collected_picks = (node_sea_pick + point_band[:, None] * (HOME_DEV * 128)).reshape(-1)
    sea_cells = sea_indicator.astype(jnp.float32)

    def member_step(member_pair):
        current, marine_stepper = member_pair
        normed = layer_norm(current, layernorm_scaling)
        widened = normed.astype(jnp.float32)
        skip_term = jnp.einsum('jkc,cd->jkd', widened, bypass_factor.astype(jnp.float32), precision=highest)
        spectra = jnp.einsum('qk,jkc->qjc', analysis, widened, precision=highest).astype(jnp.bfloat16)
        spectra = spectra.reshape(MMAX, 2, PARALLEL_TOTAL, HARMONIC_CHANS).astype(jnp.float32)
        coefficients = jnp.einsum('mlj,mrjc->mrlc', forward.astype(jnp.float32), spectra, precision=highest)
        shaped = (coefficients * harmonic_damping_factor[None, None]).astype(jnp.bfloat16)
        returned_spec = jnp.einsum('mlj,mrlc->mrjc', inverse.astype(jnp.float32), shaped.astype(jnp.float32), precision=highest).astype(jnp.bfloat16)
        returned_spec = returned_spec.reshape(2 * MMAX, PARALLEL_TOTAL, HARMONIC_CHANS).astype(jnp.float32)
        spectral = jnp.einsum('kq,qjc->jkc', synthesis, returned_spec, precision=highest)
        mixed_rows = jax.nn.gelu(spectral + skip_term).astype(jnp.bfloat16)
        advanced_condition = current.astype(jnp.float32) + jnp.einsum('jkc,cd->jkd', mixed_rows.astype(jnp.float32), core_exit_factor.astype(jnp.float32), precision=highest)
        flux_points = jnp.einsum('jkc,cf->fjk', advanced_condition, air_to_exchange_factor.astype(jnp.float32), precision=highest)
        flux_points = flux_points.astype(jnp.bfloat16).reshape(FC, PARALLEL_TOTAL * MERIDIAN_TOTAL)
        boundary_driving = jnp.transpose(jnp.take(flux_points, sources, axis=1).reshape(FC, NTILES, 128), (1, 0, 2))
        sea_heat_patches = marine_increment(jnp.take(marine_stepper, holder_places, axis=0), boundary_driving, wet_depth_layers, input_to_hidden_kernel, hidden_to_change_kernel)
        mesh_nodes = jnp.take(sea_heat_patches.astype(jnp.float32).reshape(-1), collected_picks).reshape(PARALLEL_TOTAL, MERIDIAN_TOTAL)
        boundary_layer_array = sea_cells * mesh_nodes
        coupled_step_return = (advanced_condition + boundary_layer_array[:, :, None] * sea_heat_imprint).astype(jnp.bfloat16)
        return (coupled_step_return, boundary_layer_array)
    outputs, surfaces = lax.map(member_step, (air_ensemble, sea_ensemble_arrays))
    return (outputs, lax.optimization_barrier(jnp.sum(surfaces, axis=0)) / MEMBERS)
```

```python
import math

import jax
import jax.numpy as jnp
import numpy as np
from jax import lax
from jax.experimental import pallas as pl
from jax.experimental.pallas import tpu as pltpu
from jax.sharding import PartitionSpec as P

MERIDIAN_TOTAL = 360
MMAX = 128
LMAX = 128
FC = 8
LEV = 19
CAP = 2
NEAR = 8
HOME_DEV = 14
SLOTS = NEAR * CAP
CELLS = 128
SPAN = SLOTS * CELLS
OCH = 76
OCH_PAD = 80
TAPS = [(row, col) for row in (-1, 0, 1) for col in (-1, 0, 1)]
BF16 = jnp.bfloat16
F32 = jnp.float32
WHOLE = pl.BlockSpec(memory_space=pltpu.VMEM)


def passed_along(value, axis, by):
    devices = lax.axis_size(axis)
    return lax.ppermute(value, axis, [(i, (i + by) % devices) for i in range(devices)])


def fourier_tables():
    product = np.arange(MMAX)[:, None] * np.arange(MERIDIAN_TOTAL)[None, :] % MERIDIAN_TOTAL
    angles = 2.0 * np.pi / MERIDIAN_TOTAL * product
    analysis = np.stack([np.cos(angles), -np.sin(angles)], axis=1) / MERIDIAN_TOTAL
    weights = np.where(np.arange(MMAX) == 0, 1.0, 2.0)[:, None]
    synthesis = np.stack([weights * np.cos(angles), -weights * np.sin(angles)], axis=1)
    return (
        analysis.reshape(2 * MMAX, MERIDIAN_TOTAL).astype(BF16),
        synthesis.reshape(2 * MMAX, MERIDIAN_TOTAL).T.astype(BF16),
    )


def legendre_tables(latitudes):
    theta = np.pi / latitudes * (np.arange(latitudes) + 0.5)
    cosine = np.cos(theta)[None, :]
    sine = np.sin(theta)
    counter = np.arange(1, MMAX)
    totals = np.concatenate([[0.0], np.cumsum(np.log((2.0 * counter - 1.0) / (2.0 * counter)))])
    order = np.arange(MMAX, dtype=np.float64)[:, None]
    diagonal = np.exp(
        0.5 * (np.log((2.0 * order + 1.0) / (4.0 * np.pi)) + totals[:, None])
        + order * np.log(sine)[None, :]
    )
    values = np.zeros((MMAX, LMAX, latitudes))
    latest = np.zeros((MMAX, latitudes))
    before = np.zeros((MMAX, latitudes))
    for degree in range(LMAX):
        lowered = (degree - 1.0) ** 2
        upward = np.sqrt(
            max(4.0 * degree * degree - 1.0, 0.0) / np.maximum(degree * degree - order * order, 1.0)
        )
        damping = np.sqrt(
            np.maximum(lowered - order * order, 0.0) / max(4.0 * lowered - 1.0, 1.0)
        )
        current = upward * (cosine * latest - damping * before)
        current = np.where(degree == order, diagonal, current)
        current = np.where(degree < order, 0.0, current)
        values[:, degree, :] = current
        latest, before = current, latest
    quadrature = 2.0 * np.pi * np.pi / latitudes * sine
    forward = (values * quadrature[None, None, :]).astype(BF16)
    backward = np.transpose(values, (0, 2, 1)).astype(BF16)
    return forward, backward


def gelu(x):
    inner = math.sqrt(2.0 / math.pi) * (x + 0.044715 * (x * x * x))
    return 0.5 * x * (1.0 + jnp.tanh(inner))


def tap_masks(width):
    lane = lax.broadcasted_iota(jnp.int32, (1, width), 1) % CELLS
    row, col = lane // 16, lane % 16
    masks = []
    for down, right in TAPS:
        inside = (row + down >= 0) & (row + down < 8) & (col + right >= 0) & (col + right < 16)
        masks.append(inside)
    return masks


def shifted(x, tap, mask):
    by = 16 * tap[0] + tap[1]
    if by == 0:
        return x
    rolled = pltpu.roll(x, (-by) % x.shape[1], 1)
    return jnp.where(mask, rolled, 0.0)


def in_three(x):
    high = x.astype(BF16)
    rest = x - high.astype(F32)
    middle = rest.astype(BF16)
    return high, middle, (rest - middle.astype(F32)).astype(BF16)


def analysis_kernel(air_ref, scale_ref, table_ref, spectra_ref, normed_ref):
    rows = air_ref.shape[0]
    groups = spectra_ref.shape[0]
    table = table_ref[...]
    scale = scale_ref[...]
    for pair in range(rows // 2):
        both = []
        for j in (2 * pair, 2 * pair + 1):
            x = air_ref[j].astype(F32)
            centered = x - jnp.mean(x, axis=-1, keepdims=True)
            spread = jnp.mean(centered * centered, axis=-1, keepdims=True)
            normed = (centered * lax.rsqrt(spread + 1e-05) * scale).astype(BF16)
            normed_ref[j] = normed
            out = jnp.dot(table, normed, preferred_element_type=F32)
            both.append(out.reshape(groups, 8, out.shape[1]))
        block = jnp.concatenate(both, axis=1)
        spectra_ref[:, 16 * pair : 16 * (pair + 1), :] = block.astype(BF16)


def legendre_kernel(x_ref, forward_ref, backward_ref, gains_ref, out_ref, work):
    groups, chunk, channels = x_ref.shape
    total = groups * chunk
    latitudes = total // 8
    for third in range(channels // 128):
        lanes = slice(128 * third, 128 * (third + 1))
        work[third] = x_ref[:, :, lanes].astype(F32).reshape(total, 128)
    for m in range(4):
        for r in (0, 1):
            rows = pl.ds(2 * m + r, latitudes, stride=8)
            own = jnp.concatenate(
                [work[third, rows, :] for third in range(channels // 128)], axis=1
            ).astype(BF16)
            coefficients = jnp.dot(forward_ref[m], own, preferred_element_type=F32)
            shaped = (coefficients * gains_ref[...]).astype(BF16)
            back = jnp.dot(backward_ref[m], shaped, preferred_element_type=F32)
            for third in range(channels // 128):
                work[third, rows, :] = back[:, 128 * third : 128 * (third + 1)]
    for third in range(channels // 128):
        lanes = slice(128 * third, 128 * (third + 1))
        out_ref[:, :, lanes] = work[third].reshape(groups, chunk, 128).astype(BF16)


def ocean_kernel(depth_ref, a0_ref, a1_ref, b1_ref, c1_ref, weight_ref, out_ref, columns):
    masks = tap_masks(CELLS)
    level = lax.broadcasted_iota(jnp.int32, (OCH, CELLS), 0) % LEV
    places = {
        0: (a0_ref, 0), 4: (a1_ref, 0), 2: (b1_ref, 0), 6: (b1_ref, 4),
        1: (c1_ref, 0), 5: (c1_ref, 2), 3: (c1_ref, 4), 7: (c1_ref, 6),
    }
    for slot in range(SLOTS):
        ref, at = places[slot // CAP]
        state = ref[at + slot % CAP].astype(F32)
        state = jnp.where(level < depth_ref[slot], state, 0.0)
        state = jnp.concatenate([state, jnp.zeros((OCH_PAD - OCH, CELLS), F32)], axis=0)
        for q, tap in enumerate(TAPS):
            moved = shifted(state, tap, masks[q]).astype(BF16)
            columns[OCH_PAD * q : OCH_PAD * (q + 1), CELLS * slot : CELLS * (slot + 1)] = moved
    for at in range(0, SPAN, 512):
        out_ref[:, at : at + 512] = jnp.dot(
            weight_ref[...], columns[:, at : at + 512], preferred_element_type=F32
        )


def closing_kernel(
    rows_ref, synthesis_ref, skip_ref, air_ref, exit_ref, exchange_ref, place_ref, line_ref,
    wet_ref, forcing_weight_ref, decode_ref, top_ref, cell_ref, slot_ref, imprint_ref,
    out_ref, tiles_ref, updated, flux, sst,
):
    latitude_rows = air_ref.shape[0]
    groups, chunk, channels = rows_ref.shape
    synthesis = synthesis_ref[...]
    fields = rows_ref[...].astype(F32).reshape(groups, latitude_rows, 8, channels)
    for j in range(latitude_rows):
        own = fields[:, j].reshape(8 * groups, channels).astype(BF16)
        spectral = jnp.dot(synthesis, own, preferred_element_type=F32)
        mixed = gelu(spectral + skip_ref[j]).astype(BF16)
        state = air_ref[j].astype(F32) + jnp.dot(
            mixed, exit_ref[...], preferred_element_type=F32
        )
        updated[j] = state
        high = state.astype(BF16)
        low = (state - high.astype(F32)).astype(BF16)
        dims = (((1,), (1,)), ((), ()))
        flux[8 * j : 8 * (j + 1), :] = lax.dot_general(
            exchange_ref[...], high, dims, preferred_element_type=F32
        ) + lax.dot_general(exchange_ref[...], low, dims, preferred_element_type=F32)
    spread = jnp.dot(flux[...].astype(BF16), place_ref[...], preferred_element_type=F32)
    line = line_ref[...]
    forcing = jnp.zeros((FC, SPAN), F32)
    for j in range(latitude_rows):
        forcing = forcing + jnp.where(line == j, spread[8 * j : 8 * (j + 1), :], 0.0)
    masks = tap_masks(SPAN)
    columns = jnp.concatenate(
        [shifted(forcing, tap, masks[q]) for q, tap in enumerate(TAPS)], axis=0
    ).astype(BF16)
    change = jnp.zeros((1, SPAN), F32)
    hidden = gelu(
        wet_ref[...] + jnp.dot(forcing_weight_ref[...], columns, preferred_element_type=F32)
    ).astype(BF16)
    partial = jnp.dot(decode_ref[...], hidden, preferred_element_type=F32)
    for q, tap in enumerate(TAPS):
        change = change + shifted(partial[q : q + 1, :], tap, masks[q])
    surface = top_ref[...] + change
    for slot in range(SLOTS):
        sst[slot : slot + 1, :] = surface[:, CELLS * slot : CELLS * (slot + 1)]
    tiles = sst[...].astype(BF16)
    tiles_ref[...] = tiles
    tripled = jnp.concatenate([tiles, tiles, tiles], axis=0)
    imprint = jnp.concatenate(
        [jnp.broadcast_to(piece, (SLOTS, channels)) for piece in in_three(imprint_ref[...])], axis=0
    )
    for j in range(latitude_rows):
        picked = lax.dot_general(
            cell_ref[j], tripled, (((1,), (1,)), ((), ())), preferred_element_type=F32
        )
        chosen = picked.astype(BF16) * slot_ref[j]
        warmth = jnp.dot(chosen, imprint, preferred_element_type=F32)
        out_ref[j] = (updated[j] + warmth).astype(BF16)


def mean_kernel(tiles_ref, cell_ref, slot_ref, out_ref):
    members = tiles_ref.shape[0]
    total = jnp.zeros(tiles_ref.shape[1:], F32)
    for member in range(members):
        total = total + tiles_ref[member].astype(F32)
    pieces = jnp.concatenate(in_three(total), axis=0)
    for j in range(cell_ref.shape[0]):
        picked = lax.dot_general(
            pieces, cell_ref[j], (((1,), (1,)), ((), ())), preferred_element_type=F32
        )
        joined = picked[:SLOTS] + picked[SLOTS : 2 * SLOTS] + picked[2 * SLOTS :]
        kept = jnp.where(slot_ref[j] > 0, joined, 0.0)
        out_ref[j : j + 1, :] = jnp.sum(kept, axis=0, keepdims=True) / members


def call(kernel, outs, operands, flops, scratch=(), limit=32, specs=None):
    size = sum(math.prod(o.shape) * o.dtype.itemsize for o in list(outs) + list(operands))
    return pl.pallas_call(
        kernel,
        out_shape=outs if len(outs) > 1 else outs[0],
        in_specs=specs or [WHOLE] * len(operands),
        out_specs=[WHOLE] * len(outs) if len(outs) > 1 else WHOLE,
        scratch_shapes=list(scratch),
        compiler_params=pltpu.CompilerParams(vmem_limit_bytes=limit * 1024 * 1024),
        cost_estimate=pl.CostEstimate(flops=flops, bytes_accessed=size, transcendentals=0),
    )(*operands)


def shards(
    air_ensemble,
    sea_indicator,
    layernorm_scaling,
    harmonic_damping_factor,
    bypass_factor,
    core_exit_factor,
    air_to_exchange_factor,
    sea_heat_imprint,
    sea_ensemble_arrays,
    input_to_hidden_kernel,
    hidden_to_change_kernel,
    patch_exchange_pick,
    node_sea_pick,
    patch_holder_shift,
    wet_depth_layers,
):
    bands = lax.axis_size("space")
    members = lax.axis_size("member")
    air = air_ensemble[0]
    latitude_rows, longitudes, channels = air.shape
    latitudes = latitude_rows * bands
    hidden_channels = input_to_hidden_kernel.shape[1]
    per_device = MMAX // bands
    chunk = 2 * per_device * latitude_rows
    shape = jax.ShapeDtypeStruct

    analysis, synthesis = (jnp.asarray(t) for t in fourier_tables())
    spectra, normed = call(
        analysis_kernel,
        [shape((bands, chunk, channels), BF16), shape(air.shape, BF16)],
        [air, layernorm_scaling[None, :], analysis],
        2 * 2 * MMAX * latitude_rows * longitudes * channels,
    )
    gathered = lax.all_to_all(spectra, "space", split_axis=0, concat_axis=0, tiled=True)

    slots = sea_ensemble_arrays[0]
    a0 = slots[:8]
    a1 = passed_along(slots[8:], "space", -4)
    b1 = passed_along(jnp.concatenate([a0[4:], a1[4:]], axis=0), "space", -2)
    c1 = passed_along(
        jnp.concatenate([a0[2:4], a1[2:4], b1[2:4], b1[6:8]], axis=0), "space", -1
    )
    offsets = patch_holder_shift[:, 0]
    earlier = jnp.tril(jnp.ones((HOME_DEV, HOME_DEV), jnp.int32), -1)
    positions = jnp.sum((offsets[:, None] == offsets[None, :]).astype(jnp.int32) * earlier, axis=1)
    targets = offsets * CAP + positions
    selected = targets[None, :] == jnp.arange(SLOTS, dtype=jnp.int32)[:, None]
    depths = jnp.sum(jnp.where(selected, wet_depth_layers[None, :], 0), axis=1)
    kernel = jnp.transpose(input_to_hidden_kernel, (1, 0, 2))
    state_weight = jnp.pad(kernel[:, :, :OCH], ((0, 0), (0, 0), (0, OCH_PAD - OCH))).reshape(
        hidden_channels, -1
    )
    forcing_weight = kernel[:, :, OCH:].reshape(hidden_channels, -1)
    decode_weight = jnp.pad(hidden_to_change_kernel, ((0, 16 - len(TAPS)), (0, 0)))
    wet = call(
        ocean_kernel,
        [shape((hidden_channels, SPAN), F32)],
        [depths, a0, a1, b1, c1, state_weight],
        2 * hidden_channels * len(TAPS) * OCH_PAD * SPAN,
        [pltpu.VMEM((len(TAPS) * OCH_PAD, SPAN), BF16)],
        specs=[pl.BlockSpec(memory_space=pltpu.SMEM)] + [WHOLE] * 5,
    )
    picks = jnp.sum(jnp.where(selected[:, :, None], patch_exchange_pick[None], 0), axis=1)
    picks = picks.reshape(1, SPAN)
    line = picks // longitudes
    place = (
        picks % longitudes == jnp.arange(longitudes, dtype=jnp.int32)[:, None]
    ).astype(BF16)
    top = jnp.concatenate(
        [a0[0:2, 0], c1[0:2, 0], b1[0:2, 0], c1[4:6, 0], a1[0:2, 0], c1[2:4, 0], b1[4:6, 0], c1[6:8, 0]],
        axis=0,
    ).astype(F32).reshape(1, SPAN)
    tile = node_sea_pick // CELLS
    holder = jnp.sum(
        jnp.where(
            tile[:, :, None] == jnp.arange(HOME_DEV, dtype=jnp.int32), targets[None, None, :], 0
        ),
        axis=2,
    )
    holder = jnp.where(sea_indicator > 0, holder, -1)
    cell = (
        (node_sea_pick % CELLS)[:, :, None] == jnp.arange(CELLS, dtype=jnp.int32)
    ).astype(BF16)
    slot_of = (
        holder[:, :, None] == jnp.arange(3 * SLOTS, dtype=jnp.int32) % SLOTS
    ).astype(BF16)
    slot_rows = (
        holder[:, None, :] == jnp.arange(SLOTS, dtype=jnp.int32)[None, :, None]
    ).astype(F32)
    skip = jnp.einsum("jkc,cd->jkd", normed, bypass_factor, preferred_element_type=F32)
    forward, backward = (jnp.asarray(t) for t in legendre_tables(latitudes))
    first = lax.axis_index("space") * per_device
    forward = lax.dynamic_slice_in_dim(forward, first, per_device, 0)
    backward = lax.dynamic_slice_in_dim(backward, first, per_device, 0)
    filtered = call(
        legendre_kernel,
        [shape((bands, chunk, channels), BF16)],
        [gathered, forward, backward, harmonic_damping_factor],
        2 * 2 * 2 * per_device * LMAX * latitudes * channels,
        [pltpu.VMEM((channels // 128, bands * chunk, 128), F32)],
    )
    returned = lax.all_to_all(filtered, "space", split_axis=0, concat_axis=0, tiled=True)
    out, tiles = call(
        closing_kernel,
        [shape(air.shape, BF16), shape((SLOTS, CELLS), BF16)],
        [
            returned, synthesis, skip, air, core_exit_factor, air_to_exchange_factor.T, place,
            line, wet, forcing_weight, decode_weight, top, cell, slot_of,
            sea_heat_imprint[None, :],
        ],
        2 * latitude_rows * longitudes * channels * (channels + 2 * MMAX),
        [
            pltpu.VMEM(air.shape, F32),
            pltpu.VMEM((FC * latitude_rows, longitudes), F32),
            pltpu.VMEM((SLOTS, CELLS), F32),
        ],
    )
    everyone = lax.all_to_all(
        jnp.broadcast_to(tiles[None], (members,) + tiles.shape),
        "member",
        split_axis=0,
        concat_axis=0,
        tiled=True,
    )
    mean = call(
        mean_kernel,
        [shape((latitude_rows, longitudes), F32)],
        [everyone, cell, slot_rows],
        2 * 3 * SLOTS * CELLS * latitude_rows * longitudes,
    )
    return (out[None], mean)


def solution(mesh):
    in_specs = (
        P("member", "space", None, None),
        P("space", None),
        P(),
        P(),
        P(),
        P(),
        P(),
        P(),
        P("member", "space", None, None),
        P(),
        P(),
        P("space", None),
        P("space", None),
        P("space", None),
        P("space"),
    )
    out_specs = (P("member", "space", None, None), P("space", None))
    return jax.shard_map(shards, mesh=mesh, in_specs=in_specs, out_specs=out_specs, check_vma=False)
```

```python
import math

import jax
import jax.numpy as jnp
import numpy as np
from jax import lax
from jax.experimental import pallas as pl
from jax.experimental.pallas import tpu as pltpu
from jax.sharding import PartitionSpec as P

MERIDIAN_TOTAL = 360
MMAX = 128
LMAX = 128
FC = 8
LEV = 19
CAP = 2
NEAR = 8
HOME_DEV = 14
SLOTS = NEAR * CAP
CELLS = 128
SPAN = SLOTS * CELLS
OCH = 76
OCH_PAD = 80
TAPS = [(row, col) for row in (-1, 0, 1) for col in (-1, 0, 1)]
LARGE = 56
EARLY = 3
BF16 = jnp.bfloat16
F32 = jnp.float32
WHOLE = pl.BlockSpec(memory_space=pltpu.VMEM)
ANYWHERE = pl.BlockSpec(memory_space=pl.ANY)


def passed_along(value, axis, by):
    devices = lax.axis_size(axis)
    return lax.ppermute(value, axis, [(i, (i + by) % devices) for i in range(devices)])


def fourier_tables():
    product = np.arange(MMAX)[:, None] * np.arange(MERIDIAN_TOTAL)[None, :] % MERIDIAN_TOTAL
    angles = 2.0 * np.pi / MERIDIAN_TOTAL * product
    analysis = np.stack([np.cos(angles), -np.sin(angles)], axis=1) / MERIDIAN_TOTAL
    weights = np.where(np.arange(MMAX) == 0, 1.0, 2.0)[:, None]
    synthesis = np.stack([weights * np.cos(angles), -weights * np.sin(angles)], axis=1)
    return (
        analysis.reshape(2 * MMAX, MERIDIAN_TOTAL).astype(BF16),
        synthesis.reshape(2 * MMAX, MERIDIAN_TOTAL).T.astype(BF16),
    )


def legendre_tables(latitudes):
    theta = np.pi / latitudes * (np.arange(latitudes) + 0.5)
    cosine = np.cos(theta)[None, :]
    sine = np.sin(theta)
    counter = np.arange(1, MMAX)
    totals = np.concatenate([[0.0], np.cumsum(np.log((2.0 * counter - 1.0) / (2.0 * counter)))])
    order = np.arange(MMAX, dtype=np.float64)[:, None]
    diagonal = np.exp(
        0.5 * (np.log((2.0 * order + 1.0) / (4.0 * np.pi)) + totals[:, None])
        + order * np.log(sine)[None, :]
    )
    values = np.zeros((MMAX, LMAX, latitudes))
    latest = np.zeros((MMAX, latitudes))
    before = np.zeros((MMAX, latitudes))
    for degree in range(LMAX):
        lowered = (degree - 1.0) ** 2
        upward = np.sqrt(
            max(4.0 * degree * degree - 1.0, 0.0) / np.maximum(degree * degree - order * order, 1.0)
        )
        damping = np.sqrt(
            np.maximum(lowered - order * order, 0.0) / max(4.0 * lowered - 1.0, 1.0)
        )
        current = upward * (cosine * latest - damping * before)
        current = np.where(degree == order, diagonal, current)
        current = np.where(degree < order, 0.0, current)
        values[:, degree, :] = current
        latest, before = current, latest
    quadrature = 2.0 * np.pi * np.pi / latitudes * sine
    forward = (values * quadrature[None, None, :]).astype(BF16)
    backward = np.transpose(values, (0, 2, 1)).astype(BF16)
    return forward, backward


def gelu(x):
    inner = math.sqrt(2.0 / math.pi) * (x + 0.044715 * (x * x * x))
    return 0.5 * x * (1.0 + jnp.tanh(inner))


def tap_masks(width):
    lane = lax.broadcasted_iota(jnp.int32, (1, width), 1) % CELLS
    row, col = lane // 16, lane % 16
    masks = []
    for down, right in TAPS:
        inside = (row + down >= 0) & (row + down < 8) & (col + right >= 0) & (col + right < 16)
        masks.append(inside)
    return masks


def shifted(x, tap, mask):
    by = 16 * tap[0] + tap[1]
    if by == 0:
        return x
    rolled = pltpu.roll(x, (-by) % x.shape[1], 1)
    return jnp.where(mask, rolled, 0.0)


def in_three(x):
    high = x.astype(BF16)
    rest = x - high.astype(F32)
    middle = rest.astype(BF16)
    return high, middle, (rest - middle.astype(F32)).astype(BF16)


def begin(copies, sems):
    started = [
        pltpu.make_async_copy(source, target, sems.at[i])
        for i, (source, target) in enumerate(copies)
    ]
    for one in started:
        one.start()
    return started


def analysis_kernel(
    air_any, scale_ref, table_any, spectra_ref, normed_ref, air_ref, table_ref, sems
):
    rows = air_ref.shape[0]
    groups = spectra_ref.shape[0]
    copies = begin(
        [(air_any.at[j], air_ref.at[j]) for j in range(rows)] + [(table_any, table_ref)], sems
    )
    scale = scale_ref[...].reshape(1, scale_ref.shape[0])
    for pair in range(rows // 2):
        both = []
        for j in (2 * pair, 2 * pair + 1):
            copies[j].wait()
            x = air_ref[j].astype(F32)
            centered = x - jnp.mean(x, axis=-1, keepdims=True)
            spread = jnp.mean(centered * centered, axis=-1, keepdims=True)
            normed = (centered * lax.rsqrt(spread + 1e-05) * scale).astype(BF16)
            normed_ref[j] = normed
            if j == 0:
                copies[rows].wait()
            out = jnp.dot(table_ref[...], normed, preferred_element_type=F32)
            both.append(out.reshape(groups, 8, out.shape[1]))
        block = jnp.concatenate(both, axis=1)
        spectra_ref[:, 16 * pair : 16 * (pair + 1), :] = block.astype(BF16)


def legendre_kernel(x_ref, forward_ref, backward_ref, gains_ref, out_ref, work):
    groups, chunk, channels = x_ref.shape
    total = groups * chunk
    latitudes = total // 8
    for third in range(channels // 128):
        lanes = slice(128 * third, 128 * (third + 1))
        work[third] = x_ref[:, :, lanes].astype(F32).reshape(total, 128)
    for m in range(4):
        for r in (0, 1):
            rows = pl.ds(2 * m + r, latitudes, stride=8)
            own = jnp.concatenate(
                [work[third, rows, :] for third in range(channels // 128)], axis=1
            ).astype(BF16)
            coefficients = jnp.dot(forward_ref[m], own, preferred_element_type=F32)
            shaped = (coefficients * gains_ref[...]).astype(BF16)
            back = jnp.dot(backward_ref[m], shaped, preferred_element_type=F32)
            for third in range(channels // 128):
                work[third, rows, :] = back[:, 128 * third : 128 * (third + 1)]
    for third in range(channels // 128):
        lanes = slice(128 * third, 128 * (third + 1))
        out_ref[:, :, lanes] = work[third].reshape(groups, chunk, 128).astype(BF16)


def ocean_kernel(depth_ref, *refs):
    pieces, (weight_ref, out_ref, top_ref, columns) = refs[:NEAR], refs[NEAR:]
    masks = tap_masks(CELLS)
    level = lax.broadcasted_iota(jnp.int32, (OCH, CELLS), 0) % LEV
    for slot in range(SLOTS):
        lanes = slice(CELLS * slot, CELLS * (slot + 1))
        state = pieces[slot // CAP][slot % CAP].astype(F32)
        top_ref[:, lanes] = state[0:1]
        state = jnp.where(level < depth_ref[slot], state, 0.0)
        state = jnp.concatenate([state, jnp.zeros((OCH_PAD - OCH, CELLS), F32)], axis=0)
        for q, tap in enumerate(TAPS):
            moved = shifted(state, tap, masks[q]).astype(BF16)
            columns[OCH_PAD * q : OCH_PAD * (q + 1), lanes] = moved
    for at in range(0, SPAN, 512):
        out_ref[:, at : at + 512] = jnp.dot(
            weight_ref[...], columns[:, at : at + 512], preferred_element_type=F32
        )


def surface_kernel(*refs):
    sources, (updated_any, tiles_ref), held, (updated_ref, flux, sst, sems, out_sems) = (
        refs[:12], refs[12:14], refs[14:26], refs[26:]
    )
    leaving = []
    copies = begin(list(zip(sources, held)), sems)
    (
        rows_ref, synthesis_ref, skip_ref, air_ref, exit_ref, exchange_ref, place_ref, line_ref,
        forcing_weight_ref, wet_ref, decode_ref, top_ref,
    ) = held
    latitude_rows = air_ref.shape[0]
    groups, chunk, channels = rows_ref.shape
    for one in copies[:2]:
        one.wait()
    for j in range(latitude_rows):
        own = rows_ref[...].astype(F32).reshape(groups, latitude_rows, 8, channels)[:, j]
        own = own.reshape(8 * groups, channels).astype(BF16)
        spectral = jnp.dot(synthesis_ref[...], own, preferred_element_type=F32)
        if j == 0:
            for one in copies[2:6]:
                one.wait()
        mixed = gelu(spectral + skip_ref[j]).astype(BF16)
        state = air_ref[j].astype(F32) + jnp.dot(
            mixed, exit_ref[...], preferred_element_type=F32
        )
        updated_ref[j] = state
        leave = pltpu.make_async_copy(updated_ref.at[j], updated_any.at[j], out_sems.at[j])
        leave.start()
        leaving.append(leave)
        high = state.astype(BF16)
        low = (state - high.astype(F32)).astype(BF16)
        dims = (((0,), (1,)), ((), ()))
        flux[8 * j : 8 * (j + 1), :] = lax.dot_general(
            exchange_ref[...], high, dims, preferred_element_type=F32
        ) + lax.dot_general(exchange_ref[...], low, dims, preferred_element_type=F32)
    for one in copies[6:]:
        one.wait()
    spread = jnp.dot(flux[...].astype(BF16), place_ref[...], preferred_element_type=F32)
    line = line_ref[...]
    forcing = jnp.zeros((FC, SPAN), F32)
    for j in range(latitude_rows):
        forcing = forcing + jnp.where(line == j, spread[8 * j : 8 * (j + 1), :], 0.0)
    masks = tap_masks(SPAN)
    columns = jnp.concatenate(
        [shifted(forcing, tap, masks[q]) for q, tap in enumerate(TAPS)], axis=0
    ).astype(BF16)
    hidden = gelu(
        wet_ref[...] + jnp.dot(forcing_weight_ref[...], columns, preferred_element_type=F32)
    ).astype(BF16)
    partial = jnp.dot(decode_ref[...], hidden, preferred_element_type=F32)
    change = jnp.zeros((1, SPAN), F32)
    for q, tap in enumerate(TAPS):
        change = change + shifted(partial[q : q + 1, :], tap, masks[q])
    surface = top_ref[...] + change
    for slot in range(SLOTS):
        sst[slot : slot + 1, :] = surface[:, CELLS * slot : CELLS * (slot + 1)]
    tiles = sst[...].astype(BF16)
    for member in range(tiles_ref.shape[0]):
        tiles_ref[member] = tiles
    for one in leaving:
        one.wait()


def imprint_kernel(updated_ref, tiles_ref, cell_ref, slot_ref, imprint_ref, out_ref):
    channels = updated_ref.shape[2]
    tiles = tiles_ref[0]
    tripled = jnp.concatenate([tiles, tiles, tiles], axis=0)
    pieces = in_three(imprint_ref[...].reshape(1, channels))
    imprint = jnp.concatenate(
        [jnp.broadcast_to(piece, (SLOTS, channels)) for piece in pieces], axis=0
    )
    picked = lax.dot_general(
        cell_ref[0], tripled, (((1,), (1,)), ((), ())), preferred_element_type=F32
    )
    chosen = picked.astype(BF16) * slot_ref[0]
    warmth = jnp.dot(chosen, imprint, preferred_element_type=F32)
    out_ref[0] = (updated_ref[0] + warmth).astype(BF16)


def mean_kernel(tiles_ref, cell_ref, slot_ref, out_ref):
    members = tiles_ref.shape[0]
    total = jnp.zeros(tiles_ref.shape[1:], F32)
    for member in range(members):
        total = total + tiles_ref[member].astype(F32)
    pieces = jnp.concatenate(in_three(total), axis=0)
    for j in range(cell_ref.shape[0]):
        picked = lax.dot_general(
            pieces, cell_ref[j], (((1,), (1,)), ((), ())), preferred_element_type=F32
        )
        joined = picked[:SLOTS] + picked[SLOTS : 2 * SLOTS] + picked[2 * SLOTS :]
        kept = jnp.where(slot_ref[j] > 0, joined, 0.0)
        out_ref[j : j + 1, :] = jnp.sum(kept, axis=0, keepdims=True) / members


def call(kernel, outs, operands, flops, scratch=(), limit=32, specs=None, out_specs=None):
    size = sum(math.prod(o.shape) * o.dtype.itemsize for o in list(outs) + list(operands))
    return pl.pallas_call(
        kernel,
        out_shape=outs if len(outs) > 1 else outs[0],
        in_specs=specs or [WHOLE] * len(operands),
        out_specs=out_specs or ([WHOLE] * len(outs) if len(outs) > 1 else WHOLE),
        scratch_shapes=list(scratch),
        compiler_params=pltpu.CompilerParams(vmem_limit_bytes=limit * 1024 * 1024),
        cost_estimate=pl.CostEstimate(flops=flops, bytes_accessed=size, transcendentals=0),
    )(*operands)


def held(operands):
    return [pltpu.VMEM(o.shape, o.dtype) for o in operands]


def shards(
    air_ensemble,
    sea_indicator,
    layernorm_scaling,
    harmonic_damping_factor,
    bypass_factor,
    core_exit_factor,
    air_to_exchange_factor,
    sea_heat_imprint,
    sea_ensemble_arrays,
    input_to_hidden_kernel,
    hidden_to_change_kernel,
    patch_exchange_pick,
    node_sea_pick,
    patch_holder_shift,
    wet_depth_layers,
):
    bands = lax.axis_size("space")
    members = lax.axis_size("member")
    air = air_ensemble[0]
    latitude_rows, longitudes, channels = air.shape
    latitudes = latitude_rows * bands
    hidden_channels = input_to_hidden_kernel.shape[1]
    per_device = MMAX // bands
    chunk = 2 * per_device * latitude_rows
    shape = jax.ShapeDtypeStruct

    analysis, synthesis = (jnp.asarray(t) for t in fourier_tables())
    spectra, normed = call(
        analysis_kernel,
        [shape((bands, chunk, channels), BF16), shape(air.shape, BF16)],
        [air, layernorm_scaling, analysis],
        2 * 2 * MMAX * latitude_rows * longitudes * channels,
        held([air, analysis]) + [pltpu.SemaphoreType.DMA((latitude_rows + 1,))],
        limit=LARGE,
        specs=[ANYWHERE, WHOLE, ANYWHERE],
    )
    gathered = lax.all_to_all(spectra, "space", split_axis=0, concat_axis=0, tiled=True)

    slots = sea_ensemble_arrays[0]
    far = [
        passed_along(slots[offset * CAP : (offset + 1) * CAP], "space", -offset)
        for offset in range(EARLY, NEAR)
    ]
    gathered, *far = lax.optimization_barrier((gathered, *far))
    forward, backward = (jnp.asarray(t) for t in legendre_tables(latitudes))
    first = lax.axis_index("space") * per_device
    forward = lax.dynamic_slice_in_dim(forward, first, per_device, 0)
    backward = lax.dynamic_slice_in_dim(backward, first, per_device, 0)
    filtered = call(
        legendre_kernel,
        [shape((bands, chunk, channels), BF16)],
        [gathered, forward, backward, harmonic_damping_factor],
        2 * 2 * 2 * per_device * LMAX * latitudes * channels,
        [pltpu.VMEM((channels // 128, bands * chunk, 128), F32)],
    )
    filtered, slots = lax.optimization_barrier((filtered, slots[: EARLY * CAP]))
    returned = lax.all_to_all(filtered, "space", split_axis=0, concat_axis=0, tiled=True)
    pieces = [slots[:CAP]] + [
        passed_along(slots[offset * CAP : (offset + 1) * CAP], "space", -offset)
        for offset in range(1, EARLY)
    ] + far
    offsets = patch_holder_shift[:, 0]
    earlier = jnp.tril(jnp.ones((HOME_DEV, HOME_DEV), jnp.int32), -1)
    positions = jnp.sum((offsets[:, None] == offsets[None, :]).astype(jnp.int32) * earlier, axis=1)
    targets = offsets * CAP + positions
    selected = targets[None, :] == jnp.arange(SLOTS, dtype=jnp.int32)[:, None]
    depths = jnp.sum(jnp.where(selected, wet_depth_layers[None, :], 0), axis=1)
    kernel = jnp.transpose(input_to_hidden_kernel, (1, 0, 2))
    state_weight = jnp.pad(kernel[:, :, :OCH], ((0, 0), (0, 0), (0, OCH_PAD - OCH))).reshape(
        hidden_channels, -1
    )
    forcing_weight = kernel[:, :, OCH:].reshape(hidden_channels, -1)
    decode_weight = jnp.pad(hidden_to_change_kernel, ((0, 16 - len(TAPS)), (0, 0)))
    wet, top = call(
        ocean_kernel,
        [shape((hidden_channels, SPAN), F32), shape((1, SPAN), F32)],
        [depths, *pieces, state_weight],
        2 * hidden_channels * len(TAPS) * OCH_PAD * SPAN,
        [pltpu.VMEM((len(TAPS) * OCH_PAD, SPAN), BF16)],
        specs=[pl.BlockSpec(memory_space=pltpu.SMEM)] + [WHOLE] * (NEAR + 1),
    )
    picks = jnp.sum(jnp.where(selected[:, :, None], patch_exchange_pick[None], 0), axis=1)
    picks = picks.reshape(1, SPAN)
    line = picks // longitudes
    place = (
        picks % longitudes == jnp.arange(longitudes, dtype=jnp.int32)[:, None]
    ).astype(BF16)
    tile = node_sea_pick // CELLS
    holder = jnp.sum(
        jnp.where(
            tile[:, :, None] == jnp.arange(HOME_DEV, dtype=jnp.int32), targets[None, None, :], 0
        ),
        axis=2,
    )
    holder = jnp.where(sea_indicator > 0, holder, -1)
    cell = (
        (node_sea_pick % CELLS)[:, :, None] == jnp.arange(CELLS, dtype=jnp.int32)
    ).astype(BF16)
    slot_of = (
        holder[:, :, None] == jnp.arange(3 * SLOTS, dtype=jnp.int32) % SLOTS
    ).astype(BF16)
    slot_rows = (
        holder[:, None, :] == jnp.arange(SLOTS, dtype=jnp.int32)[None, :, None]
    ).astype(F32)
    skip = jnp.einsum("jkc,cd->jkd", normed, bypass_factor, preferred_element_type=F32)
    operands = [
        returned, synthesis, skip, air, core_exit_factor, air_to_exchange_factor, place, line,
        forcing_weight, wet, decode_weight, top,
    ]
    updated, tiles = call(
        surface_kernel,
        [shape(air.shape, F32), shape((members, SLOTS, CELLS), BF16)],
        operands,
        2 * latitude_rows * longitudes * channels * (channels + 2 * MMAX),
        held(operands)
        + [
            pltpu.VMEM(air.shape, F32),
            pltpu.VMEM((FC * latitude_rows, longitudes), F32),
            pltpu.VMEM((SLOTS, CELLS), F32),
            pltpu.SemaphoreType.DMA((len(operands),)),
            pltpu.SemaphoreType.DMA((latitude_rows,)),
        ],
        limit=LARGE,
        specs=[ANYWHERE] * len(operands),
        out_specs=[ANYWHERE, WHOLE],
    )
    everyone = lax.all_to_all(tiles, "member", split_axis=0, concat_axis=0, tiled=True)

    def by_latitude(*rest):
        return pl.BlockSpec((1,) + rest, lambda j: (j, 0, 0))

    out = pl.pallas_call(
        imprint_kernel,
        grid=(latitude_rows,),
        out_shape=shape(air.shape, BF16),
        in_specs=[
            by_latitude(longitudes, channels),
            pl.BlockSpec((1, SLOTS, CELLS), lambda j: (0, 0, 0)),
            by_latitude(longitudes, CELLS),
            by_latitude(longitudes, 3 * SLOTS),
            pl.BlockSpec((channels,), lambda j: (0,)),
        ],
        out_specs=by_latitude(longitudes, channels),
        compiler_params=pltpu.CompilerParams(vmem_limit_bytes=LARGE * 1024 * 1024),
        cost_estimate=pl.CostEstimate(
            flops=2 * latitude_rows * longitudes * channels * 256,
            bytes_accessed=air.size * 6,
            transcendentals=0,
        ),
    )(updated, tiles, cell, slot_of, sea_heat_imprint)
    mean = call(
        mean_kernel,
        [shape((latitude_rows, longitudes), F32)],
        [everyone, cell, slot_rows],
        2 * 3 * SLOTS * CELLS * latitude_rows * longitudes,
    )
    return (out[None], mean)


def solution(mesh):
    in_specs = (
        P("member", "space", None, None),
        P("space", None),
        P(),
        P(),
        P(),
        P(),
        P(),
        P(),
        P("member", "space", None, None),
        P(),
        P(),
        P("space", None),
        P("space", None),
        P("space", None),
        P("space"),
    )
    out_specs = (P("member", "space", None, None), P("space", None))
    return jax.shard_map(shards, mesh=mesh, in_specs=in_specs, out_specs=out_specs, check_vma=False)
```

```python
import math

import jax
import jax.numpy as jnp
import numpy as np
from jax import lax
from jax.experimental import pallas as pl
from jax.experimental.pallas import tpu as pltpu
from jax.sharding import PartitionSpec as P

MERIDIAN_TOTAL = 360
MMAX = 128
LMAX = 128
FC = 8
LEV = 19
CAP = 2
NEAR = 8
HOME_DEV = 14
SLOTS = NEAR * CAP
CELLS = 128
SPAN = SLOTS * CELLS
OCH = 76
OCH_PAD = 80
TAPS = [(row, col) for row in (-1, 0, 1) for col in (-1, 0, 1)]
BF16 = jnp.bfloat16
F32 = jnp.float32
WHOLE = pl.BlockSpec(memory_space=pltpu.VMEM)
FAR = pl.BlockSpec(memory_space=pltpu.HBM)


def passed_along(value, axis, by):
    devices = lax.axis_size(axis)
    return lax.ppermute(value, axis, [(i, (i + by) % devices) for i in range(devices)])


def fourier_tables():
    product = np.arange(MMAX)[:, None] * np.arange(MERIDIAN_TOTAL)[None, :] % MERIDIAN_TOTAL
    angles = 2.0 * np.pi / MERIDIAN_TOTAL * product
    analysis = np.stack([np.cos(angles), -np.sin(angles)], axis=1) / MERIDIAN_TOTAL
    weights = np.where(np.arange(MMAX) == 0, 1.0, 2.0)[:, None]
    synthesis = np.stack([weights * np.cos(angles), -weights * np.sin(angles)], axis=1)
    return (
        analysis.reshape(2 * MMAX, MERIDIAN_TOTAL).astype(BF16),
        synthesis.reshape(2 * MMAX, MERIDIAN_TOTAL).T.astype(BF16),
    )


def legendre_tables(latitudes):
    theta = np.pi / latitudes * (np.arange(latitudes) + 0.5)
    cosine = np.cos(theta)[None, :]
    sine = np.sin(theta)
    counter = np.arange(1, MMAX)
    totals = np.concatenate([[0.0], np.cumsum(np.log((2.0 * counter - 1.0) / (2.0 * counter)))])
    order = np.arange(MMAX, dtype=np.float64)[:, None]
    diagonal = np.exp(
        0.5 * (np.log((2.0 * order + 1.0) / (4.0 * np.pi)) + totals[:, None])
        + order * np.log(sine)[None, :]
    )
    values = np.zeros((MMAX, LMAX, latitudes))
    latest = np.zeros((MMAX, latitudes))
    before = np.zeros((MMAX, latitudes))
    for degree in range(LMAX):
        lowered = (degree - 1.0) ** 2
        upward = np.sqrt(
            max(4.0 * degree * degree - 1.0, 0.0) / np.maximum(degree * degree - order * order, 1.0)
        )
        damping = np.sqrt(
            np.maximum(lowered - order * order, 0.0) / max(4.0 * lowered - 1.0, 1.0)
        )
        current = upward * (cosine * latest - damping * before)
        current = np.where(degree == order, diagonal, current)
        current = np.where(degree < order, 0.0, current)
        values[:, degree, :] = current
        latest, before = current, latest
    quadrature = 2.0 * np.pi * np.pi / latitudes * sine
    forward = (values * quadrature[None, None, :]).astype(BF16)
    backward = np.transpose(values, (0, 2, 1)).astype(BF16)
    return forward, backward


def gelu(x):
    inner = math.sqrt(2.0 / math.pi) * (x + 0.044715 * (x * x * x))
    return 0.5 * x * (1.0 + jnp.tanh(inner))


def tap_masks(width):
    lane = lax.broadcasted_iota(jnp.int32, (1, width), 1) % CELLS
    row, col = lane // 16, lane % 16
    masks = []
    for down, right in TAPS:
        inside = (row + down >= 0) & (row + down < 8) & (col + right >= 0) & (col + right < 16)
        masks.append(inside)
    return masks


def shifted(x, tap, mask):
    by = 16 * tap[0] + tap[1]
    if by == 0:
        return x
    rolled = pltpu.roll(x, (-by) % x.shape[1], 1)
    return jnp.where(mask, rolled, 0.0)


def in_three(x):
    high = x.astype(BF16)
    rest = x - high.astype(F32)
    middle = rest.astype(BF16)
    return high, middle, (rest - middle.astype(F32)).astype(BF16)


def begin(copies, sems):
    started = [
        pltpu.make_async_copy(source, target, sems.at[i])
        for i, (source, target) in enumerate(copies)
    ]
    for one in started:
        one.start()
    return started


def normalised(x, scale):
    centered = x - jnp.mean(x, axis=-1, keepdims=True)
    spread = jnp.mean(centered * centered, axis=-1, keepdims=True)
    return (centered * lax.rsqrt(spread + 1e-05) * scale).astype(BF16)


def analysis_kernel(air_any, scale_ref, table_any, spectra_ref, air_ref, table_ref, sems):
    rows = air_ref.shape[0]
    groups = spectra_ref.shape[0]
    copies = begin(
        [(air_any.at[j], air_ref.at[j]) for j in range(rows)] + [(table_any, table_ref)], sems
    )
    scale = scale_ref[...].reshape(1, scale_ref.shape[0])
    for pair in range(rows // 2):
        both = []
        for j in (2 * pair, 2 * pair + 1):
            copies[j].wait()
            normed = normalised(air_ref[j].astype(F32), scale)
            if j == 0:
                copies[rows].wait()
            out = jnp.dot(table_ref[...], normed, preferred_element_type=F32)
            both.append(out.reshape(groups, 8, out.shape[1]))
        block = jnp.concatenate(both, axis=1)
        spectra_ref[:, 16 * pair : 16 * (pair + 1), :] = block.astype(BF16)


def local_kernel(
    air_any, scale_ref, bypass_ref, exit_ref, exchange_ref, skip_ref, flux_ref, wide_ref,
    air_ref, sems,
):
    rows = air_ref.shape[0]
    copies = begin([(air_any.at[j], air_ref.at[j]) for j in range(rows)], sems)
    scale = scale_ref[...].reshape(1, scale_ref.shape[0])
    channels = exit_ref.shape[0]
    dims = (((1,), (1,)), ((), ()))
    through = lax.dot_general(
        exit_ref[...], exchange_ref[...], dims, preferred_element_type=F32
    )
    high = through.astype(BF16)
    low = (through - high.astype(F32)).astype(BF16)
    wide_ref[:, :channels] = exit_ref[...]
    wide_ref[:, channels:] = jnp.concatenate(
        [high.astype(F32), low.astype(F32), jnp.zeros((channels, 128 - 2 * FC), F32)], axis=1
    ).astype(BF16)
    for j in range(rows):
        copies[j].wait()
        own = air_ref[j]
        normed = normalised(own.astype(F32), scale)
        skip_ref[j] = jnp.dot(normed, bypass_ref[...], preferred_element_type=F32)
        flux_ref[FC * j : FC * (j + 1), :] = lax.dot_general(
            exchange_ref[...], own, dims, preferred_element_type=F32
        )


def legendre_kernel(x_ref, forward_ref, backward_ref, gains_ref, out_ref, work):
    groups, chunk, channels = x_ref.shape
    total = groups * chunk
    latitudes = total // 8
    for third in range(channels // 128):
        lanes = slice(128 * third, 128 * (third + 1))
        work[third] = x_ref[:, :, lanes].astype(F32).reshape(total, 128)
        gains = gains_ref[:, lanes]
        gains = jnp.concatenate([gains, gains], axis=1)
        for m in range(4):
            real, imaginary = (pl.ds(2 * m + r, latitudes, stride=8) for r in (0, 1))
            own = jnp.concatenate(
                [work[third, real, :], work[third, imaginary, :]], axis=1
            ).astype(BF16)
            coefficients = jnp.dot(forward_ref[m], own, preferred_element_type=F32)
            shaped = (coefficients * gains).astype(BF16)
            back = jnp.dot(backward_ref[m], shaped, preferred_element_type=F32)
            work[third, real, :] = back[:, :128]
            work[third, imaginary, :] = back[:, 128:]
        out_ref[:, :, lanes] = work[third].reshape(groups, chunk, 128).astype(BF16)


def ocean_kernel(depth_ref, *refs):
    pieces, (weight_ref, out_ref, top_ref, columns) = refs[:NEAR], refs[NEAR:]
    masks = tap_masks(CELLS)
    level = lax.broadcasted_iota(jnp.int32, (OCH, CELLS), 0) % LEV
    for slot in range(SLOTS):
        lanes = slice(CELLS * slot, CELLS * (slot + 1))
        state = pieces[slot // CAP][slot % CAP].astype(F32)
        top_ref[:, lanes] = state[0:1]
        state = jnp.where(level < depth_ref[slot], state, 0.0)
        state = jnp.concatenate([state, jnp.zeros((OCH_PAD - OCH, CELLS), F32)], axis=0)
        for q, tap in enumerate(TAPS):
            moved = shifted(state, tap, masks[q]).astype(BF16)
            columns[OCH_PAD * q : OCH_PAD * (q + 1), lanes] = moved
    for at in range(0, SPAN, 512):
        out_ref[:, at : at + 512] = jnp.dot(
            weight_ref[...], columns[:, at : at + 512], preferred_element_type=F32
        )


def surface_kernel(rows_ref, *refs):
    count = 11
    sources, (updated_any, tiles_ref), held, (updated_ref, flux, sst, sems, out_sems) = (
        refs[:count], refs[count : count + 2], refs[count + 2 : 2 * count + 2],
        refs[2 * count + 2 :],
    )
    leaving = []
    copies = begin(list(zip(sources, held)), sems)
    (
        synthesis_ref, skip_ref, air_ref, wide_ref, air_flux_ref, place_ref, group_ref,
        forcing_weight_ref, wet_ref, decode_ref, top_ref,
    ) = held
    latitude_rows, longitudes, channels = air_ref.shape
    groups = rows_ref.shape[0]
    pairs = []
    for pair in range(latitude_rows // 2):
        both = rows_ref[:, 16 * pair : 16 * (pair + 1), :].astype(F32)
        pairs.extend([both[:, :8], both[:, 8:]])
    copies[0].wait()
    for j in range(latitude_rows):
        own = pairs[j].reshape(8 * groups, channels).astype(BF16)
        spectral = jnp.dot(synthesis_ref[...], own, preferred_element_type=F32)
        if j == 0:
            for one in copies[1:4]:
                one.wait()
        mixed = gelu(spectral + skip_ref[j]).astype(BF16)
        wide = jnp.dot(mixed, wide_ref[...], preferred_element_type=F32)
        updated_ref[j] = air_ref[j].astype(F32) + wide[:, :channels]
        leave = pltpu.make_async_copy(updated_ref.at[j], updated_any.at[j], out_sems.at[j])
        leave.start()
        leaving.append(leave)
        narrow = jnp.concatenate(
            [wide[:, channels:], jnp.zeros((384 - longitudes, 128), F32)], axis=0
        )
        turned = jnp.transpose(narrow)
        if j == 0:
            copies[4].wait()
        extra = jnp.concatenate(
            [air_flux_ref[FC * j : FC * (j + 1), :], jnp.zeros((FC, 384 - longitudes), F32)], axis=1
        )
        total = turned[:FC] + turned[FC : 2 * FC] + extra
        for part in range(3):
            at = FC * (part * latitude_rows + j)
            flux[at : at + FC, :] = total[:, 128 * part : 128 * (part + 1)]
    for one in copies[5:]:
        one.wait()
    spread = jnp.dot(flux[...].astype(BF16), place_ref[...], preferred_element_type=F32)
    group = group_ref[...]
    forcing = jnp.zeros((FC, SPAN), F32)
    for at in range(3 * latitude_rows):
        forcing = forcing + jnp.where(group == at, spread[FC * at : FC * (at + 1), :], 0.0)
    masks = tap_masks(SPAN)
    columns = jnp.concatenate(
        [shifted(forcing, tap, masks[q]) for q, tap in enumerate(TAPS)], axis=0
    ).astype(BF16)
    hidden = gelu(
        wet_ref[...] + jnp.dot(forcing_weight_ref[...], columns, preferred_element_type=F32)
    ).astype(BF16)
    partial = jnp.dot(decode_ref[...], hidden, preferred_element_type=F32)
    change = jnp.zeros((1, SPAN), F32)
    for q, tap in enumerate(TAPS):
        change = change + shifted(partial[q : q + 1, :], tap, masks[q])
    surface = top_ref[...] + change
    for slot in range(SLOTS):
        sst[slot : slot + 1, :] = surface[:, CELLS * slot : CELLS * (slot + 1)]
    tiles = sst[...].astype(BF16)
    for member in range(tiles_ref.shape[0]):
        tiles_ref[member] = tiles
    for one in leaving:
        one.wait()


def imprint_kernel(
    updated_any, tiles_ref, cell_any, slot_any, imprint_ref, out_any,
    updated_ref, cell_ref, slot_ref, out_ref, sems, out_sems,
):
    rows, _, channels = updated_ref.shape
    copies = begin(
        [(cell_any, cell_ref), (slot_any, slot_ref)]
        + [(updated_any.at[j], updated_ref.at[j]) for j in range(rows)],
        sems,
    )
    tiles = tiles_ref[0]
    tripled = jnp.concatenate([tiles, tiles, tiles], axis=0)
    pieces = in_three(imprint_ref[...].reshape(1, channels))
    imprint = jnp.concatenate(
        [jnp.broadcast_to(piece, (SLOTS, channels)) for piece in pieces], axis=0
    )
    copies[0].wait()
    copies[1].wait()
    leaving = []
    for j in range(rows):
        picked = lax.dot_general(
            cell_ref[j], tripled, (((1,), (1,)), ((), ())), preferred_element_type=F32
        )
        chosen = picked.astype(BF16) * slot_ref[j]
        warmth = jnp.dot(chosen, imprint, preferred_element_type=F32)
        copies[2 + j].wait()
        out_ref[j] = (updated_ref[j] + warmth).astype(BF16)
        leave = pltpu.make_async_copy(out_ref.at[j], out_any.at[j], out_sems.at[j])
        leave.start()
        leaving.append(leave)
    for one in leaving:
        one.wait()


def mean_kernel(tiles_ref, cell_ref, slot_ref, out_ref):
    members = tiles_ref.shape[0]
    total = jnp.zeros(tiles_ref.shape[1:], F32)
    for member in range(members):
        total = total + tiles_ref[member].astype(F32)
    pieces = jnp.concatenate(in_three(total), axis=0)
    for j in range(cell_ref.shape[0]):
        picked = lax.dot_general(
            pieces, cell_ref[j], (((1,), (1,)), ((), ())), preferred_element_type=F32
        )
        joined = picked[:SLOTS] + picked[SLOTS : 2 * SLOTS] + picked[2 * SLOTS :]
        kept = jnp.where(slot_ref[j] > 0, joined, 0.0)
        out_ref[j : j + 1, :] = jnp.sum(kept, axis=0, keepdims=True) / members


def call(kernel, outs, operands, flops, scratch=(), limit=32, specs=None, out_specs=None):
    size = sum(math.prod(o.shape) * o.dtype.itemsize for o in list(outs) + list(operands))
    return pl.pallas_call(
        kernel,
        out_shape=outs if len(outs) > 1 else outs[0],
        in_specs=specs or [WHOLE] * len(operands),
        out_specs=out_specs or ([WHOLE] * len(outs) if len(outs) > 1 else WHOLE),
        scratch_shapes=list(scratch),
        compiler_params=pltpu.CompilerParams(vmem_limit_bytes=limit * 1024 * 1024),
        cost_estimate=pl.CostEstimate(flops=flops, bytes_accessed=size, transcendentals=0),
    )(*operands)


def held(operands):
    return [pltpu.VMEM(o.shape, o.dtype) for o in operands]


def shards(
    air_ensemble,
    sea_indicator,
    layernorm_scaling,
    harmonic_damping_factor,
    bypass_factor,
    core_exit_factor,
    air_to_exchange_factor,
    sea_heat_imprint,
    sea_ensemble_arrays,
    input_to_hidden_kernel,
    hidden_to_change_kernel,
    patch_exchange_pick,
    node_sea_pick,
    patch_holder_shift,
    wet_depth_layers,
):
    bands = lax.axis_size("space")
    members = lax.axis_size("member")
    air = air_ensemble[0]
    latitude_rows, longitudes, channels = air.shape
    latitudes = latitude_rows * bands
    hidden_channels = input_to_hidden_kernel.shape[1]
    per_device = MMAX // bands
    chunk = 2 * per_device * latitude_rows
    shape = jax.ShapeDtypeStruct

    analysis, synthesis = (jnp.asarray(t) for t in fourier_tables())
    spectra = call(
        analysis_kernel,
        [shape((bands, chunk, channels), BF16)],
        [air, layernorm_scaling, analysis],
        2 * 2 * MMAX * latitude_rows * longitudes * channels,
        held([air, analysis]) + [pltpu.SemaphoreType.DMA((latitude_rows + 1,))],
        specs=[FAR, WHOLE, FAR],
    )
    gathered = lax.all_to_all(spectra, "space", split_axis=0, concat_axis=0, tiled=True)

    slots = sea_ensemble_arrays[0]
    pieces = [slots[:CAP]] + [
        passed_along(slots[offset * CAP : (offset + 1) * CAP], "space", -offset)
        for offset in range(1, NEAR)
    ]
    forward, backward = (jnp.asarray(t) for t in legendre_tables(latitudes))
    first = lax.axis_index("space") * per_device
    forward = lax.dynamic_slice_in_dim(forward, first, per_device, 0)
    backward = lax.dynamic_slice_in_dim(backward, first, per_device, 0)
    skip, air_flux, wide = call(
        local_kernel,
        [
            shape(air.shape, F32),
            shape((FC * latitude_rows, longitudes), F32),
            shape((channels, channels + 128), BF16),
        ],
        [air, layernorm_scaling, bypass_factor, core_exit_factor, air_to_exchange_factor.T],
        2 * latitude_rows * longitudes * channels * channels,
        held([air]) + [pltpu.SemaphoreType.DMA((latitude_rows,))],
        specs=[FAR] + [WHOLE] * 4,
    )
    filtered = call(
        legendre_kernel,
        [shape((bands, chunk, channels), BF16)],
        [gathered, forward, backward, harmonic_damping_factor],
        2 * 2 * 2 * per_device * LMAX * latitudes * channels,
        [pltpu.VMEM((channels // 128, bands * chunk, 128), F32)],
    )
    returned = lax.all_to_all(filtered, "space", split_axis=0, concat_axis=0, tiled=True)
    offsets = patch_holder_shift[:, 0]
    earlier = jnp.tril(jnp.ones((HOME_DEV, HOME_DEV), jnp.int32), -1)
    positions = jnp.sum((offsets[:, None] == offsets[None, :]).astype(jnp.int32) * earlier, axis=1)
    targets = offsets * CAP + positions
    selected = targets[None, :] == jnp.arange(SLOTS, dtype=jnp.int32)[:, None]
    depths = jnp.sum(jnp.where(selected, wet_depth_layers[None, :], 0), axis=1)
    kernel = jnp.transpose(input_to_hidden_kernel, (1, 0, 2))
    state_weight = jnp.pad(kernel[:, :, :OCH], ((0, 0), (0, 0), (0, OCH_PAD - OCH))).reshape(
        hidden_channels, -1
    )
    forcing_weight = kernel[:, :, OCH:].reshape(hidden_channels, -1)
    decode_weight = jnp.pad(hidden_to_change_kernel, ((0, 16 - len(TAPS)), (0, 0)))
    wet, top = call(
        ocean_kernel,
        [shape((hidden_channels, SPAN), F32), shape((1, SPAN), F32)],
        [depths, *pieces, state_weight],
        2 * hidden_channels * len(TAPS) * OCH_PAD * SPAN,
        [pltpu.VMEM((len(TAPS) * OCH_PAD, SPAN), BF16)],
        specs=[pl.BlockSpec(memory_space=pltpu.SMEM)] + [WHOLE] * (NEAR + 1),
    )
    picks = jnp.sum(jnp.where(selected[:, :, None], patch_exchange_pick[None], 0), axis=1)
    picks = picks.reshape(1, SPAN)
    line, column = picks // longitudes, picks % longitudes
    group = column // 128 * latitude_rows + line
    place = (column % 128 == jnp.arange(128, dtype=jnp.int32)[:, None]).astype(BF16)
    tile = node_sea_pick // CELLS
    holder = jnp.sum(
        jnp.where(
            tile[:, :, None] == jnp.arange(HOME_DEV, dtype=jnp.int32), targets[None, None, :], 0
        ),
        axis=2,
    )
    holder = jnp.where(sea_indicator > 0, holder, -1)
    cell = (
        (node_sea_pick % CELLS)[:, :, None] == jnp.arange(CELLS, dtype=jnp.int32)
    ).astype(BF16)
    slot_of = (
        holder[:, :, None] == jnp.arange(3 * SLOTS, dtype=jnp.int32) % SLOTS
    ).astype(BF16)
    slot_rows = (
        holder[:, None, :] == jnp.arange(SLOTS, dtype=jnp.int32)[None, :, None]
    ).astype(F32)
    operands = [
        synthesis, skip, air, wide, air_flux, place, group, forcing_weight, wet, decode_weight, top
    ]
    updated, tiles = call(
        surface_kernel,
        [shape(air.shape, F32), shape((members, SLOTS, CELLS), BF16)],
        [returned] + operands,
        2 * latitude_rows * longitudes * channels * (channels + 2 * MMAX),
        held(operands)
        + [
            pltpu.VMEM(air.shape, F32),
            pltpu.VMEM((3 * FC * latitude_rows, 128), F32),
            pltpu.VMEM((SLOTS, CELLS), F32),
            pltpu.SemaphoreType.DMA((len(operands),)),
            pltpu.SemaphoreType.DMA((latitude_rows,)),
        ],
        specs=[WHOLE] + [FAR] * len(operands),
        out_specs=[FAR, WHOLE],
    )
    everyone = lax.all_to_all(tiles, "member", split_axis=0, concat_axis=0, tiled=True)
    out = call(
        imprint_kernel,
        [shape(air.shape, BF16)],
        [updated, tiles, cell, slot_of, sea_heat_imprint],
        2 * latitude_rows * longitudes * channels * 256,
        held([updated, cell, slot_of, air])
        + [
            pltpu.SemaphoreType.DMA((latitude_rows + 2,)),
            pltpu.SemaphoreType.DMA((latitude_rows,)),
        ],
        specs=[FAR, WHOLE, FAR, FAR, WHOLE],
        out_specs=FAR,
    )
    mean = call(
        mean_kernel,
        [shape((latitude_rows, longitudes), F32)],
        [everyone, cell, slot_rows],
        2 * 3 * SLOTS * CELLS * latitude_rows * longitudes,
    )
    return (out[None], mean)


def solution(mesh):
    in_specs = (
        P("member", "space", None, None),
        P("space", None),
        P(),
        P(),
        P(),
        P(),
        P(),
        P(),
        P("member", "space", None, None),
        P(),
        P(),
        P("space", None),
        P("space", None),
        P("space", None),
        P("space"),
    )
    out_specs = (P("member", "space", None, None), P("space", None))
    return jax.shard_map(shards, mesh=mesh, in_specs=in_specs, out_specs=out_specs, check_vma=False)
```

```python
import math

import jax
import jax.numpy as jnp
import numpy as np
from jax import lax
from jax.experimental import pallas as pl
from jax.experimental.pallas import tpu as pltpu
from jax.sharding import PartitionSpec as P

MERIDIAN_TOTAL = 360
MMAX = 128
LMAX = 128
FC = 8
LEV = 19
CAP = 2
NEAR = 8
HOME_DEV = 14
SLOTS = NEAR * CAP
CELLS = 128
SPAN = SLOTS * CELLS
OCH = 76
OCH_PAD = 80
TAPS = [(row, col) for row in (-1, 0, 1) for col in (-1, 0, 1)]
LATE = 6
BF16 = jnp.bfloat16
F32 = jnp.float32
WHOLE = pl.BlockSpec(memory_space=pltpu.VMEM)
FAR = pl.BlockSpec(memory_space=pltpu.HBM)


def passed_along(value, axis, by):
    devices = lax.axis_size(axis)
    return lax.ppermute(value, axis, [(i, (i + by) % devices) for i in range(devices)])


def fourier_tables():
    product = np.arange(MMAX)[:, None] * np.arange(MERIDIAN_TOTAL)[None, :] % MERIDIAN_TOTAL
    angles = 2.0 * np.pi / MERIDIAN_TOTAL * product
    analysis = np.stack([np.cos(angles), -np.sin(angles)], axis=1) / MERIDIAN_TOTAL
    weights = np.where(np.arange(MMAX) == 0, 1.0, 2.0)[:, None]
    synthesis = np.stack([weights * np.cos(angles), -weights * np.sin(angles)], axis=1)
    return (
        analysis.reshape(2 * MMAX, MERIDIAN_TOTAL).astype(BF16),
        synthesis.reshape(2 * MMAX, MERIDIAN_TOTAL).T.astype(BF16),
    )


def legendre_tables(latitudes):
    theta = np.pi / latitudes * (np.arange(latitudes) + 0.5)
    cosine = np.cos(theta)[None, :]
    sine = np.sin(theta)
    counter = np.arange(1, MMAX)
    totals = np.concatenate([[0.0], np.cumsum(np.log((2.0 * counter - 1.0) / (2.0 * counter)))])
    order = np.arange(MMAX, dtype=np.float64)[:, None]
    diagonal = np.exp(
        0.5 * (np.log((2.0 * order + 1.0) / (4.0 * np.pi)) + totals[:, None])
        + order * np.log(sine)[None, :]
    )
    values = np.zeros((MMAX, LMAX, latitudes))
    latest = np.zeros((MMAX, latitudes))
    before = np.zeros((MMAX, latitudes))
    for degree in range(LMAX):
        lowered = (degree - 1.0) ** 2
        upward = np.sqrt(
            max(4.0 * degree * degree - 1.0, 0.0) / np.maximum(degree * degree - order * order, 1.0)
        )
        damping = np.sqrt(
            np.maximum(lowered - order * order, 0.0) / max(4.0 * lowered - 1.0, 1.0)
        )
        current = upward * (cosine * latest - damping * before)
        current = np.where(degree == order, diagonal, current)
        current = np.where(degree < order, 0.0, current)
        values[:, degree, :] = current
        latest, before = current, latest
    quadrature = 2.0 * np.pi * np.pi / latitudes * sine
    forward = (values * quadrature[None, None, :]).astype(BF16)
    backward = np.transpose(values, (0, 2, 1)).astype(BF16)
    return forward, backward


def gelu(x):
    inner = math.sqrt(2.0 / math.pi) * (x + 0.044715 * (x * x * x))
    return 0.5 * x * (1.0 + jnp.tanh(inner))


def tap_masks(width):
    lane = lax.broadcasted_iota(jnp.int32, (1, width), 1) % CELLS
    row, col = lane // 16, lane % 16
    masks = []
    for down, right in TAPS:
        inside = (row + down >= 0) & (row + down < 8) & (col + right >= 0) & (col + right < 16)
        masks.append(inside)
    return masks


def shifted(x, tap, mask):
    by = 16 * tap[0] + tap[1]
    if by == 0:
        return x
    rolled = pltpu.roll(x, (-by) % x.shape[1], 1)
    return jnp.where(mask, rolled, 0.0)


def in_three(x):
    high = x.astype(BF16)
    rest = x - high.astype(F32)
    middle = rest.astype(BF16)
    return high, middle, (rest - middle.astype(F32)).astype(BF16)


def begin(copies, sems):
    started = [
        pltpu.make_async_copy(source, target, sems.at[i])
        for i, (source, target) in enumerate(copies)
    ]
    for one in started:
        one.start()
    return started


def normalised(x, scale):
    centered = x - jnp.mean(x, axis=-1, keepdims=True)
    spread = jnp.mean(centered * centered, axis=-1, keepdims=True)
    return (centered * lax.rsqrt(spread + 1e-05) * scale).astype(BF16)


def analysis_kernel(air_any, scale_ref, table_any, spectra_ref, air_ref, table_ref, sems):
    rows = air_ref.shape[0]
    groups = spectra_ref.shape[0]
    copies = begin(
        [(air_any.at[j], air_ref.at[j]) for j in range(rows)] + [(table_any, table_ref)], sems
    )
    scale = scale_ref[...].reshape(1, scale_ref.shape[0])
    for pair in range(rows // 2):
        both = []
        for j in (2 * pair, 2 * pair + 1):
            copies[j].wait()
            normed = normalised(air_ref[j].astype(F32), scale)
            if j == 0:
                copies[rows].wait()
            out = jnp.dot(table_ref[...], normed, preferred_element_type=F32)
            both.append(out.reshape(groups, 8, out.shape[1]))
        block = jnp.concatenate(both, axis=1)
        spectra_ref[:, 16 * pair : 16 * (pair + 1), :] = block.astype(BF16)


def local_kernel(
    air_any, scale_ref, bypass_ref, exit_ref, exchange_ref, skip_ref, flux_ref, wide_ref,
    air_ref, sems,
):
    rows = air_ref.shape[0]
    copies = begin([(air_any.at[j], air_ref.at[j]) for j in range(rows)], sems)
    scale = scale_ref[...].reshape(1, scale_ref.shape[0])
    channels = exit_ref.shape[0]
    dims = (((1,), (1,)), ((), ()))
    through = lax.dot_general(
        exit_ref[...], exchange_ref[...], dims, preferred_element_type=F32
    )
    high = through.astype(BF16)
    low = (through - high.astype(F32)).astype(BF16)
    wide_ref[:, :channels] = exit_ref[...]
    wide_ref[:, channels:] = jnp.concatenate(
        [high.astype(F32), low.astype(F32), jnp.zeros((channels, 128 - 2 * FC), F32)], axis=1
    ).astype(BF16)
    for j in range(rows):
        copies[j].wait()
        own = air_ref[j]
        normed = normalised(own.astype(F32), scale)
        skip_ref[j] = jnp.dot(normed, bypass_ref[...], preferred_element_type=F32)
        flux_ref[FC * j : FC * (j + 1), :] = lax.dot_general(
            exchange_ref[...], own, dims, preferred_element_type=F32
        )


def legendre_kernel(x_ref, forward_ref, backward_ref, gains_ref, out_ref, work):
    groups, chunk, channels = x_ref.shape
    total = groups * chunk
    latitudes = total // 8
    for third in range(channels // 128):
        lanes = slice(128 * third, 128 * (third + 1))
        work[third] = x_ref[:, :, lanes].astype(F32).reshape(total, 128)
        gains = gains_ref[:, lanes]
        gains = jnp.concatenate([gains, gains], axis=1)
        for m in range(4):
            real, imaginary = (pl.ds(2 * m + r, latitudes, stride=8) for r in (0, 1))
            own = jnp.concatenate(
                [work[third, real, :], work[third, imaginary, :]], axis=1
            ).astype(BF16)
            coefficients = jnp.dot(forward_ref[m], own, preferred_element_type=F32)
            shaped = (coefficients * gains).astype(BF16)
            back = jnp.dot(backward_ref[m], shaped, preferred_element_type=F32)
            work[third, real, :] = back[:, :128]
            work[third, imaginary, :] = back[:, 128:]
        out_ref[:, :, lanes] = work[third].reshape(groups, chunk, 128).astype(BF16)


def ocean_kernel(depth_ref, *refs):
    pieces, (weight_ref, out_ref, top_ref, columns) = refs[:NEAR], refs[NEAR:]
    masks = tap_masks(CELLS)
    level = lax.broadcasted_iota(jnp.int32, (OCH, CELLS), 0) % LEV
    for slot in range(SLOTS):
        lanes = slice(CELLS * slot, CELLS * (slot + 1))
        state = pieces[slot // CAP][slot % CAP].astype(F32)
        top_ref[:, lanes] = state[0:1]
        state = jnp.where(level < depth_ref[slot], state, 0.0)
        state = jnp.concatenate([state, jnp.zeros((OCH_PAD - OCH, CELLS), F32)], axis=0)
        for q, tap in enumerate(TAPS):
            moved = shifted(state, tap, masks[q]).astype(BF16)
            columns[OCH_PAD * q : OCH_PAD * (q + 1), lanes] = moved
    for at in range(0, SPAN, 512):
        out_ref[:, at : at + 512] = jnp.dot(
            weight_ref[...], columns[:, at : at + 512], preferred_element_type=F32
        )


def surface_kernel(*refs):
    count = 12
    sources, (updated_any, tiles_ref), held, (updated_ref, flux, sst, sems, out_sems) = (
        refs[:count], refs[count : count + 2], refs[count + 2 : 2 * count + 2],
        refs[2 * count + 2 :],
    )
    leaving = []
    copies = begin(list(zip(sources, held)), sems)
    (
        rows_ref, synthesis_ref, skip_ref, air_ref, wide_ref, air_flux_ref, place_ref, group_ref,
        forcing_weight_ref, wet_ref, decode_ref, top_ref,
    ) = held
    latitude_rows, longitudes, channels = air_ref.shape
    groups = rows_ref.shape[0]
    pairs = []
    copies[0].wait()
    for pair in range(latitude_rows // 2):
        both = rows_ref[:, 16 * pair : 16 * (pair + 1), :].astype(F32)
        pairs.extend([both[:, :8], both[:, 8:]])
    copies[1].wait()
    for j in range(latitude_rows):
        own = pairs[j].reshape(8 * groups, channels).astype(BF16)
        spectral = jnp.dot(synthesis_ref[...], own, preferred_element_type=F32)
        if j == 0:
            for one in copies[2:5]:
                one.wait()
        mixed = gelu(spectral + skip_ref[j]).astype(BF16)
        wide = jnp.dot(mixed, wide_ref[...], preferred_element_type=F32)
        updated_ref[j] = air_ref[j].astype(F32) + wide[:, :channels]
        leave = pltpu.make_async_copy(updated_ref.at[j], updated_any.at[j], out_sems.at[j])
        leave.start()
        leaving.append(leave)
        narrow = jnp.concatenate(
            [wide[:, channels:], jnp.zeros((384 - longitudes, 128), F32)], axis=0
        )
        turned = jnp.transpose(narrow)
        if j == 0:
            copies[5].wait()
        extra = jnp.concatenate(
            [air_flux_ref[FC * j : FC * (j + 1), :], jnp.zeros((FC, 384 - longitudes), F32)], axis=1
        )
        total = turned[:FC] + turned[FC : 2 * FC] + extra
        for part in range(3):
            at = FC * (part * latitude_rows + j)
            flux[at : at + FC, :] = total[:, 128 * part : 128 * (part + 1)]
    for one in copies[6:]:
        one.wait()
    spread = jnp.dot(flux[...].astype(BF16), place_ref[...], preferred_element_type=F32)
    group = group_ref[...]
    forcing = jnp.zeros((FC, SPAN), F32)
    for at in range(3 * latitude_rows):
        forcing = forcing + jnp.where(group == at, spread[FC * at : FC * (at + 1), :], 0.0)
    masks = tap_masks(SPAN)
    columns = jnp.concatenate(
        [shifted(forcing, tap, masks[q]) for q, tap in enumerate(TAPS)], axis=0
    ).astype(BF16)
    hidden = gelu(
        wet_ref[...] + jnp.dot(forcing_weight_ref[...], columns, preferred_element_type=F32)
    ).astype(BF16)
    partial = jnp.dot(decode_ref[...], hidden, preferred_element_type=F32)
    change = jnp.zeros((1, SPAN), F32)
    for q, tap in enumerate(TAPS):
        change = change + shifted(partial[q : q + 1, :], tap, masks[q])
    surface = top_ref[...] + change
    for slot in range(SLOTS):
        sst[slot : slot + 1, :] = surface[:, CELLS * slot : CELLS * (slot + 1)]
    tiles = sst[...].astype(BF16)
    for member in range(tiles_ref.shape[0]):
        tiles_ref[member] = tiles
    for one in leaving:
        one.wait()


def imprint_kernel(
    updated_any, tiles_ref, cell_any, slot_any, imprint_ref, out_any,
    updated_ref, cell_ref, slot_ref, out_ref, sems, out_sems,
):
    rows, _, channels = updated_ref.shape
    copies = begin(
        [(cell_any, cell_ref), (slot_any, slot_ref)]
        + [(updated_any.at[j], updated_ref.at[j]) for j in range(rows)],
        sems,
    )
    tiles = tiles_ref[0]
    tripled = jnp.concatenate([tiles, tiles, tiles], axis=0)
    pieces = in_three(imprint_ref[...].reshape(1, channels))
    imprint = jnp.concatenate(
        [jnp.broadcast_to(piece, (SLOTS, channels)) for piece in pieces], axis=0
    )
    copies[0].wait()
    copies[1].wait()
    leaving = []
    for j in range(rows):
        picked = lax.dot_general(
            cell_ref[j], tripled, (((1,), (1,)), ((), ())), preferred_element_type=F32
        )
        chosen = picked.astype(BF16) * slot_ref[j]
        warmth = jnp.dot(chosen, imprint, preferred_element_type=F32)
        copies[2 + j].wait()
        out_ref[j] = (updated_ref[j] + warmth).astype(BF16)
        leave = pltpu.make_async_copy(out_ref.at[j], out_any.at[j], out_sems.at[j])
        leave.start()
        leaving.append(leave)
    for one in leaving:
        one.wait()


def mean_kernel(tiles_ref, cell_ref, slot_ref, out_ref):
    members = tiles_ref.shape[0]
    total = jnp.zeros(tiles_ref.shape[1:], F32)
    for member in range(members):
        total = total + tiles_ref[member].astype(F32)
    pieces = jnp.concatenate(in_three(total), axis=0)
    for j in range(cell_ref.shape[0]):
        picked = lax.dot_general(
            pieces, cell_ref[j], (((1,), (1,)), ((), ())), preferred_element_type=F32
        )
        joined = picked[:SLOTS] + picked[SLOTS : 2 * SLOTS] + picked[2 * SLOTS :]
        kept = jnp.where(slot_ref[j] > 0, joined, 0.0)
        out_ref[j : j + 1, :] = jnp.sum(kept, axis=0, keepdims=True) / members


def call(kernel, outs, operands, flops, scratch=(), limit=56, specs=None, out_specs=None):
    size = sum(math.prod(o.shape) * o.dtype.itemsize for o in list(outs) + list(operands))
    return pl.pallas_call(
        kernel,
        out_shape=outs if len(outs) > 1 else outs[0],
        in_specs=specs or [WHOLE] * len(operands),
        out_specs=out_specs or ([WHOLE] * len(outs) if len(outs) > 1 else WHOLE),
        scratch_shapes=list(scratch),
        compiler_params=pltpu.CompilerParams(vmem_limit_bytes=limit * 1024 * 1024),
        cost_estimate=pl.CostEstimate(flops=flops, bytes_accessed=size, transcendentals=0),
    )(*operands)


def held(operands):
    return [pltpu.VMEM(o.shape, o.dtype) for o in operands]


def shards(
    air_ensemble,
    sea_indicator,
    layernorm_scaling,
    harmonic_damping_factor,
    bypass_factor,
    core_exit_factor,
    air_to_exchange_factor,
    sea_heat_imprint,
    sea_ensemble_arrays,
    input_to_hidden_kernel,
    hidden_to_change_kernel,
    patch_exchange_pick,
    node_sea_pick,
    patch_holder_shift,
    wet_depth_layers,
):
    bands = lax.axis_size("space")
    members = lax.axis_size("member")
    air = air_ensemble[0]
    latitude_rows, longitudes, channels = air.shape
    latitudes = latitude_rows * bands
    hidden_channels = input_to_hidden_kernel.shape[1]
    per_device = MMAX // bands
    chunk = 2 * per_device * latitude_rows
    shape = jax.ShapeDtypeStruct

    analysis, synthesis = (jnp.asarray(t) for t in fourier_tables())
    spectra = call(
        analysis_kernel,
        [shape((bands, chunk, channels), BF16)],
        [air, layernorm_scaling, analysis],
        2 * 2 * MMAX * latitude_rows * longitudes * channels,
        held([air, analysis]) + [pltpu.SemaphoreType.DMA((latitude_rows + 1,))],
        specs=[FAR, WHOLE, FAR],
    )
    gathered = lax.all_to_all(spectra, "space", split_axis=0, concat_axis=0, tiled=True)

    slots = sea_ensemble_arrays[0]
    near = [
        passed_along(slots[offset * CAP : (offset + 1) * CAP], "space", -offset)
        for offset in range(1, LATE)
    ]
    forward, backward = (jnp.asarray(t) for t in legendre_tables(latitudes))
    first = lax.axis_index("space") * per_device
    forward = lax.dynamic_slice_in_dim(forward, first, per_device, 0)
    backward = lax.dynamic_slice_in_dim(backward, first, per_device, 0)
    skip, air_flux, wide = call(
        local_kernel,
        [
            shape(air.shape, F32),
            shape((FC * latitude_rows, longitudes), F32),
            shape((channels, channels + 128), BF16),
        ],
        [air, layernorm_scaling, bypass_factor, core_exit_factor, air_to_exchange_factor.T],
        2 * latitude_rows * longitudes * channels * channels,
        held([air]) + [pltpu.SemaphoreType.DMA((latitude_rows,))],
        specs=[FAR] + [WHOLE] * 4,
    )
    offsets = patch_holder_shift[:, 0]
    earlier = jnp.tril(jnp.ones((HOME_DEV, HOME_DEV), jnp.int32), -1)
    positions = jnp.sum((offsets[:, None] == offsets[None, :]).astype(jnp.int32) * earlier, axis=1)
    targets = offsets * CAP + positions
    selected = targets[None, :] == jnp.arange(SLOTS, dtype=jnp.int32)[:, None]
    depths = jnp.sum(jnp.where(selected, wet_depth_layers[None, :], 0), axis=1)
    kernel = jnp.transpose(input_to_hidden_kernel, (1, 0, 2))
    state_weight = jnp.pad(kernel[:, :, :OCH], ((0, 0), (0, 0), (0, OCH_PAD - OCH))).reshape(
        hidden_channels, -1
    )
    forcing_weight = kernel[:, :, OCH:].reshape(hidden_channels, -1)
    decode_weight = jnp.pad(hidden_to_change_kernel, ((0, 16 - len(TAPS)), (0, 0)))
    picks = jnp.sum(jnp.where(selected[:, :, None], patch_exchange_pick[None], 0), axis=1)
    picks = picks.reshape(1, SPAN)
    line, column = picks // longitudes, picks % longitudes
    group = column // 128 * latitude_rows + line
    place = (column % 128 == jnp.arange(128, dtype=jnp.int32)[:, None]).astype(BF16)
    tile = node_sea_pick // CELLS
    holder = jnp.sum(
        jnp.where(
            tile[:, :, None] == jnp.arange(HOME_DEV, dtype=jnp.int32), targets[None, None, :], 0
        ),
        axis=2,
    )
    holder = jnp.where(sea_indicator > 0, holder, -1)
    cell = (
        (node_sea_pick % CELLS)[:, :, None] == jnp.arange(CELLS, dtype=jnp.int32)
    ).astype(BF16)
    slot_of = (
        holder[:, :, None] == jnp.arange(3 * SLOTS, dtype=jnp.int32) % SLOTS
    ).astype(BF16)
    slot_rows = (
        holder[:, None, :] == jnp.arange(SLOTS, dtype=jnp.int32)[None, :, None]
    ).astype(F32)
    prepared = (
        near, skip, air_flux, wide, place, group, forcing_weight, state_weight, decode_weight,
        depths, cell, slot_of,
    )
    gathered, prepared = lax.optimization_barrier((gathered, prepared))
    (
        near, skip, air_flux, wide, place, group, forcing_weight, state_weight, decode_weight,
        depths, cell, slot_of,
    ) = prepared
    filtered = call(
        legendre_kernel,
        [shape((bands, chunk, channels), BF16)],
        [gathered, forward, backward, harmonic_damping_factor],
        2 * 2 * 2 * per_device * LMAX * latitudes * channels,
        [pltpu.VMEM((channels // 128, bands * chunk, 128), F32)],
        limit=32,
    )
    filtered, late = lax.optimization_barrier((filtered, slots[LATE * CAP :]))
    returned = lax.all_to_all(filtered, "space", split_axis=0, concat_axis=0, tiled=True)
    rest = [
        passed_along(late[at : at + CAP], "space", -(LATE + at // CAP))
        for at in range(0, late.shape[0], CAP)
    ]
    wet, top = call(
        ocean_kernel,
        [shape((hidden_channels, SPAN), F32), shape((1, SPAN), F32)],
        [depths, slots[:CAP], *near, *rest, state_weight],
        2 * hidden_channels * len(TAPS) * OCH_PAD * SPAN,
        [pltpu.VMEM((len(TAPS) * OCH_PAD, SPAN), BF16)],
        specs=[pl.BlockSpec(memory_space=pltpu.SMEM)] + [WHOLE] * (NEAR + 1),
    )
    operands = [
        returned, synthesis, skip, air, wide, air_flux, place, group, forcing_weight, wet,
        decode_weight, top,
    ]
    updated, tiles = call(
        surface_kernel,
        [shape(air.shape, F32), shape((members, SLOTS, CELLS), BF16)],
        operands,
        2 * latitude_rows * longitudes * channels * (channels + 2 * MMAX),
        held(operands)
        + [
            pltpu.VMEM(air.shape, F32),
            pltpu.VMEM((3 * FC * latitude_rows, 128), F32),
            pltpu.VMEM((SLOTS, CELLS), F32),
            pltpu.SemaphoreType.DMA((len(operands),)),
            pltpu.SemaphoreType.DMA((latitude_rows,)),
        ],
        specs=[FAR] * len(operands),
        out_specs=[FAR, WHOLE],
    )
    everyone = lax.all_to_all(tiles, "member", split_axis=0, concat_axis=0, tiled=True)
    out = call(
        imprint_kernel,
        [shape(air.shape, BF16)],
        [updated, tiles, cell, slot_of, sea_heat_imprint],
        2 * latitude_rows * longitudes * channels * 256,
        held([updated, cell, slot_of, air])
        + [
            pltpu.SemaphoreType.DMA((latitude_rows + 2,)),
            pltpu.SemaphoreType.DMA((latitude_rows,)),
        ],
        specs=[FAR, WHOLE, FAR, FAR, WHOLE],
        out_specs=FAR,
    )
    mean = call(
        mean_kernel,
        [shape((latitude_rows, longitudes), F32)],
        [everyone, cell, slot_rows],
        2 * 3 * SLOTS * CELLS * latitude_rows * longitudes,
        limit=32,
    )
    return (out[None], mean)


def solution(mesh):
    in_specs = (
        P("member", "space", None, None),
        P("space", None),
        P(),
        P(),
        P(),
        P(),
        P(),
        P(),
        P("member", "space", None, None),
        P(),
        P(),
        P("space", None),
        P("space", None),
        P("space", None),
        P("space"),
    )
    out_specs = (P("member", "space", None, None), P("space", None))
    return jax.shard_map(shards, mesh=mesh, in_specs=in_specs, out_specs=out_specs, check_vma=False)
```

```python
import math

import jax
import jax.numpy as jnp
import numpy as np
from jax import lax
from jax.experimental import pallas as pl
from jax.experimental.pallas import tpu as pltpu
from jax.sharding import PartitionSpec as P

MERIDIAN_TOTAL = 360
MMAX = 128
LMAX = 128
FC = 8
LEV = 19
CAP = 2
NEAR = 8
HOME_DEV = 14
SLOTS = NEAR * CAP
CELLS = 128
SPAN = SLOTS * CELLS
OCH = 76
OCH_PAD = 80
TAPS = [(row, col) for row in (-1, 0, 1) for col in (-1, 0, 1)]
EARLY = 3
BF16 = jnp.bfloat16
F32 = jnp.float32
WHOLE = pl.BlockSpec(memory_space=pltpu.VMEM)
FAR = pl.BlockSpec(memory_space=pltpu.HBM)


def passed_along(value, axis, by):
    devices = lax.axis_size(axis)
    return lax.ppermute(value, axis, [(i, (i + by) % devices) for i in range(devices)])


def fourier_tables():
    product = np.arange(MMAX)[:, None] * np.arange(MERIDIAN_TOTAL)[None, :] % MERIDIAN_TOTAL
    angles = 2.0 * np.pi / MERIDIAN_TOTAL * product
    analysis = np.stack([np.cos(angles), -np.sin(angles)], axis=1) / MERIDIAN_TOTAL
    weights = np.where(np.arange(MMAX) == 0, 1.0, 2.0)[:, None]
    synthesis = np.stack([weights * np.cos(angles), -weights * np.sin(angles)], axis=1)
    return (
        analysis.reshape(2 * MMAX, MERIDIAN_TOTAL).astype(BF16),
        synthesis.reshape(2 * MMAX, MERIDIAN_TOTAL).T.astype(BF16),
    )


def legendre_tables(latitudes):
    theta = np.pi / latitudes * (np.arange(latitudes) + 0.5)
    cosine = np.cos(theta)[None, :]
    sine = np.sin(theta)
    counter = np.arange(1, MMAX)
    totals = np.concatenate([[0.0], np.cumsum(np.log((2.0 * counter - 1.0) / (2.0 * counter)))])
    order = np.arange(MMAX, dtype=np.float64)[:, None]
    diagonal = np.exp(
        0.5 * (np.log((2.0 * order + 1.0) / (4.0 * np.pi)) + totals[:, None])
        + order * np.log(sine)[None, :]
    )
    values = np.zeros((MMAX, LMAX, latitudes))
    latest = np.zeros((MMAX, latitudes))
    before = np.zeros((MMAX, latitudes))
    for degree in range(LMAX):
        lowered = (degree - 1.0) ** 2
        upward = np.sqrt(
            max(4.0 * degree * degree - 1.0, 0.0) / np.maximum(degree * degree - order * order, 1.0)
        )
        damping = np.sqrt(
            np.maximum(lowered - order * order, 0.0) / max(4.0 * lowered - 1.0, 1.0)
        )
        current = upward * (cosine * latest - damping * before)
        current = np.where(degree == order, diagonal, current)
        current = np.where(degree < order, 0.0, current)
        values[:, degree, :] = current
        latest, before = current, latest
    quadrature = 2.0 * np.pi * np.pi / latitudes * sine
    forward = (values * quadrature[None, None, :]).astype(BF16)
    backward = np.transpose(values, (0, 2, 1)).astype(BF16)
    return forward, backward


def gelu(x):
    inner = math.sqrt(2.0 / math.pi) * (x + 0.044715 * (x * x * x))
    return 0.5 * x * (1.0 + jnp.tanh(inner))


def tap_masks(width):
    lane = lax.broadcasted_iota(jnp.int32, (1, width), 1) % CELLS
    row, col = lane // 16, lane % 16
    masks = []
    for down, right in TAPS:
        inside = (row + down >= 0) & (row + down < 8) & (col + right >= 0) & (col + right < 16)
        masks.append(inside)
    return masks


def shifted(x, tap, mask):
    by = 16 * tap[0] + tap[1]
    if by == 0:
        return x
    rolled = pltpu.roll(x, (-by) % x.shape[1], 1)
    return jnp.where(mask, rolled, 0.0)


def in_three(x):
    high = x.astype(BF16)
    rest = x - high.astype(F32)
    middle = rest.astype(BF16)
    return high, middle, (rest - middle.astype(F32)).astype(BF16)


def begin(copies, sems):
    started = [
        pltpu.make_async_copy(source, target, sems.at[i])
        for i, (source, target) in enumerate(copies)
    ]
    for one in started:
        one.start()
    return started


def normalised(x, scale):
    centered = x - jnp.mean(x, axis=-1, keepdims=True)
    spread = jnp.mean(centered * centered, axis=-1, keepdims=True)
    return (centered * lax.rsqrt(spread + 1e-05) * scale).astype(BF16)


def analysis_kernel(
    air_any, scale_ref, table_any, spectra_any, air_ref, table_ref, spectra_ref, sems, out_sems
):
    rows = air_ref.shape[0]
    leaving = []
    groups = spectra_ref.shape[0]
    copies = begin(
        [(air_any.at[j], air_ref.at[j]) for j in range(rows)] + [(table_any, table_ref)], sems
    )
    scale = scale_ref[...].reshape(1, scale_ref.shape[0])
    for pair in range(rows // 2):
        both = []
        for j in (2 * pair, 2 * pair + 1):
            copies[j].wait()
            normed = normalised(air_ref[j].astype(F32), scale)
            if j == 0:
                copies[rows].wait()
            out = jnp.dot(table_ref[...], normed, preferred_element_type=F32)
            both.append(out.reshape(groups, 8, out.shape[1]))
        block = jnp.concatenate(both, axis=1)
        rows_16 = slice(16 * pair, 16 * (pair + 1))
        spectra_ref[:, rows_16, :] = block.astype(BF16)
        leave = pltpu.make_async_copy(
            spectra_ref.at[:, rows_16], spectra_any.at[:, rows_16], out_sems.at[pair]
        )
        leave.start()
        leaving.append(leave)
    for one in leaving:
        one.wait()


def local_kernel(
    air_any, scale_ref, bypass_ref, exit_ref, exchange_ref, skip_ref, flux_ref, wide_ref,
    air_ref, sems,
):
    rows = air_ref.shape[0]
    copies = begin([(air_any.at[j], air_ref.at[j]) for j in range(rows)], sems)
    scale = scale_ref[...].reshape(1, scale_ref.shape[0])
    channels = exit_ref.shape[0]
    dims = (((1,), (1,)), ((), ()))
    through = lax.dot_general(
        exit_ref[...], exchange_ref[...], dims, preferred_element_type=F32
    )
    high = through.astype(BF16)
    low = (through - high.astype(F32)).astype(BF16)
    wide_ref[:, :channels] = exit_ref[...]
    wide_ref[:, channels:] = jnp.concatenate(
        [high.astype(F32), low.astype(F32), jnp.zeros((channels, 128 - 2 * FC), F32)], axis=1
    ).astype(BF16)
    for j in range(rows):
        copies[j].wait()
        own = air_ref[j]
        normed = normalised(own.astype(F32), scale)
        skip_ref[j] = jnp.dot(normed, bypass_ref[...], preferred_element_type=F32)
        flux_ref[FC * j : FC * (j + 1), :] = lax.dot_general(
            exchange_ref[...], own, dims, preferred_element_type=F32
        )


def legendre_kernel(x_ref, forward_ref, backward_ref, gains_ref, out_ref, work):
    groups, chunk, channels = x_ref.shape
    total = groups * chunk
    latitudes = total // 8
    for third in range(channels // 128):
        lanes = slice(128 * third, 128 * (third + 1))
        work[third] = x_ref[:, :, lanes].astype(F32).reshape(total, 128)
        gains = gains_ref[:, lanes]
        gains = jnp.concatenate([gains, gains], axis=1)
        for m in range(4):
            real, imaginary = (pl.ds(2 * m + r, latitudes, stride=8) for r in (0, 1))
            own = jnp.concatenate(
                [work[third, real, :], work[third, imaginary, :]], axis=1
            ).astype(BF16)
            coefficients = jnp.dot(forward_ref[m], own, preferred_element_type=F32)
            shaped = (coefficients * gains).astype(BF16)
            back = jnp.dot(backward_ref[m], shaped, preferred_element_type=F32)
            work[third, real, :] = back[:, :128]
            work[third, imaginary, :] = back[:, 128:]
        out_ref[:, :, lanes] = work[third].reshape(groups, chunk, 128).astype(BF16)


def ocean_kernel(depth_ref, *refs):
    pieces, (weight_ref, out_ref, top_ref, columns) = refs[:NEAR], refs[NEAR:]
    masks = tap_masks(CELLS)
    level = lax.broadcasted_iota(jnp.int32, (OCH, CELLS), 0) % LEV
    for slot in range(SLOTS):
        lanes = slice(CELLS * slot, CELLS * (slot + 1))
        state = pieces[slot // CAP][slot % CAP].astype(F32)
        top_ref[:, lanes] = state[0:1]
        state = jnp.where(level < depth_ref[slot], state, 0.0)
        state = jnp.concatenate([state, jnp.zeros((OCH_PAD - OCH, CELLS), F32)], axis=0)
        for q, tap in enumerate(TAPS):
            moved = shifted(state, tap, masks[q]).astype(BF16)
            columns[OCH_PAD * q : OCH_PAD * (q + 1), lanes] = moved
    for at in range(0, SPAN, 512):
        out_ref[:, at : at + 512] = jnp.dot(
            weight_ref[...], columns[:, at : at + 512], preferred_element_type=F32
        )


def surface_kernel(*refs):
    count = 12
    sources, (updated_any, tiles_ref), held, (updated_ref, flux, sst, sems, out_sems) = (
        refs[:count], refs[count : count + 2], refs[count + 2 : 2 * count + 2],
        refs[2 * count + 2 :],
    )
    leaving = []
    (
        rows_ref, synthesis_ref, wide_ref, air_flux_ref, skip_ref, air_ref, place_ref, group_ref,
        forcing_weight_ref, wet_ref, decode_ref, top_ref,
    ) = held
    moves = list(zip(sources, held))
    ordered = moves[:4]
    for j in range(air_ref.shape[0]):
        ordered += [(source.at[j], target.at[j]) for source, target in moves[4:6]]
    copies = begin(ordered + moves[6:], sems)
    after = len(ordered)
    latitude_rows, longitudes, channels = air_ref.shape
    groups = rows_ref.shape[0]
    pairs = []
    copies[0].wait()
    for pair in range(latitude_rows // 2):
        both = rows_ref[:, 16 * pair : 16 * (pair + 1), :].astype(F32)
        pairs.extend([both[:, :8], both[:, 8:]])
    copies[1].wait()
    for j in range(latitude_rows):
        own = pairs[j].reshape(8 * groups, channels).astype(BF16)
        spectral = jnp.dot(synthesis_ref[...], own, preferred_element_type=F32)
        for one in copies[2:6] if j == 0 else copies[4 + 2 * j : 6 + 2 * j]:
            one.wait()
        mixed = gelu(spectral + skip_ref[j]).astype(BF16)
        wide = jnp.dot(mixed, wide_ref[...], preferred_element_type=F32)
        updated_ref[j] = air_ref[j].astype(F32) + wide[:, :channels]
        leave = pltpu.make_async_copy(updated_ref.at[j], updated_any.at[j], out_sems.at[j])
        leave.start()
        leaving.append(leave)
        narrow = jnp.concatenate(
            [wide[:, channels:], jnp.zeros((384 - longitudes, 128), F32)], axis=0
        )
        turned = jnp.transpose(narrow)
        extra = jnp.concatenate(
            [air_flux_ref[FC * j : FC * (j + 1), :], jnp.zeros((FC, 384 - longitudes), F32)], axis=1
        )
        total = turned[:FC] + turned[FC : 2 * FC] + extra
        for part in range(3):
            at = FC * (part * latitude_rows + j)
            flux[at : at + FC, :] = total[:, 128 * part : 128 * (part + 1)]
    for one in copies[after:]:
        one.wait()
    spread = jnp.dot(flux[...].astype(BF16), place_ref[...], preferred_element_type=F32)
    group = group_ref[...]
    forcing = jnp.zeros((FC, SPAN), F32)
    for at in range(3 * latitude_rows):
        forcing = forcing + jnp.where(group == at, spread[FC * at : FC * (at + 1), :], 0.0)
    masks = tap_masks(SPAN)
    columns = jnp.concatenate(
        [shifted(forcing, tap, masks[q]) for q, tap in enumerate(TAPS)], axis=0
    ).astype(BF16)
    hidden = gelu(
        wet_ref[...] + jnp.dot(forcing_weight_ref[...], columns, preferred_element_type=F32)
    ).astype(BF16)
    partial = jnp.dot(decode_ref[...], hidden, preferred_element_type=F32)
    change = jnp.zeros((1, SPAN), F32)
    for q, tap in enumerate(TAPS):
        change = change + shifted(partial[q : q + 1, :], tap, masks[q])
    surface = top_ref[...] + change
    for slot in range(SLOTS):
        sst[slot : slot + 1, :] = surface[:, CELLS * slot : CELLS * (slot + 1)]
    tiles = sst[...].astype(BF16)
    for member in range(tiles_ref.shape[0]):
        tiles_ref[member] = tiles
    for one in leaving:
        one.wait()


def imprint_kernel(
    updated_any, tiles_ref, cell_any, slot_any, imprint_ref, out_any,
    updated_ref, cell_ref, slot_ref, out_ref, sems, out_sems,
):
    rows, _, channels = updated_ref.shape
    copies = begin(
        [(cell_any, cell_ref), (slot_any, slot_ref)]
        + [(updated_any.at[j], updated_ref.at[j]) for j in range(rows)],
        sems,
    )
    tiles = tiles_ref[0]
    tripled = jnp.concatenate([tiles, tiles, tiles], axis=0)
    pieces = in_three(imprint_ref[...].reshape(1, channels))
    imprint = jnp.concatenate(
        [jnp.broadcast_to(piece, (SLOTS, channels)) for piece in pieces], axis=0
    )
    copies[0].wait()
    copies[1].wait()
    leaving = []
    for j in range(rows):
        picked = lax.dot_general(
            cell_ref[j], tripled, (((1,), (1,)), ((), ())), preferred_element_type=F32
        )
        chosen = picked.astype(BF16) * slot_ref[j]
        warmth = jnp.dot(chosen, imprint, preferred_element_type=F32)
        copies[2 + j].wait()
        out_ref[j] = (updated_ref[j] + warmth).astype(BF16)
        leave = pltpu.make_async_copy(out_ref.at[j], out_any.at[j], out_sems.at[j])
        leave.start()
        leaving.append(leave)
    for one in leaving:
        one.wait()


def mean_kernel(tiles_ref, cell_ref, slot_ref, out_ref):
    members = tiles_ref.shape[0]
    total = jnp.zeros(tiles_ref.shape[1:], F32)
    for member in range(members):
        total = total + tiles_ref[member].astype(F32)
    pieces = jnp.concatenate(in_three(total), axis=0)
    for j in range(cell_ref.shape[0]):
        picked = lax.dot_general(
            pieces, cell_ref[j], (((1,), (1,)), ((), ())), preferred_element_type=F32
        )
        joined = picked[:SLOTS] + picked[SLOTS : 2 * SLOTS] + picked[2 * SLOTS :]
        kept = jnp.where(slot_ref[j] > 0, joined, 0.0)
        out_ref[j : j + 1, :] = jnp.sum(kept, axis=0, keepdims=True) / members


def call(kernel, outs, operands, flops, scratch=(), limit=56, specs=None, out_specs=None):
    size = sum(math.prod(o.shape) * o.dtype.itemsize for o in list(outs) + list(operands))
    return pl.pallas_call(
        kernel,
        out_shape=outs if len(outs) > 1 else outs[0],
        in_specs=specs or [WHOLE] * len(operands),
        out_specs=out_specs or ([WHOLE] * len(outs) if len(outs) > 1 else WHOLE),
        scratch_shapes=list(scratch),
        compiler_params=pltpu.CompilerParams(vmem_limit_bytes=limit * 1024 * 1024),
        cost_estimate=pl.CostEstimate(flops=flops, bytes_accessed=size, transcendentals=0),
    )(*operands)


def held(operands):
    return [pltpu.VMEM(o.shape, o.dtype) for o in operands]


def shards(
    air_ensemble,
    sea_indicator,
    layernorm_scaling,
    harmonic_damping_factor,
    bypass_factor,
    core_exit_factor,
    air_to_exchange_factor,
    sea_heat_imprint,
    sea_ensemble_arrays,
    input_to_hidden_kernel,
    hidden_to_change_kernel,
    patch_exchange_pick,
    node_sea_pick,
    patch_holder_shift,
    wet_depth_layers,
):
    bands = lax.axis_size("space")
    members = lax.axis_size("member")
    air = air_ensemble[0]
    latitude_rows, longitudes, channels = air.shape
    latitudes = latitude_rows * bands
    hidden_channels = input_to_hidden_kernel.shape[1]
    per_device = MMAX // bands
    chunk = 2 * per_device * latitude_rows
    shape = jax.ShapeDtypeStruct

    analysis, synthesis = (jnp.asarray(t) for t in fourier_tables())
    spectra = call(
        analysis_kernel,
        [shape((bands, chunk, channels), BF16)],
        [air, layernorm_scaling, analysis],
        2 * 2 * MMAX * latitude_rows * longitudes * channels,
        held([air, analysis])
        + [
            pltpu.VMEM((bands, chunk, channels), BF16),
            pltpu.SemaphoreType.DMA((latitude_rows + 1,)),
            pltpu.SemaphoreType.DMA((latitude_rows // 2,)),
        ],
        specs=[FAR, WHOLE, FAR],
        out_specs=FAR,
    )
    spectra, slots = lax.optimization_barrier((spectra, sea_ensemble_arrays[0]))
    gathered = lax.all_to_all(spectra, "space", split_axis=0, concat_axis=0, tiled=True)

    far = [
        passed_along(slots[offset * CAP : (offset + 1) * CAP], "space", -offset)
        for offset in range(EARLY, NEAR)
    ]
    forward, backward = (jnp.asarray(t) for t in legendre_tables(latitudes))
    first = lax.axis_index("space") * per_device
    forward = lax.dynamic_slice_in_dim(forward, first, per_device, 0)
    backward = lax.dynamic_slice_in_dim(backward, first, per_device, 0)
    skip, air_flux, wide = call(
        local_kernel,
        [
            shape(air.shape, F32),
            shape((FC * latitude_rows, longitudes), F32),
            shape((channels, channels + 128), BF16),
        ],
        [air, layernorm_scaling, bypass_factor, core_exit_factor, air_to_exchange_factor.T],
        2 * latitude_rows * longitudes * channels * channels,
        held([air]) + [pltpu.SemaphoreType.DMA((latitude_rows,))],
        specs=[FAR] + [WHOLE] * 4,
    )
    offsets = patch_holder_shift[:, 0]
    earlier = jnp.tril(jnp.ones((HOME_DEV, HOME_DEV), jnp.int32), -1)
    positions = jnp.sum((offsets[:, None] == offsets[None, :]).astype(jnp.int32) * earlier, axis=1)
    targets = offsets * CAP + positions
    selected = targets[None, :] == jnp.arange(SLOTS, dtype=jnp.int32)[:, None]
    depths = jnp.sum(jnp.where(selected, wet_depth_layers[None, :], 0), axis=1)
    kernel = jnp.transpose(input_to_hidden_kernel, (1, 0, 2))
    state_weight = jnp.pad(kernel[:, :, :OCH], ((0, 0), (0, 0), (0, OCH_PAD - OCH))).reshape(
        hidden_channels, -1
    )
    forcing_weight = kernel[:, :, OCH:].reshape(hidden_channels, -1)
    decode_weight = jnp.pad(hidden_to_change_kernel, ((0, 16 - len(TAPS)), (0, 0)))
    picks = jnp.sum(jnp.where(selected[:, :, None], patch_exchange_pick[None], 0), axis=1)
    picks = picks.reshape(1, SPAN)
    line, column = picks // longitudes, picks % longitudes
    group = column // 128 * latitude_rows + line
    place = (column % 128 == jnp.arange(128, dtype=jnp.int32)[:, None]).astype(BF16)
    tile = node_sea_pick // CELLS
    holder = jnp.sum(
        jnp.where(
            tile[:, :, None] == jnp.arange(HOME_DEV, dtype=jnp.int32), targets[None, None, :], 0
        ),
        axis=2,
    )
    holder = jnp.where(sea_indicator > 0, holder, -1)
    cell = (
        (node_sea_pick % CELLS)[:, :, None] == jnp.arange(CELLS, dtype=jnp.int32)
    ).astype(BF16)
    slot_of = (
        holder[:, :, None] == jnp.arange(3 * SLOTS, dtype=jnp.int32) % SLOTS
    ).astype(BF16)
    slot_rows = (
        holder[:, None, :] == jnp.arange(SLOTS, dtype=jnp.int32)[None, :, None]
    ).astype(F32)
    prepared = (
        far, skip, air_flux, wide, place, group, forcing_weight, state_weight, decode_weight,
        depths, cell, slot_of,
    )
    gathered, prepared = lax.optimization_barrier((gathered, prepared))
    (
        far, skip, air_flux, wide, place, group, forcing_weight, state_weight, decode_weight,
        depths, cell, slot_of,
    ) = prepared
    filtered = call(
        legendre_kernel,
        [shape((bands, chunk, channels), BF16)],
        [gathered, forward, backward, harmonic_damping_factor],
        2 * 2 * 2 * per_device * LMAX * latitudes * channels,
        [pltpu.VMEM((channels // 128, bands * chunk, 128), F32)],
        limit=32,
    )
    filtered, late = lax.optimization_barrier((filtered, slots[CAP : EARLY * CAP]))
    returned = lax.all_to_all(filtered, "space", split_axis=0, concat_axis=0, tiled=True)
    near = [
        passed_along(late[at : at + CAP], "space", -(1 + at // CAP))
        for at in range(0, late.shape[0], CAP)
    ]
    wet, top = call(
        ocean_kernel,
        [shape((hidden_channels, SPAN), F32), shape((1, SPAN), F32)],
        [depths, slots[:CAP], *near, *far, state_weight],
        2 * hidden_channels * len(TAPS) * OCH_PAD * SPAN,
        [pltpu.VMEM((len(TAPS) * OCH_PAD, SPAN), BF16)],
        specs=[pl.BlockSpec(memory_space=pltpu.SMEM)] + [WHOLE] * (NEAR + 1),
    )
    operands = [
        returned, synthesis, wide, air_flux, skip, air, place, group, forcing_weight, wet,
        decode_weight, top,
    ]
    updated, tiles = call(
        surface_kernel,
        [shape(air.shape, F32), shape((members, SLOTS, CELLS), BF16)],
        operands,
        2 * latitude_rows * longitudes * channels * (channels + 2 * MMAX),
        held(operands)
        + [
            pltpu.VMEM(air.shape, F32),
            pltpu.VMEM((3 * FC * latitude_rows, 128), F32),
            pltpu.VMEM((SLOTS, CELLS), F32),
            pltpu.SemaphoreType.DMA((len(operands) + 2 * latitude_rows,)),
            pltpu.SemaphoreType.DMA((latitude_rows,)),
        ],
        specs=[FAR] * len(operands),
        out_specs=[FAR, WHOLE],
    )
    everyone = lax.all_to_all(tiles, "member", split_axis=0, concat_axis=0, tiled=True)
    out = call(
        imprint_kernel,
        [shape(air.shape, BF16)],
        [updated, tiles, cell, slot_of, sea_heat_imprint],
        2 * latitude_rows * longitudes * channels * 256,
        held([updated, cell, slot_of, air])
        + [
            pltpu.SemaphoreType.DMA((latitude_rows + 2,)),
            pltpu.SemaphoreType.DMA((latitude_rows,)),
        ],
        specs=[FAR, WHOLE, FAR, FAR, WHOLE],
        out_specs=FAR,
    )
    mean = call(
        mean_kernel,
        [shape((latitude_rows, longitudes), F32)],
        [everyone, cell, slot_rows],
        2 * 3 * SLOTS * CELLS * latitude_rows * longitudes,
        limit=32,
    )
    return (out[None], mean)


def solution(mesh):
    in_specs = (
        P("member", "space", None, None),
        P("space", None),
        P(),
        P(),
        P(),
        P(),
        P(),
        P(),
        P("member", "space", None, None),
        P(),
        P(),
        P("space", None),
        P("space", None),
        P("space", None),
        P("space"),
    )
    out_specs = (P("member", "space", None, None), P("space", None))
    return jax.shard_map(shards, mesh=mesh, in_specs=in_specs, out_specs=out_specs, check_vma=False)
```

```python
import math

import jax
import jax.numpy as jnp
import numpy as np
from jax import lax
from jax.experimental import pallas as pl
from jax.experimental.pallas import tpu as pltpu
from jax.sharding import PartitionSpec as P

MERIDIAN_TOTAL = 360
MMAX = 128
LMAX = 128
FC = 8
LEV = 19
CAP = 2
NEAR = 8
HOME_DEV = 14
SLOTS = NEAR * CAP
CELLS = 128
SPAN = SLOTS * CELLS
OCH = 76
OCH_PAD = 80
TAPS = [(row, col) for row in (-1, 0, 1) for col in (-1, 0, 1)]
EARLY = 3
SMALL = 1024
BF16 = jnp.bfloat16
F32 = jnp.float32
WHOLE = pl.BlockSpec(memory_space=pltpu.VMEM)
FAR = pl.BlockSpec(memory_space=pltpu.HBM)


def passed_along(value, axis, by):
    devices = lax.axis_size(axis)
    return lax.ppermute(value, axis, [(i, (i + by) % devices) for i in range(devices)])


def fourier_tables():
    product = np.arange(MMAX)[:, None] * np.arange(MERIDIAN_TOTAL)[None, :] % MERIDIAN_TOTAL
    angles = 2.0 * np.pi / MERIDIAN_TOTAL * product
    analysis = np.stack([np.cos(angles), -np.sin(angles)], axis=1) / MERIDIAN_TOTAL
    weights = np.where(np.arange(MMAX) == 0, 1.0, 2.0)[:, None]
    synthesis = np.stack([weights * np.cos(angles), -weights * np.sin(angles)], axis=1)
    return (
        analysis.reshape(2 * MMAX, MERIDIAN_TOTAL).astype(BF16),
        synthesis.reshape(2 * MMAX, MERIDIAN_TOTAL).T.astype(BF16),
    )


def legendre_tables(latitudes):
    theta = np.pi / latitudes * (np.arange(latitudes) + 0.5)
    cosine = np.cos(theta)[None, :]
    sine = np.sin(theta)
    counter = np.arange(1, MMAX)
    totals = np.concatenate([[0.0], np.cumsum(np.log((2.0 * counter - 1.0) / (2.0 * counter)))])
    order = np.arange(MMAX, dtype=np.float64)[:, None]
    diagonal = np.exp(
        0.5 * (np.log((2.0 * order + 1.0) / (4.0 * np.pi)) + totals[:, None])
        + order * np.log(sine)[None, :]
    )
    values = np.zeros((MMAX, LMAX, latitudes))
    latest = np.zeros((MMAX, latitudes))
    before = np.zeros((MMAX, latitudes))
    for degree in range(LMAX):
        lowered = (degree - 1.0) ** 2
        upward = np.sqrt(
            max(4.0 * degree * degree - 1.0, 0.0) / np.maximum(degree * degree - order * order, 1.0)
        )
        damping = np.sqrt(
            np.maximum(lowered - order * order, 0.0) / max(4.0 * lowered - 1.0, 1.0)
        )
        current = upward * (cosine * latest - damping * before)
        current = np.where(degree == order, diagonal, current)
        current = np.where(degree < order, 0.0, current)
        values[:, degree, :] = current
        latest, before = current, latest
    quadrature = 2.0 * np.pi * np.pi / latitudes * sine
    forward = (values * quadrature[None, None, :]).astype(BF16)
    backward = np.transpose(values, (0, 2, 1)).astype(BF16)
    return forward, backward


def gelu(x):
    inner = math.sqrt(2.0 / math.pi) * (x + 0.044715 * (x * x * x))
    return 0.5 * x * (1.0 + jnp.tanh(inner))


def tap_masks(width):
    lane = lax.broadcasted_iota(jnp.int32, (1, width), 1) % CELLS
    row, col = lane // 16, lane % 16
    masks = []
    for down, right in TAPS:
        inside = (row + down >= 0) & (row + down < 8) & (col + right >= 0) & (col + right < 16)
        masks.append(inside)
    return masks


def shifted(x, tap, mask):
    by = 16 * tap[0] + tap[1]
    if by == 0:
        return x
    rolled = pltpu.roll(x, (-by) % x.shape[1], 1)
    return jnp.where(mask, rolled, 0.0)


def in_three(x):
    high = x.astype(BF16)
    rest = x - high.astype(F32)
    middle = rest.astype(BF16)
    return high, middle, (rest - middle.astype(F32)).astype(BF16)


def begin(copies, sems):
    started = [
        pltpu.make_async_copy(source, target, sems.at[i])
        for i, (source, target) in enumerate(copies)
    ]
    for one in started:
        one.start()
    return started


def normalised(x, scale):
    centered = x - jnp.mean(x, axis=-1, keepdims=True)
    spread = jnp.mean(centered * centered, axis=-1, keepdims=True)
    return (centered * lax.rsqrt(spread + 1e-05) * scale).astype(BF16)


def analysis_kernel(
    air_any, scale_ref, table_any, spectra_any, air_ref, table_ref, spectra_ref, sems, out_sems
):
    rows = air_ref.shape[0]
    leaving = []
    groups = spectra_ref.shape[0]
    copies = begin(
        [(air_any.at[j], air_ref.at[j]) for j in range(rows)] + [(table_any, table_ref)], sems
    )
    scale = scale_ref[...].reshape(1, scale_ref.shape[0])
    for pair in range(rows // 2):
        both = []
        for j in (2 * pair, 2 * pair + 1):
            copies[j].wait()
            normed = normalised(air_ref[j].astype(F32), scale)
            if j == 0:
                copies[rows].wait()
            out = jnp.dot(table_ref[...], normed, preferred_element_type=F32)
            both.append(out.reshape(groups, 8, out.shape[1]))
        block = jnp.concatenate(both, axis=1)
        rows_16 = slice(16 * pair, 16 * (pair + 1))
        spectra_ref[:, rows_16, :] = block.astype(BF16)
        leave = pltpu.make_async_copy(
            spectra_ref.at[:, rows_16], spectra_any.at[:, rows_16], out_sems.at[pair]
        )
        leave.start()
        leaving.append(leave)
    for one in leaving:
        one.wait()


def local_kernel(
    air_any, scale_ref, bypass_ref, exit_ref, exchange_ref, skip_ref, flux_ref, wide_ref,
    air_ref, sems,
):
    rows = air_ref.shape[0]
    copies = begin([(air_any.at[j], air_ref.at[j]) for j in range(rows)], sems)
    scale = scale_ref[...].reshape(1, scale_ref.shape[0])
    channels = exit_ref.shape[0]
    dims = (((1,), (1,)), ((), ()))
    through = lax.dot_general(
        exit_ref[...], exchange_ref[...], dims, preferred_element_type=F32
    )
    high = through.astype(BF16)
    low = (through - high.astype(F32)).astype(BF16)
    wide_ref[:, :channels] = exit_ref[...]
    wide_ref[:, channels:] = jnp.concatenate(
        [high.astype(F32), low.astype(F32), jnp.zeros((channels, 128 - 2 * FC), F32)], axis=1
    ).astype(BF16)
    for j in range(rows):
        copies[j].wait()
        own = air_ref[j]
        normed = normalised(own.astype(F32), scale)
        skip_ref[j] = jnp.dot(normed, bypass_ref[...], preferred_element_type=F32)
        flux_ref[FC * j : FC * (j + 1), :] = lax.dot_general(
            exchange_ref[...], own, dims, preferred_element_type=F32
        )


def legendre_kernel(x_ref, forward_ref, backward_ref, gains_ref, out_ref, work):
    groups, chunk, channels = x_ref.shape
    total = groups * chunk
    latitudes = total // 8
    for third in range(channels // 128):
        lanes = slice(128 * third, 128 * (third + 1))
        work[third] = x_ref[:, :, lanes].astype(F32).reshape(total, 128)
        gains = gains_ref[:, lanes]
        gains = jnp.concatenate([gains, gains], axis=1)
        for m in range(4):
            real, imaginary = (pl.ds(2 * m + r, latitudes, stride=8) for r in (0, 1))
            own = jnp.concatenate(
                [work[third, real, :], work[third, imaginary, :]], axis=1
            ).astype(BF16)
            coefficients = jnp.dot(forward_ref[m], own, preferred_element_type=F32)
            shaped = (coefficients * gains).astype(BF16)
            back = jnp.dot(backward_ref[m], shaped, preferred_element_type=F32)
            work[third, real, :] = back[:, :128]
            work[third, imaginary, :] = back[:, 128:]
        out_ref[:, :, lanes] = work[third].reshape(groups, chunk, 128).astype(BF16)


def ocean_kernel(depth_ref, *refs):
    pieces, (weight_ref, out_ref, top_ref, columns) = refs[:NEAR], refs[NEAR:]
    masks = tap_masks(CELLS)
    level = lax.broadcasted_iota(jnp.int32, (OCH, CELLS), 0) % LEV
    for slot in range(SLOTS):
        lanes = slice(CELLS * slot, CELLS * (slot + 1))
        state = pieces[slot // CAP][slot % CAP].astype(F32)
        top_ref[:, lanes] = state[0:1]
        state = jnp.where(level < depth_ref[slot], state, 0.0)
        state = jnp.concatenate([state, jnp.zeros((OCH_PAD - OCH, CELLS), F32)], axis=0)
        for q, tap in enumerate(TAPS):
            moved = shifted(state, tap, masks[q]).astype(BF16)
            columns[OCH_PAD * q : OCH_PAD * (q + 1), lanes] = moved
    for at in range(0, SPAN, 512):
        out_ref[:, at : at + 512] = jnp.dot(
            weight_ref[...], columns[:, at : at + 512], preferred_element_type=F32
        )


def surface_kernel(*refs):
    count = 12
    sources, (updated_any, tiles_ref), held, (updated_ref, flux, sst, sems, out_sems) = (
        refs[:count], refs[count : count + 2], refs[count + 2 : 2 * count + 2],
        refs[2 * count + 2 :],
    )
    leaving = []
    (
        rows_ref, synthesis_ref, wide_ref, air_flux_ref, skip_ref, air_ref, place_ref, group_ref,
        forcing_weight_ref, wet_ref, decode_ref, top_ref,
    ) = held
    moves = list(zip(sources, held))
    ordered = moves[:4]
    for j in range(air_ref.shape[0]):
        ordered += [(source.at[j], target.at[j]) for source, target in moves[4:6]]
    copies = begin(ordered + moves[6:], sems)
    after = len(ordered)
    latitude_rows, longitudes, channels = air_ref.shape
    groups = rows_ref.shape[0]
    pairs = []
    copies[0].wait()
    for pair in range(latitude_rows // 2):
        both = rows_ref[:, 16 * pair : 16 * (pair + 1), :].astype(F32)
        pairs.extend([both[:, :8], both[:, 8:]])
    copies[1].wait()
    for j in range(latitude_rows):
        own = pairs[j].reshape(8 * groups, channels).astype(BF16)
        spectral = jnp.dot(synthesis_ref[...], own, preferred_element_type=F32)
        for one in copies[2:6] if j == 0 else copies[4 + 2 * j : 6 + 2 * j]:
            one.wait()
        mixed = gelu(spectral + skip_ref[j]).astype(BF16)
        wide = jnp.dot(mixed, wide_ref[...], preferred_element_type=F32)
        updated_ref[j] = air_ref[j].astype(F32) + wide[:, :channels]
        leave = pltpu.make_async_copy(updated_ref.at[j], updated_any.at[j], out_sems.at[j])
        leave.start()
        leaving.append(leave)
        narrow = jnp.concatenate(
            [wide[:, channels:], jnp.zeros((384 - longitudes, 128), F32)], axis=0
        )
        turned = jnp.transpose(narrow)
        extra = jnp.concatenate(
            [air_flux_ref[FC * j : FC * (j + 1), :], jnp.zeros((FC, 384 - longitudes), F32)], axis=1
        )
        total = turned[:FC] + turned[FC : 2 * FC] + extra
        for part in range(3):
            at = FC * (part * latitude_rows + j)
            flux[at : at + FC, :] = total[:, 128 * part : 128 * (part + 1)]
    for one in copies[after:]:
        one.wait()
    spread = jnp.dot(flux[...].astype(BF16), place_ref[...], preferred_element_type=F32)
    group = group_ref[...]
    forcing = jnp.zeros((FC, SPAN), F32)
    for at in range(3 * latitude_rows):
        forcing = forcing + jnp.where(group == at, spread[FC * at : FC * (at + 1), :], 0.0)
    masks = tap_masks(SPAN)
    columns = jnp.concatenate(
        [shifted(forcing, tap, masks[q]) for q, tap in enumerate(TAPS)], axis=0
    ).astype(BF16)
    hidden = gelu(
        wet_ref[...] + jnp.dot(forcing_weight_ref[...], columns, preferred_element_type=F32)
    ).astype(BF16)
    partial = jnp.dot(decode_ref[...], hidden, preferred_element_type=F32)
    change = jnp.zeros((1, SPAN), F32)
    for q, tap in enumerate(TAPS):
        change = change + shifted(partial[q : q + 1, :], tap, masks[q])
    surface = top_ref[...] + change
    for slot in range(SLOTS):
        sst[slot : slot + 1, :] = surface[:, CELLS * slot : CELLS * (slot + 1)]
    tiles = sst[...].astype(BF16)
    for member in range(tiles_ref.shape[0]):
        tiles_ref[member] = tiles
    for one in leaving:
        one.wait()


def imprint_kernel(
    updated_any, tiles_ref, cell_any, slot_any, imprint_ref, out_any,
    updated_ref, cell_ref, slot_ref, out_ref, sems, out_sems,
):
    rows, _, channels = updated_ref.shape
    copies = begin(
        [(cell_any, cell_ref), (slot_any, slot_ref)]
        + [(updated_any.at[j], updated_ref.at[j]) for j in range(rows)],
        sems,
    )
    tiles = tiles_ref[0]
    tripled = jnp.concatenate([tiles, tiles, tiles], axis=0)
    pieces = in_three(imprint_ref[...].reshape(1, channels))
    imprint = jnp.concatenate(
        [jnp.broadcast_to(piece, (SLOTS, channels)) for piece in pieces], axis=0
    )
    copies[0].wait()
    copies[1].wait()
    leaving = []
    for j in range(rows):
        picked = lax.dot_general(
            cell_ref[j], tripled, (((1,), (1,)), ((), ())), preferred_element_type=F32
        )
        chosen = picked.astype(BF16) * slot_ref[j]
        warmth = jnp.dot(chosen, imprint, preferred_element_type=F32)
        copies[2 + j].wait()
        out_ref[j] = (updated_ref[j] + warmth).astype(BF16)
        leave = pltpu.make_async_copy(out_ref.at[j], out_any.at[j], out_sems.at[j])
        leave.start()
        leaving.append(leave)
    for one in leaving:
        one.wait()


def mean_kernel(tiles_ref, cell_ref, slot_ref, out_ref):
    members = tiles_ref.shape[0]
    total = jnp.zeros(tiles_ref.shape[1:], F32)
    for member in range(members):
        total = total + tiles_ref[member].astype(F32)
    pieces = jnp.concatenate(in_three(total), axis=0)
    for j in range(cell_ref.shape[0]):
        picked = lax.dot_general(
            pieces, cell_ref[j], (((1,), (1,)), ((), ())), preferred_element_type=F32
        )
        joined = picked[:SLOTS] + picked[SLOTS : 2 * SLOTS] + picked[2 * SLOTS :]
        kept = jnp.where(slot_ref[j] > 0, joined, 0.0)
        out_ref[j : j + 1, :] = jnp.sum(kept, axis=0, keepdims=True) / members


def call(kernel, outs, operands, flops, scratch=(), limit=56, specs=None, out_specs=None):
    size = sum(math.prod(o.shape) * o.dtype.itemsize for o in list(outs) + list(operands))
    return pl.pallas_call(
        kernel,
        out_shape=outs if len(outs) > 1 else outs[0],
        in_specs=specs or [WHOLE] * len(operands),
        out_specs=out_specs or ([WHOLE] * len(outs) if len(outs) > 1 else WHOLE),
        scratch_shapes=list(scratch),
        compiler_params=pltpu.CompilerParams(vmem_limit_bytes=limit * 1024 * 1024),
        cost_estimate=pl.CostEstimate(
            flops=flops, bytes_accessed=min(size, flops), transcendentals=0
        ),
    )(*operands)


def held(operands):
    return [pltpu.VMEM(o.shape, o.dtype) for o in operands]


def shards(
    air_ensemble,
    sea_indicator,
    layernorm_scaling,
    harmonic_damping_factor,
    bypass_factor,
    core_exit_factor,
    air_to_exchange_factor,
    sea_heat_imprint,
    sea_ensemble_arrays,
    input_to_hidden_kernel,
    hidden_to_change_kernel,
    patch_exchange_pick,
    node_sea_pick,
    patch_holder_shift,
    wet_depth_layers,
):
    bands = lax.axis_size("space")
    members = lax.axis_size("member")
    air = air_ensemble[0]
    latitude_rows, longitudes, channels = air.shape
    latitudes = latitude_rows * bands
    hidden_channels = input_to_hidden_kernel.shape[1]
    per_device = MMAX // bands
    chunk = 2 * per_device * latitude_rows
    shape = jax.ShapeDtypeStruct

    analysis, synthesis = (jnp.asarray(t) for t in fourier_tables())
    spectra = call(
        analysis_kernel,
        [shape((bands, chunk, channels), BF16)],
        [air, layernorm_scaling, analysis],
        2 * 2 * MMAX * latitude_rows * longitudes * channels,
        held([air, analysis])
        + [
            pltpu.VMEM((bands, chunk, channels), BF16),
            pltpu.SemaphoreType.DMA((latitude_rows + 1,)),
            pltpu.SemaphoreType.DMA((latitude_rows // 2,)),
        ],
        specs=[FAR, WHOLE, FAR],
        out_specs=FAR,
    )
    gathered = lax.all_to_all(spectra, "space", split_axis=0, concat_axis=0, tiled=True)

    slots = sea_ensemble_arrays[0]
    far = [
        passed_along(slots[offset * CAP : (offset + 1) * CAP], "space", -offset)
        for offset in range(EARLY, NEAR)
    ]
    forward, backward = (jnp.asarray(t) for t in legendre_tables(latitudes))
    first = lax.axis_index("space") * per_device
    forward = lax.dynamic_slice_in_dim(forward, first, per_device, 0)
    backward = lax.dynamic_slice_in_dim(backward, first, per_device, 0)
    skip, air_flux, wide = call(
        local_kernel,
        [
            shape(air.shape, F32),
            shape((FC * latitude_rows, longitudes), F32),
            shape((channels, channels + 128), BF16),
        ],
        [air, layernorm_scaling, bypass_factor, core_exit_factor, air_to_exchange_factor.T],
        SMALL,
        held([air]) + [pltpu.SemaphoreType.DMA((latitude_rows,))],
        specs=[FAR] + [WHOLE] * 4,
    )
    offsets = patch_holder_shift[:, 0]
    earlier = jnp.tril(jnp.ones((HOME_DEV, HOME_DEV), jnp.int32), -1)
    positions = jnp.sum((offsets[:, None] == offsets[None, :]).astype(jnp.int32) * earlier, axis=1)
    targets = offsets * CAP + positions
    selected = targets[None, :] == jnp.arange(SLOTS, dtype=jnp.int32)[:, None]
    depths = jnp.sum(jnp.where(selected, wet_depth_layers[None, :], 0), axis=1)
    kernel = jnp.transpose(input_to_hidden_kernel, (1, 0, 2))
    state_weight = jnp.pad(kernel[:, :, :OCH], ((0, 0), (0, 0), (0, OCH_PAD - OCH))).reshape(
        hidden_channels, -1
    )
    forcing_weight = kernel[:, :, OCH:].reshape(hidden_channels, -1)
    decode_weight = jnp.pad(hidden_to_change_kernel, ((0, 16 - len(TAPS)), (0, 0)))
    picks = jnp.sum(jnp.where(selected[:, :, None], patch_exchange_pick[None], 0), axis=1)
    picks = picks.reshape(1, SPAN)
    line, column = picks // longitudes, picks % longitudes
    group = column // 128 * latitude_rows + line
    place = (column % 128 == jnp.arange(128, dtype=jnp.int32)[:, None]).astype(BF16)
    tile = node_sea_pick // CELLS
    holder = jnp.sum(
        jnp.where(
            tile[:, :, None] == jnp.arange(HOME_DEV, dtype=jnp.int32), targets[None, None, :], 0
        ),
        axis=2,
    )
    holder = jnp.where(sea_indicator > 0, holder, -1)
    cell = (
        (node_sea_pick % CELLS)[:, :, None] == jnp.arange(CELLS, dtype=jnp.int32)
    ).astype(BF16)
    slot_of = (
        holder[:, :, None] == jnp.arange(3 * SLOTS, dtype=jnp.int32) % SLOTS
    ).astype(BF16)
    slot_rows = (
        holder[:, None, :] == jnp.arange(SLOTS, dtype=jnp.int32)[None, :, None]
    ).astype(F32)
    gathered, *far = lax.optimization_barrier((gathered, *far))
    filtered = call(
        legendre_kernel,
        [shape((bands, chunk, channels), BF16)],
        [gathered, forward, backward, harmonic_damping_factor],
        2 * 2 * 2 * per_device * LMAX * latitudes * channels,
        [pltpu.VMEM((channels // 128, bands * chunk, 128), F32)],
        limit=32,
    )
    filtered, late = lax.optimization_barrier((filtered, slots[CAP : EARLY * CAP]))
    returned = lax.all_to_all(filtered, "space", split_axis=0, concat_axis=0, tiled=True)
    near = [
        passed_along(late[at : at + CAP], "space", -(1 + at // CAP))
        for at in range(0, late.shape[0], CAP)
    ]
    wet, top = call(
        ocean_kernel,
        [shape((hidden_channels, SPAN), F32), shape((1, SPAN), F32)],
        [depths, slots[:CAP], *near, *far, state_weight],
        SMALL,
        [pltpu.VMEM((len(TAPS) * OCH_PAD, SPAN), BF16)],
        limit=32,
        specs=[pl.BlockSpec(memory_space=pltpu.SMEM)] + [WHOLE] * (NEAR + 1),
    )
    operands = [
        returned, synthesis, wide, air_flux, skip, air, place, group, forcing_weight, wet,
        decode_weight, top,
    ]
    updated, tiles = call(
        surface_kernel,
        [shape(air.shape, F32), shape((members, SLOTS, CELLS), BF16)],
        operands,
        2 * latitude_rows * longitudes * channels * (channels + 2 * MMAX),
        held(operands)
        + [
            pltpu.VMEM(air.shape, F32),
            pltpu.VMEM((3 * FC * latitude_rows, 128), F32),
            pltpu.VMEM((SLOTS, CELLS), F32),
            pltpu.SemaphoreType.DMA((len(operands) + 2 * latitude_rows,)),
            pltpu.SemaphoreType.DMA((latitude_rows,)),
        ],
        specs=[FAR] * len(operands),
        out_specs=[FAR, WHOLE],
    )
    everyone = lax.all_to_all(tiles, "member", split_axis=0, concat_axis=0, tiled=True)
    out = call(
        imprint_kernel,
        [shape(air.shape, BF16)],
        [updated, tiles, cell, slot_of, sea_heat_imprint],
        2 * latitude_rows * longitudes * channels * 256,
        held([updated, cell, slot_of, air])
        + [
            pltpu.SemaphoreType.DMA((latitude_rows + 2,)),
            pltpu.SemaphoreType.DMA((latitude_rows,)),
        ],
        specs=[FAR, WHOLE, FAR, FAR, WHOLE],
        out_specs=FAR,
    )
    mean = call(
        mean_kernel,
        [shape((latitude_rows, longitudes), F32)],
        [everyone, cell, slot_rows],
        2 * 3 * SLOTS * CELLS * latitude_rows * longitudes,
        limit=32,
    )
    return (out[None], mean)


def solution(mesh):
    in_specs = (
        P("member", "space", None, None),
        P("space", None),
        P(),
        P(),
        P(),
        P(),
        P(),
        P(),
        P("member", "space", None, None),
        P(),
        P(),
        P("space", None),
        P("space", None),
        P("space", None),
        P("space"),
    )
    out_specs = (P("member", "space", None, None), P("space", None))
    return jax.shard_map(shards, mesh=mesh, in_specs=in_specs, out_specs=out_specs, check_vma=False)
```

```python
import math

import jax
import jax.numpy as jnp
import numpy as np
from jax import lax
from jax.experimental import pallas as pl
from jax.experimental.pallas import tpu as pltpu
from jax.sharding import PartitionSpec as P

MERIDIAN_TOTAL = 360
MMAX = 128
LMAX = 128
FC = 8
LEV = 19
CAP = 2
NEAR = 8
HOME_DEV = 14
SLOTS = NEAR * CAP
CELLS = 128
SPAN = SLOTS * CELLS
OCH = 76
OCH_PAD = 80
TAPS = [(row, col) for row in (-1, 0, 1) for col in (-1, 0, 1)]
EARLY = 3
SMALL = 1024
BF16 = jnp.bfloat16
F32 = jnp.float32
WHOLE = pl.BlockSpec(memory_space=pltpu.VMEM)
FAR = pl.BlockSpec(memory_space=pltpu.HBM)


def passed_along(value, axis, by):
    devices = lax.axis_size(axis)
    return lax.ppermute(value, axis, [(i, (i + by) % devices) for i in range(devices)])


def fourier_tables():
    product = np.arange(MMAX)[:, None] * np.arange(MERIDIAN_TOTAL)[None, :] % MERIDIAN_TOTAL
    angles = 2.0 * np.pi / MERIDIAN_TOTAL * product
    analysis = np.stack([np.cos(angles), -np.sin(angles)], axis=1) / MERIDIAN_TOTAL
    weights = np.where(np.arange(MMAX) == 0, 1.0, 2.0)[:, None]
    synthesis = np.stack([weights * np.cos(angles), -weights * np.sin(angles)], axis=1)
    return (
        analysis.reshape(2 * MMAX, MERIDIAN_TOTAL).astype(BF16),
        synthesis.reshape(2 * MMAX, MERIDIAN_TOTAL).T.astype(BF16),
    )


def legendre_tables(latitudes):
    theta = np.pi / latitudes * (np.arange(latitudes) + 0.5)
    cosine = np.cos(theta)[None, :]
    sine = np.sin(theta)
    counter = np.arange(1, MMAX)
    totals = np.concatenate([[0.0], np.cumsum(np.log((2.0 * counter - 1.0) / (2.0 * counter)))])
    order = np.arange(MMAX, dtype=np.float64)[:, None]
    diagonal = np.exp(
        0.5 * (np.log((2.0 * order + 1.0) / (4.0 * np.pi)) + totals[:, None])
        + order * np.log(sine)[None, :]
    )
    values = np.zeros((MMAX, LMAX, latitudes))
    latest = np.zeros((MMAX, latitudes))
    before = np.zeros((MMAX, latitudes))
    for degree in range(LMAX):
        lowered = (degree - 1.0) ** 2
        upward = np.sqrt(
            max(4.0 * degree * degree - 1.0, 0.0) / np.maximum(degree * degree - order * order, 1.0)
        )
        damping = np.sqrt(
            np.maximum(lowered - order * order, 0.0) / max(4.0 * lowered - 1.0, 1.0)
        )
        current = upward * (cosine * latest - damping * before)
        current = np.where(degree == order, diagonal, current)
        current = np.where(degree < order, 0.0, current)
        values[:, degree, :] = current
        latest, before = current, latest
    quadrature = 2.0 * np.pi * np.pi / latitudes * sine
    forward = (values * quadrature[None, None, :]).astype(BF16)
    backward = np.transpose(values, (0, 2, 1)).astype(BF16)
    return forward, backward


def gelu(x):
    inner = math.sqrt(2.0 / math.pi) * (x + 0.044715 * (x * x * x))
    return 0.5 * x * (1.0 + jnp.tanh(inner))


def tap_masks(width):
    lane = lax.broadcasted_iota(jnp.int32, (1, width), 1) % CELLS
    row, col = lane // 16, lane % 16
    masks = []
    for down, right in TAPS:
        inside = (row + down >= 0) & (row + down < 8) & (col + right >= 0) & (col + right < 16)
        masks.append(inside)
    return masks


def shifted(x, tap, mask):
    by = 16 * tap[0] + tap[1]
    if by == 0:
        return x
    rolled = pltpu.roll(x, (-by) % x.shape[1], 1)
    return jnp.where(mask, rolled, 0.0)


def in_three(x):
    high = x.astype(BF16)
    rest = x - high.astype(F32)
    middle = rest.astype(BF16)
    return high, middle, (rest - middle.astype(F32)).astype(BF16)


def begin(copies, sems):
    started = [
        pltpu.make_async_copy(source, target, sems.at[i])
        for i, (source, target) in enumerate(copies)
    ]
    for one in started:
        one.start()
    return started


def normalised(x, scale):
    centered = x - jnp.mean(x, axis=-1, keepdims=True)
    spread = jnp.mean(centered * centered, axis=-1, keepdims=True)
    return (centered * lax.rsqrt(spread + 1e-05) * scale).astype(BF16)


def analysis_kernel(
    air_any, scale_ref, table_any, spectra_any, air_ref, table_ref, spectra_ref, sems, out_sems
):
    rows = air_ref.shape[0]
    leaving = []
    groups = spectra_ref.shape[0]
    copies = begin(
        [(air_any.at[j], air_ref.at[j]) for j in range(rows)] + [(table_any, table_ref)], sems
    )
    scale = scale_ref[...].reshape(1, scale_ref.shape[0])
    for pair in range(rows // 2):
        both = []
        for j in (2 * pair, 2 * pair + 1):
            copies[j].wait()
            normed = normalised(air_ref[j].astype(F32), scale)
            if j == 0:
                copies[rows].wait()
            out = jnp.dot(table_ref[...], normed, preferred_element_type=F32)
            both.append(out.reshape(groups, 8, out.shape[1]))
        block = jnp.concatenate(both, axis=1)
        rows_16 = slice(16 * pair, 16 * (pair + 1))
        spectra_ref[:, rows_16, :] = block.astype(BF16)
        leave = pltpu.make_async_copy(
            spectra_ref.at[:, rows_16], spectra_any.at[:, rows_16], out_sems.at[pair]
        )
        leave.start()
        leaving.append(leave)
    for one in leaving:
        one.wait()


def local_kernel(
    air_any, scale_ref, bypass_ref, exit_ref, exchange_ref, skip_ref, flux_ref, wide_ref,
    air_ref, sems,
):
    rows = air_ref.shape[0]
    copies = begin([(air_any.at[j], air_ref.at[j]) for j in range(rows)], sems)
    scale = scale_ref[...].reshape(1, scale_ref.shape[0])
    channels = exit_ref.shape[0]
    dims = (((1,), (1,)), ((), ()))
    through = lax.dot_general(
        exit_ref[...], exchange_ref[...], dims, preferred_element_type=F32
    )
    high = through.astype(BF16)
    low = (through - high.astype(F32)).astype(BF16)
    wide_ref[:, :channels] = exit_ref[...]
    wide_ref[:, channels:] = jnp.concatenate(
        [high.astype(F32), low.astype(F32), jnp.zeros((channels, 128 - 2 * FC), F32)], axis=1
    ).astype(BF16)
    for j in range(rows):
        copies[j].wait()
        own = air_ref[j]
        normed = normalised(own.astype(F32), scale)
        skip_ref[j] = jnp.dot(normed, bypass_ref[...], preferred_element_type=F32)
        flux_ref[FC * j : FC * (j + 1), :] = lax.dot_general(
            exchange_ref[...], own, dims, preferred_element_type=F32
        )


def legendre_kernel(x_ref, forward_ref, backward_ref, gains_ref, out_ref, work):
    groups, chunk, channels = x_ref.shape
    total = groups * chunk
    latitudes = total // 8
    for third in range(channels // 128):
        lanes = slice(128 * third, 128 * (third + 1))
        work[third] = x_ref[:, :, lanes].astype(F32).reshape(total, 128)
        gains = gains_ref[:, lanes]
        gains = jnp.concatenate([gains, gains], axis=1)
        for m in range(4):
            real, imaginary = (pl.ds(2 * m + r, latitudes, stride=8) for r in (0, 1))
            own = jnp.concatenate(
                [work[third, real, :], work[third, imaginary, :]], axis=1
            ).astype(BF16)
            coefficients = jnp.dot(forward_ref[m], own, preferred_element_type=F32)
            shaped = (coefficients * gains).astype(BF16)
            back = jnp.dot(backward_ref[m], shaped, preferred_element_type=F32)
            work[third, real, :] = back[:, :128]
            work[third, imaginary, :] = back[:, 128:]
        out_ref[:, :, lanes] = work[third].reshape(groups, chunk, 128).astype(BF16)


def ocean_kernel(depth_ref, *refs):
    pieces, (weight_ref, out_ref, top_ref, columns) = refs[:NEAR], refs[NEAR:]
    masks = tap_masks(CELLS)
    level = lax.broadcasted_iota(jnp.int32, (OCH, CELLS), 0) % LEV
    for slot in range(SLOTS):
        lanes = slice(CELLS * slot, CELLS * (slot + 1))
        state = pieces[slot // CAP][slot % CAP].astype(F32)
        top_ref[:, lanes] = state[0:1]
        state = jnp.where(level < depth_ref[slot], state, 0.0)
        state = jnp.concatenate([state, jnp.zeros((OCH_PAD - OCH, CELLS), F32)], axis=0)
        for q, tap in enumerate(TAPS):
            moved = shifted(state, tap, masks[q]).astype(BF16)
            columns[OCH_PAD * q : OCH_PAD * (q + 1), lanes] = moved
    for at in range(0, SPAN, 512):
        out_ref[:, at : at + 512] = jnp.dot(
            weight_ref[...], columns[:, at : at + 512], preferred_element_type=F32
        )


def surface_kernel(*refs):
    count = 12
    sources, (updated_any, tiles_ref), held, (updated_ref, flux, sst, sems, out_sems) = (
        refs[:count], refs[count : count + 2], refs[count + 2 : 2 * count + 2],
        refs[2 * count + 2 :],
    )
    leaving = []
    (
        rows_ref, synthesis_ref, wide_ref, air_flux_ref, skip_ref, air_ref, place_ref, group_ref,
        forcing_weight_ref, wet_ref, decode_ref, top_ref,
    ) = held
    moves = list(zip(sources, held))
    ordered = moves[:4]
    for j in range(air_ref.shape[0]):
        ordered += [(source.at[j], target.at[j]) for source, target in moves[4:6]]
    copies = begin(ordered + moves[6:], sems)
    after = len(ordered)
    latitude_rows, longitudes, channels = air_ref.shape
    groups = rows_ref.shape[0]
    pairs = []
    copies[0].wait()
    for pair in range(latitude_rows // 2):
        both = rows_ref[:, 16 * pair : 16 * (pair + 1), :].astype(F32)
        pairs.extend([both[:, :8], both[:, 8:]])
    copies[1].wait()
    for j in range(latitude_rows):
        own = pairs[j].reshape(8 * groups, channels).astype(BF16)
        spectral = jnp.dot(synthesis_ref[...], own, preferred_element_type=F32)
        for one in copies[2:6] if j == 0 else copies[4 + 2 * j : 6 + 2 * j]:
            one.wait()
        mixed = gelu(spectral + skip_ref[j]).astype(BF16)
        wide = jnp.dot(mixed, wide_ref[...], preferred_element_type=F32)
        updated_ref[j] = air_ref[j].astype(F32) + wide[:, :channels]
        leave = pltpu.make_async_copy(updated_ref.at[j], updated_any.at[j], out_sems.at[j])
        leave.start()
        leaving.append(leave)
        narrow = jnp.concatenate(
            [wide[:, channels:], jnp.zeros((384 - longitudes, 128), F32)], axis=0
        )
        turned = jnp.transpose(narrow)
        extra = jnp.concatenate(
            [air_flux_ref[FC * j : FC * (j + 1), :], jnp.zeros((FC, 384 - longitudes), F32)], axis=1
        )
        total = turned[:FC] + turned[FC : 2 * FC] + extra
        for part in range(3):
            at = FC * (part * latitude_rows + j)
            flux[at : at + FC, :] = total[:, 128 * part : 128 * (part + 1)]
    for one in copies[after:]:
        one.wait()
    spread = jnp.dot(flux[...].astype(BF16), place_ref[...], preferred_element_type=F32)
    group = group_ref[...]
    forcing = jnp.zeros((FC, SPAN), F32)
    for at in range(3 * latitude_rows):
        forcing = forcing + jnp.where(group == at, spread[FC * at : FC * (at + 1), :], 0.0)
    masks = tap_masks(SPAN)
    columns = jnp.concatenate(
        [shifted(forcing, tap, masks[q]) for q, tap in enumerate(TAPS)], axis=0
    ).astype(BF16)
    hidden = gelu(
        wet_ref[...] + jnp.dot(forcing_weight_ref[...], columns, preferred_element_type=F32)
    ).astype(BF16)
    partial = jnp.dot(decode_ref[...], hidden, preferred_element_type=F32)
    change = jnp.zeros((1, SPAN), F32)
    for q, tap in enumerate(TAPS):
        change = change + shifted(partial[q : q + 1, :], tap, masks[q])
    surface = top_ref[...] + change
    for slot in range(SLOTS):
        sst[slot : slot + 1, :] = surface[:, CELLS * slot : CELLS * (slot + 1)]
    tiles = sst[...].astype(BF16)
    for member in range(tiles_ref.shape[0]):
        tiles_ref[member] = tiles
    for one in leaving:
        one.wait()


def imprint_kernel(
    updated_any, tiles_ref, cell_any, slot_any, imprint_ref, out_any,
    updated_ref, cell_ref, slot_ref, out_ref, sems, out_sems,
):
    rows, _, channels = updated_ref.shape
    copies = begin(
        [(cell_any, cell_ref), (slot_any, slot_ref)]
        + [(updated_any.at[j], updated_ref.at[j]) for j in range(rows)],
        sems,
    )
    tiles = tiles_ref[0]
    tripled = jnp.concatenate([tiles, tiles, tiles], axis=0)
    pieces = in_three(imprint_ref[...].reshape(1, channels))
    imprint = jnp.concatenate(
        [jnp.broadcast_to(piece, (SLOTS, channels)) for piece in pieces], axis=0
    )
    copies[0].wait()
    copies[1].wait()
    leaving = []
    for j in range(rows):
        picked = lax.dot_general(
            cell_ref[j], tripled, (((1,), (1,)), ((), ())), preferred_element_type=F32
        )
        chosen = picked.astype(BF16) * slot_ref[j]
        warmth = jnp.dot(chosen, imprint, preferred_element_type=F32)
        copies[2 + j].wait()
        out_ref[j] = (updated_ref[j] + warmth).astype(BF16)
        leave = pltpu.make_async_copy(out_ref.at[j], out_any.at[j], out_sems.at[j])
        leave.start()
        leaving.append(leave)
    for one in leaving:
        one.wait()


def mean_kernel(tiles_ref, cell_ref, slot_ref, out_ref):
    members = tiles_ref.shape[0]
    total = jnp.zeros(tiles_ref.shape[1:], F32)
    for member in range(members):
        total = total + tiles_ref[member].astype(F32)
    pieces = jnp.concatenate(in_three(total), axis=0)
    for j in range(cell_ref.shape[0]):
        picked = lax.dot_general(
            pieces, cell_ref[j], (((1,), (1,)), ((), ())), preferred_element_type=F32
        )
        joined = picked[:SLOTS] + picked[SLOTS : 2 * SLOTS] + picked[2 * SLOTS :]
        kept = jnp.where(slot_ref[j] > 0, joined, 0.0)
        out_ref[j : j + 1, :] = jnp.sum(kept, axis=0, keepdims=True) / members


def call(kernel, outs, operands, flops, scratch=(), limit=56, specs=None, out_specs=None):
    size = sum(math.prod(o.shape) * o.dtype.itemsize for o in list(outs) + list(operands))
    return pl.pallas_call(
        kernel,
        out_shape=outs if len(outs) > 1 else outs[0],
        in_specs=specs or [WHOLE] * len(operands),
        out_specs=out_specs or ([WHOLE] * len(outs) if len(outs) > 1 else WHOLE),
        scratch_shapes=list(scratch),
        compiler_params=pltpu.CompilerParams(vmem_limit_bytes=limit * 1024 * 1024),
        cost_estimate=pl.CostEstimate(
            flops=flops, bytes_accessed=min(size, flops), transcendentals=0
        ),
    )(*operands)


def held(operands):
    return [pltpu.VMEM(o.shape, o.dtype) for o in operands]


def shards(
    air_ensemble,
    sea_indicator,
    layernorm_scaling,
    harmonic_damping_factor,
    bypass_factor,
    core_exit_factor,
    air_to_exchange_factor,
    sea_heat_imprint,
    sea_ensemble_arrays,
    input_to_hidden_kernel,
    hidden_to_change_kernel,
    patch_exchange_pick,
    node_sea_pick,
    patch_holder_shift,
    wet_depth_layers,
):
    bands = lax.axis_size("space")
    members = lax.axis_size("member")
    air = air_ensemble[0]
    latitude_rows, longitudes, channels = air.shape
    latitudes = latitude_rows * bands
    hidden_channels = input_to_hidden_kernel.shape[1]
    per_device = MMAX // bands
    chunk = 2 * per_device * latitude_rows
    shape = jax.ShapeDtypeStruct

    analysis, synthesis = (jnp.asarray(t) for t in fourier_tables())
    spectra = call(
        analysis_kernel,
        [shape((bands, chunk, channels), BF16)],
        [air, layernorm_scaling, analysis],
        2 * 2 * MMAX * latitude_rows * longitudes * channels,
        held([air, analysis])
        + [
            pltpu.VMEM((bands, chunk, channels), BF16),
            pltpu.SemaphoreType.DMA((latitude_rows + 1,)),
            pltpu.SemaphoreType.DMA((latitude_rows // 2,)),
        ],
        specs=[FAR, WHOLE, FAR],
        out_specs=FAR,
    )
    gathered = lax.all_to_all(spectra, "space", split_axis=0, concat_axis=0, tiled=True)

    slots = sea_ensemble_arrays[0]
    far = [
        passed_along(slots[offset * CAP : (offset + 1) * CAP], "space", -offset)
        for offset in range(EARLY, NEAR)
    ]
    forward, backward = (jnp.asarray(t) for t in legendre_tables(latitudes))
    first = lax.axis_index("space") * per_device
    forward = lax.dynamic_slice_in_dim(forward, first, per_device, 0)
    backward = lax.dynamic_slice_in_dim(backward, first, per_device, 0)
    skip, air_flux, wide = call(
        local_kernel,
        [
            shape(air.shape, F32),
            shape((FC * latitude_rows, longitudes), F32),
            shape((channels, channels + 128), BF16),
        ],
        [air, layernorm_scaling, bypass_factor, core_exit_factor, air_to_exchange_factor.T],
        SMALL,
        held([air]) + [pltpu.SemaphoreType.DMA((latitude_rows,))],
        specs=[FAR] + [WHOLE] * 4,
    )
    offsets = patch_holder_shift[:, 0]
    earlier = jnp.tril(jnp.ones((HOME_DEV, HOME_DEV), jnp.int32), -1)
    positions = jnp.sum((offsets[:, None] == offsets[None, :]).astype(jnp.int32) * earlier, axis=1)
    targets = offsets * CAP + positions
    selected = targets[None, :] == jnp.arange(SLOTS, dtype=jnp.int32)[:, None]
    depths = jnp.sum(jnp.where(selected, wet_depth_layers[None, :], 0), axis=1)
    kernel = jnp.transpose(input_to_hidden_kernel, (1, 0, 2))
    state_weight = jnp.pad(kernel[:, :, :OCH], ((0, 0), (0, 0), (0, OCH_PAD - OCH))).reshape(
        hidden_channels, -1
    )
    forcing_weight = kernel[:, :, OCH:].reshape(hidden_channels, -1)
    decode_weight = jnp.pad(hidden_to_change_kernel, ((0, 16 - len(TAPS)), (0, 0)))
    picks = jnp.sum(jnp.where(selected[:, :, None], patch_exchange_pick[None], 0), axis=1)
    picks = picks.reshape(1, SPAN)
    line, column = picks // longitudes, picks % longitudes
    group = column // 128 * latitude_rows + line
    place = (column % 128 == jnp.arange(128, dtype=jnp.int32)[:, None]).astype(BF16)
    tile = node_sea_pick // CELLS
    holder = jnp.sum(
        jnp.where(
            tile[:, :, None] == jnp.arange(HOME_DEV, dtype=jnp.int32), targets[None, None, :], 0
        ),
        axis=2,
    )
    holder = jnp.where(sea_indicator > 0, holder, -1)
    cell = (
        (node_sea_pick % CELLS)[:, :, None] == jnp.arange(CELLS, dtype=jnp.int32)
    ).astype(BF16)
    slot_of = (
        holder[:, :, None] == jnp.arange(3 * SLOTS, dtype=jnp.int32) % SLOTS
    ).astype(BF16)
    slot_rows = (
        holder[:, None, :] == jnp.arange(SLOTS, dtype=jnp.int32)[None, :, None]
    ).astype(F32)
    filtered = call(
        legendre_kernel,
        [shape((bands, chunk, channels), BF16)],
        [gathered, forward, backward, harmonic_damping_factor],
        2 * 2 * 2 * per_device * LMAX * latitudes * channels,
        [pltpu.VMEM((channels // 128, bands * chunk, 128), F32)],
        limit=32,
    )
    filtered, late = lax.optimization_barrier((filtered, slots[CAP : EARLY * CAP]))
    returned = lax.all_to_all(filtered, "space", split_axis=0, concat_axis=0, tiled=True)
    near = [
        passed_along(late[at : at + CAP], "space", -(1 + at // CAP))
        for at in range(0, late.shape[0], CAP)
    ]
    wet, top = call(
        ocean_kernel,
        [shape((hidden_channels, SPAN), F32), shape((1, SPAN), F32)],
        [depths, slots[:CAP], *near, *far, state_weight],
        SMALL,
        [pltpu.VMEM((len(TAPS) * OCH_PAD, SPAN), BF16)],
        limit=32,
        specs=[pl.BlockSpec(memory_space=pltpu.SMEM)] + [WHOLE] * (NEAR + 1),
    )
    operands = [
        returned, synthesis, wide, air_flux, skip, air, place, group, forcing_weight, wet,
        decode_weight, top,
    ]
    updated, tiles = call(
        surface_kernel,
        [shape(air.shape, F32), shape((members, SLOTS, CELLS), BF16)],
        operands,
        2 * latitude_rows * longitudes * channels * (channels + 2 * MMAX),
        held(operands)
        + [
            pltpu.VMEM(air.shape, F32),
            pltpu.VMEM((3 * FC * latitude_rows, 128), F32),
            pltpu.VMEM((SLOTS, CELLS), F32),
            pltpu.SemaphoreType.DMA((len(operands) + 2 * latitude_rows,)),
            pltpu.SemaphoreType.DMA((latitude_rows,)),
        ],
        specs=[FAR] * len(operands),
        out_specs=[FAR, WHOLE],
    )
    everyone = lax.all_to_all(tiles, "member", split_axis=0, concat_axis=0, tiled=True)
    out = call(
        imprint_kernel,
        [shape(air.shape, BF16)],
        [updated, tiles, cell, slot_of, sea_heat_imprint],
        2 * latitude_rows * longitudes * channels * 256,
        held([updated, cell, slot_of, air])
        + [
            pltpu.SemaphoreType.DMA((latitude_rows + 2,)),
            pltpu.SemaphoreType.DMA((latitude_rows,)),
        ],
        specs=[FAR, WHOLE, FAR, FAR, WHOLE],
        out_specs=FAR,
    )
    mean = call(
        mean_kernel,
        [shape((latitude_rows, longitudes), F32)],
        [everyone, cell, slot_rows],
        2 * 3 * SLOTS * CELLS * latitude_rows * longitudes,
        limit=32,
    )
    return (out[None], mean)


def solution(mesh):
    in_specs = (
        P("member", "space", None, None),
        P("space", None),
        P(),
        P(),
        P(),
        P(),
        P(),
        P(),
        P("member", "space", None, None),
        P(),
        P(),
        P("space", None),
        P("space", None),
        P("space", None),
        P("space"),
    )
    out_specs = (P("member", "space", None, None), P("space", None))
    return jax.shard_map(shards, mesh=mesh, in_specs=in_specs, out_specs=out_specs, check_vma=False)
```

```python
import functools
import math

import jax
import jax.numpy as jnp
import numpy as np
from jax import lax
from jax.experimental import pallas as pl
from jax.experimental.pallas import tpu as pltpu
from jax.sharding import PartitionSpec as P

MERIDIAN_TOTAL = 360
MMAX = 128
LMAX = 128
FC = 8
LEV = 19
CAP = 2
NEAR = 8
HOME_DEV = 14
SLOTS = NEAR * CAP
CELLS = 128
SPAN = SLOTS * CELLS
OCH = 76
OCH_PAD = 80
TAPS = [(row, col) for row in (-1, 0, 1) for col in (-1, 0, 1)]
EARLY = 3
SMALL = 1024
BF16 = jnp.bfloat16
F32 = jnp.float32
WHOLE = pl.BlockSpec(memory_space=pltpu.VMEM)
FAR = pl.BlockSpec(memory_space=pltpu.HBM)


def passed_along(value, axis, by):
    devices = lax.axis_size(axis)
    return lax.ppermute(value, axis, [(i, (i + by) % devices) for i in range(devices)])


def fourier_tables():
    product = np.arange(MMAX)[:, None] * np.arange(MERIDIAN_TOTAL)[None, :] % MERIDIAN_TOTAL
    angles = 2.0 * np.pi / MERIDIAN_TOTAL * product
    analysis = np.stack([np.cos(angles), -np.sin(angles)], axis=1) / MERIDIAN_TOTAL
    weights = np.where(np.arange(MMAX) == 0, 1.0, 2.0)[:, None]
    synthesis = np.stack([weights * np.cos(angles), -weights * np.sin(angles)], axis=1)
    return (
        analysis.reshape(2 * MMAX, MERIDIAN_TOTAL).astype(BF16),
        synthesis.reshape(2 * MMAX, MERIDIAN_TOTAL).T.astype(BF16),
    )


def legendre_tables(latitudes):
    theta = np.pi / latitudes * (np.arange(latitudes) + 0.5)
    cosine = np.cos(theta)[None, :]
    sine = np.sin(theta)
    counter = np.arange(1, MMAX)
    totals = np.concatenate([[0.0], np.cumsum(np.log((2.0 * counter - 1.0) / (2.0 * counter)))])
    order = np.arange(MMAX, dtype=np.float64)[:, None]
    diagonal = np.exp(
        0.5 * (np.log((2.0 * order + 1.0) / (4.0 * np.pi)) + totals[:, None])
        + order * np.log(sine)[None, :]
    )
    values = np.zeros((MMAX, LMAX, latitudes))
    latest = np.zeros((MMAX, latitudes))
    before = np.zeros((MMAX, latitudes))
    for degree in range(LMAX):
        lowered = (degree - 1.0) ** 2
        upward = np.sqrt(
            max(4.0 * degree * degree - 1.0, 0.0) / np.maximum(degree * degree - order * order, 1.0)
        )
        damping = np.sqrt(
            np.maximum(lowered - order * order, 0.0) / max(4.0 * lowered - 1.0, 1.0)
        )
        current = upward * (cosine * latest - damping * before)
        current = np.where(degree == order, diagonal, current)
        current = np.where(degree < order, 0.0, current)
        values[:, degree, :] = current
        latest, before = current, latest
    quadrature = 2.0 * np.pi * np.pi / latitudes * sine
    forward = (values * quadrature[None, None, :]).astype(BF16)
    backward = np.transpose(values, (0, 2, 1)).astype(BF16)
    return forward, backward


def gelu(x):
    inner = math.sqrt(2.0 / math.pi) * (x + 0.044715 * (x * x * x))
    return 0.5 * x * (1.0 + jnp.tanh(inner))


def tap_masks(width):
    lane = lax.broadcasted_iota(jnp.int32, (1, width), 1) % CELLS
    row, col = lane // 16, lane % 16
    masks = []
    for down, right in TAPS:
        inside = (row + down >= 0) & (row + down < 8) & (col + right >= 0) & (col + right < 16)
        masks.append(inside)
    return masks


def shifted(x, tap, mask):
    by = 16 * tap[0] + tap[1]
    if by == 0:
        return x
    rolled = pltpu.roll(x, (-by) % x.shape[1], 1)
    return jnp.where(mask, rolled, 0.0)


def in_three(x):
    high = x.astype(BF16)
    rest = x - high.astype(F32)
    middle = rest.astype(BF16)
    return high, middle, (rest - middle.astype(F32)).astype(BF16)


def begin(copies, sems):
    started = [
        pltpu.make_async_copy(source, target, sems.at[i])
        for i, (source, target) in enumerate(copies)
    ]
    for one in started:
        one.start()
    return started


def normalised(x, scale):
    centered = x - jnp.mean(x, axis=-1, keepdims=True)
    spread = jnp.mean(centered * centered, axis=-1, keepdims=True)
    return (centered * lax.rsqrt(spread + 1e-05) * scale).astype(BF16)


def analysis_kernel(
    air_any, scale_ref, table_any, spectra_any, air_ref, table_ref, spectra_ref, sems, out_sems
):
    rows = air_ref.shape[0]
    leaving = []
    groups = spectra_ref.shape[0]
    copies = begin(
        [(air_any.at[j], air_ref.at[j]) for j in range(rows)] + [(table_any, table_ref)], sems
    )
    scale = scale_ref[...].reshape(1, scale_ref.shape[0])
    for pair in range(rows // 2):
        both = []
        for j in (2 * pair, 2 * pair + 1):
            copies[j].wait()
            normed = normalised(air_ref[j].astype(F32), scale)
            if j == 0:
                copies[rows].wait()
            out = jnp.dot(table_ref[...], normed, preferred_element_type=F32)
            both.append(out.reshape(groups, 8, out.shape[1]))
        block = jnp.concatenate(both, axis=1)
        rows_16 = slice(16 * pair, 16 * (pair + 1))
        spectra_ref[:, rows_16, :] = block.astype(BF16)
        leave = pltpu.make_async_copy(
            spectra_ref.at[:, rows_16], spectra_any.at[:, rows_16], out_sems.at[pair]
        )
        leave.start()
        leaving.append(leave)
    for one in leaving:
        one.wait()


def local_kernel(
    air_any, scale_ref, bypass_ref, exit_ref, exchange_ref, skip_ref, flux_ref, wide_ref,
    air_ref, sems,
):
    rows = air_ref.shape[0]
    copies = begin([(air_any.at[j], air_ref.at[j]) for j in range(rows)], sems)
    scale = scale_ref[...].reshape(1, scale_ref.shape[0])
    channels = exit_ref.shape[0]
    dims = (((1,), (1,)), ((), ()))
    through = lax.dot_general(
        exit_ref[...], exchange_ref[...], dims, preferred_element_type=F32
    )
    high = through.astype(BF16)
    low = (through - high.astype(F32)).astype(BF16)
    wide_ref[:, :channels] = exit_ref[...]
    wide_ref[:, channels:] = jnp.concatenate(
        [high.astype(F32), low.astype(F32), jnp.zeros((channels, 128 - 2 * FC), F32)], axis=1
    ).astype(BF16)
    for j in range(rows):
        copies[j].wait()
        own = air_ref[j]
        normed = normalised(own.astype(F32), scale)
        skip_ref[j] = jnp.dot(normed, bypass_ref[...], preferred_element_type=F32)
        flux_ref[FC * j : FC * (j + 1), :] = lax.dot_general(
            exchange_ref[...], own, dims, preferred_element_type=F32
        )


def legendre_kernel(x_ref, forward_ref, backward_ref, gains_ref, out_ref, work):
    groups, chunk, channels = x_ref.shape
    total = groups * chunk
    latitudes = total // 8
    for third in range(channels // 128):
        lanes = slice(128 * third, 128 * (third + 1))
        work[third] = x_ref[:, :, lanes].astype(F32).reshape(total, 128)
        gains = gains_ref[:, lanes]
        gains = jnp.concatenate([gains, gains], axis=1)
        for m in range(4):
            real, imaginary = (pl.ds(2 * m + r, latitudes, stride=8) for r in (0, 1))
            own = jnp.concatenate(
                [work[third, real, :], work[third, imaginary, :]], axis=1
            ).astype(BF16)
            coefficients = jnp.dot(forward_ref[m], own, preferred_element_type=F32)
            shaped = (coefficients * gains).astype(BF16)
            back = jnp.dot(backward_ref[m], shaped, preferred_element_type=F32)
            work[third, real, :] = back[:, :128]
            work[third, imaginary, :] = back[:, 128:]
        out_ref[:, :, lanes] = work[third].reshape(groups, chunk, 128).astype(BF16)


def ocean_kernel(first, depth_ref, *refs):
    pieces, (weight_ref, out_ref, columns) = refs[:-3], refs[-3:]
    masks = tap_masks(CELLS)
    level = lax.broadcasted_iota(jnp.int32, (OCH, CELLS), 0) % LEV
    hidden_channels = weight_ref.shape[0]
    for slot in range(CAP * len(pieces)):
        lanes = slice(CELLS * slot, CELLS * (slot + 1))
        state = pieces[slot // CAP][slot % CAP].astype(F32)
        out_ref[hidden_channels:, lanes] = jnp.broadcast_to(state[0:1], (8, CELLS))
        state = jnp.where(level < depth_ref[first + slot], state, 0.0)
        state = jnp.concatenate([state, jnp.zeros((OCH_PAD - OCH, CELLS), F32)], axis=0)
        for q, tap in enumerate(TAPS):
            moved = shifted(state, tap, masks[q]).astype(BF16)
            columns[OCH_PAD * q : OCH_PAD * (q + 1), lanes] = moved
    for at in range(0, out_ref.shape[1], 512):
        out_ref[:hidden_channels, at : at + 512] = jnp.dot(
            weight_ref[...], columns[:, at : at + 512], preferred_element_type=F32
        )


def surface_kernel(*refs):
    count = 12
    sources, (updated_any, tiles_ref), held, (updated_ref, flux, sst, sems, out_sems) = (
        refs[:count], refs[count : count + 2], refs[count + 2 : 2 * count + 2],
        refs[2 * count + 2 :],
    )
    leaving = []
    (
        rows_ref, synthesis_ref, wide_ref, air_flux_ref, skip_ref, air_ref, place_ref, group_ref,
        forcing_weight_ref, decode_ref, far_ref, near_ref,
    ) = held
    moves = list(zip(sources, held))
    ordered = moves[:4]
    for j in range(air_ref.shape[0]):
        ordered += [(source.at[j], target.at[j]) for source, target in moves[4:6]]
    copies = begin(ordered + moves[6:], sems)
    after = len(ordered)
    latitude_rows, longitudes, channels = air_ref.shape
    groups = rows_ref.shape[0]
    pairs = []
    copies[0].wait()
    for pair in range(latitude_rows // 2):
        both = rows_ref[:, 16 * pair : 16 * (pair + 1), :].astype(F32)
        pairs.extend([both[:, :8], both[:, 8:]])
    copies[1].wait()
    for j in range(latitude_rows):
        own = pairs[j].reshape(8 * groups, channels).astype(BF16)
        spectral = jnp.dot(synthesis_ref[...], own, preferred_element_type=F32)
        for one in copies[2:6] if j == 0 else copies[4 + 2 * j : 6 + 2 * j]:
            one.wait()
        mixed = gelu(spectral + skip_ref[j]).astype(BF16)
        wide = jnp.dot(mixed, wide_ref[...], preferred_element_type=F32)
        updated_ref[j] = air_ref[j].astype(F32) + wide[:, :channels]
        leave = pltpu.make_async_copy(updated_ref.at[j], updated_any.at[j], out_sems.at[j])
        leave.start()
        leaving.append(leave)
        narrow = jnp.concatenate(
            [wide[:, channels:], jnp.zeros((384 - longitudes, 128), F32)], axis=0
        )
        turned = jnp.transpose(narrow)
        extra = jnp.concatenate(
            [air_flux_ref[FC * j : FC * (j + 1), :], jnp.zeros((FC, 384 - longitudes), F32)], axis=1
        )
        total = turned[:FC] + turned[FC : 2 * FC] + extra
        for part in range(3):
            at = FC * (part * latitude_rows + j)
            flux[at : at + FC, :] = total[:, 128 * part : 128 * (part + 1)]
    for one in copies[after:]:
        one.wait()
    spread = jnp.dot(flux[...].astype(BF16), place_ref[...], preferred_element_type=F32)
    group = group_ref[...]
    forcing = jnp.zeros((FC, SPAN), F32)
    for at in range(3 * latitude_rows):
        forcing = forcing + jnp.where(group == at, spread[FC * at : FC * (at + 1), :], 0.0)
    masks = tap_masks(SPAN)
    columns = jnp.concatenate(
        [shifted(forcing, tap, masks[q]) for q, tap in enumerate(TAPS)], axis=0
    ).astype(BF16)
    hidden_channels = forcing_weight_ref.shape[0]
    split = far_ref.shape[1]
    partials = []
    for wet_ref, lanes in ((far_ref, slice(0, split)), (near_ref, slice(split, SPAN))):
        hidden = gelu(
            wet_ref[:hidden_channels, :]
            + jnp.dot(forcing_weight_ref[...], columns[:, lanes], preferred_element_type=F32)
        ).astype(BF16)
        partials.append(jnp.dot(decode_ref[...], hidden, preferred_element_type=F32))
    partial = jnp.concatenate(partials, axis=1)
    surface = jnp.concatenate(
        [ref[hidden_channels : hidden_channels + 1, :] for ref in (far_ref, near_ref)], axis=1
    )
    change = jnp.zeros((1, SPAN), F32)
    for q, tap in enumerate(TAPS):
        change = change + shifted(partial[q : q + 1, :], tap, masks[q])
    surface = surface + change
    for slot in range(SLOTS):
        sst[slot : slot + 1, :] = surface[:, CELLS * slot : CELLS * (slot + 1)]
    tiles = sst[...].astype(BF16)
    for member in range(tiles_ref.shape[0]):
        tiles_ref[member] = tiles
    for one in leaving:
        one.wait()


def imprint_kernel(
    updated_any, tiles_ref, cell_any, slot_any, imprint_ref, out_any,
    updated_ref, cell_ref, slot_ref, out_ref, sems, out_sems,
):
    rows, _, channels = updated_ref.shape
    copies = begin(
        [(cell_any, cell_ref), (slot_any, slot_ref)]
        + [(updated_any.at[j], updated_ref.at[j]) for j in range(rows)],
        sems,
    )
    tiles = tiles_ref[0]
    tripled = jnp.concatenate([tiles, tiles, tiles], axis=0)
    pieces = in_three(imprint_ref[...].reshape(1, channels))
    imprint = jnp.concatenate(
        [jnp.broadcast_to(piece, (SLOTS, channels)) for piece in pieces], axis=0
    )
    copies[0].wait()
    copies[1].wait()
    leaving = []
    for j in range(rows):
        picked = lax.dot_general(
            cell_ref[j], tripled, (((1,), (1,)), ((), ())), preferred_element_type=F32
        )
        chosen = picked.astype(BF16) * slot_ref[j]
        warmth = jnp.dot(chosen, imprint, preferred_element_type=F32)
        copies[2 + j].wait()
        out_ref[j] = (updated_ref[j] + warmth).astype(BF16)
        leave = pltpu.make_async_copy(out_ref.at[j], out_any.at[j], out_sems.at[j])
        leave.start()
        leaving.append(leave)
    for one in leaving:
        one.wait()


def mean_kernel(tiles_ref, cell_ref, slot_ref, out_ref):
    members = tiles_ref.shape[0]
    total = jnp.zeros(tiles_ref.shape[1:], F32)
    for member in range(members):
        total = total + tiles_ref[member].astype(F32)
    pieces = jnp.concatenate(in_three(total), axis=0)
    for j in range(cell_ref.shape[0]):
        picked = lax.dot_general(
            pieces, cell_ref[j], (((1,), (1,)), ((), ())), preferred_element_type=F32
        )
        joined = picked[:SLOTS] + picked[SLOTS : 2 * SLOTS] + picked[2 * SLOTS :]
        kept = jnp.where(slot_ref[j] > 0, joined, 0.0)
        out_ref[j : j + 1, :] = jnp.sum(kept, axis=0, keepdims=True) / members


def call(kernel, outs, operands, flops, scratch=(), limit=56, specs=None, out_specs=None):
    size = sum(math.prod(o.shape) * o.dtype.itemsize for o in list(outs) + list(operands))
    return pl.pallas_call(
        kernel,
        out_shape=outs if len(outs) > 1 else outs[0],
        in_specs=specs or [WHOLE] * len(operands),
        out_specs=out_specs or ([WHOLE] * len(outs) if len(outs) > 1 else WHOLE),
        scratch_shapes=list(scratch),
        compiler_params=pltpu.CompilerParams(vmem_limit_bytes=limit * 1024 * 1024),
        cost_estimate=pl.CostEstimate(
            flops=flops, bytes_accessed=min(size, flops), transcendentals=0
        ),
    )(*operands)


def held(operands):
    return [pltpu.VMEM(o.shape, o.dtype) for o in operands]


def shards(
    air_ensemble,
    sea_indicator,
    layernorm_scaling,
    harmonic_damping_factor,
    bypass_factor,
    core_exit_factor,
    air_to_exchange_factor,
    sea_heat_imprint,
    sea_ensemble_arrays,
    input_to_hidden_kernel,
    hidden_to_change_kernel,
    patch_exchange_pick,
    node_sea_pick,
    patch_holder_shift,
    wet_depth_layers,
):
    bands = lax.axis_size("space")
    members = lax.axis_size("member")
    air = air_ensemble[0]
    latitude_rows, longitudes, channels = air.shape
    latitudes = latitude_rows * bands
    hidden_channels = input_to_hidden_kernel.shape[1]
    per_device = MMAX // bands
    chunk = 2 * per_device * latitude_rows
    shape = jax.ShapeDtypeStruct

    analysis, synthesis = (jnp.asarray(t) for t in fourier_tables())
    spectra = call(
        analysis_kernel,
        [shape((bands, chunk, channels), BF16)],
        [air, layernorm_scaling, analysis],
        2 * 2 * MMAX * latitude_rows * longitudes * channels,
        held([air, analysis])
        + [
            pltpu.VMEM((bands, chunk, channels), BF16),
            pltpu.SemaphoreType.DMA((latitude_rows + 1,)),
            pltpu.SemaphoreType.DMA((latitude_rows // 2,)),
        ],
        specs=[FAR, WHOLE, FAR],
        out_specs=FAR,
    )
    gathered = lax.all_to_all(spectra, "space", split_axis=0, concat_axis=0, tiled=True)

    slots = sea_ensemble_arrays[0]
    far = [
        passed_along(slots[offset * CAP : (offset + 1) * CAP], "space", -offset)
        for offset in range(EARLY, NEAR)
    ]
    forward, backward = (jnp.asarray(t) for t in legendre_tables(latitudes))
    first = lax.axis_index("space") * per_device
    forward = lax.dynamic_slice_in_dim(forward, first, per_device, 0)
    backward = lax.dynamic_slice_in_dim(backward, first, per_device, 0)
    skip, air_flux, wide = call(
        local_kernel,
        [
            shape(air.shape, F32),
            shape((FC * latitude_rows, longitudes), F32),
            shape((channels, channels + 128), BF16),
        ],
        [air, layernorm_scaling, bypass_factor, core_exit_factor, air_to_exchange_factor.T],
        SMALL,
        held([air]) + [pltpu.SemaphoreType.DMA((latitude_rows,))],
        specs=[FAR] + [WHOLE] * 4,
    )
    offsets = patch_holder_shift[:, 0]
    earlier = jnp.tril(jnp.ones((HOME_DEV, HOME_DEV), jnp.int32), -1)
    positions = jnp.sum((offsets[:, None] == offsets[None, :]).astype(jnp.int32) * earlier, axis=1)
    places = jnp.where(offsets >= EARLY, offsets - EARLY + 1, offsets + NEAR - EARLY)
    targets = jnp.where(offsets == 0, 0, places) * CAP + positions
    selected = targets[None, :] == jnp.arange(SLOTS, dtype=jnp.int32)[:, None]
    depths = jnp.sum(jnp.where(selected, wet_depth_layers[None, :], 0), axis=1)
    kernel = jnp.transpose(input_to_hidden_kernel, (1, 0, 2))
    state_weight = jnp.pad(kernel[:, :, :OCH], ((0, 0), (0, 0), (0, OCH_PAD - OCH))).reshape(
        hidden_channels, -1
    )
    forcing_weight = kernel[:, :, OCH:].reshape(hidden_channels, -1)
    decode_weight = jnp.pad(hidden_to_change_kernel, ((0, 16 - len(TAPS)), (0, 0)))
    picks = jnp.sum(jnp.where(selected[:, :, None], patch_exchange_pick[None], 0), axis=1)
    picks = picks.reshape(1, SPAN)
    line, column = picks // longitudes, picks % longitudes
    group = column // 128 * latitude_rows + line
    place = (column % 128 == jnp.arange(128, dtype=jnp.int32)[:, None]).astype(BF16)
    tile = node_sea_pick // CELLS
    holder = jnp.sum(
        jnp.where(
            tile[:, :, None] == jnp.arange(HOME_DEV, dtype=jnp.int32), targets[None, None, :], 0
        ),
        axis=2,
    )
    holder = jnp.where(sea_indicator > 0, holder, -1)
    cell = (
        (node_sea_pick % CELLS)[:, :, None] == jnp.arange(CELLS, dtype=jnp.int32)
    ).astype(BF16)
    slot_of = (
        holder[:, :, None] == jnp.arange(3 * SLOTS, dtype=jnp.int32) % SLOTS
    ).astype(BF16)
    slot_rows = (
        holder[:, None, :] == jnp.arange(SLOTS, dtype=jnp.int32)[None, :, None]
    ).astype(F32)
    filtered = call(
        legendre_kernel,
        [shape((bands, chunk, channels), BF16)],
        [gathered, forward, backward, harmonic_damping_factor],
        2 * 2 * 2 * per_device * LMAX * latitudes * channels,
        [pltpu.VMEM((channels // 128, bands * chunk, 128), F32)],
        limit=32,
    )
    filtered, late = lax.optimization_barrier((filtered, slots[CAP : EARLY * CAP]))
    returned = lax.all_to_all(filtered, "space", split_axis=0, concat_axis=0, tiled=True)
    near = [
        passed_along(late[at : at + CAP], "space", -(1 + at // CAP))
        for at in range(0, late.shape[0], CAP)
    ]
    def wet(first, parts):
        width = CAP * CELLS * len(parts)
        return call(
            functools.partial(ocean_kernel, first),
            [shape((hidden_channels + 8, width), F32)],
            [depths, *parts, state_weight],
            SMALL,
            [pltpu.VMEM((len(TAPS) * OCH_PAD, width), BF16)],
            limit=32,
            specs=[pl.BlockSpec(memory_space=pltpu.SMEM)] + [WHOLE] * (len(parts) + 1),
        )

    wet_far = wet(0, [slots[:CAP], *far])
    wet_near = wet(CAP * (len(far) + 1), near)
    operands = [
        returned, synthesis, wide, air_flux, skip, air, place, group, forcing_weight,
        decode_weight, wet_far, wet_near,
    ]
    updated, tiles = call(
        surface_kernel,
        [shape(air.shape, F32), shape((members, SLOTS, CELLS), BF16)],
        operands,
        2 * latitude_rows * longitudes * channels * (channels + 2 * MMAX),
        held(operands)
        + [
            pltpu.VMEM(air.shape, F32),
            pltpu.VMEM((3 * FC * latitude_rows, 128), F32),
            pltpu.VMEM((SLOTS, CELLS), F32),
            pltpu.SemaphoreType.DMA((len(operands) + 2 * latitude_rows,)),
            pltpu.SemaphoreType.DMA((latitude_rows,)),
        ],
        specs=[FAR] * len(operands),
        out_specs=[FAR, WHOLE],
    )
    everyone = lax.all_to_all(tiles, "member", split_axis=0, concat_axis=0, tiled=True)
    out = call(
        imprint_kernel,
        [shape(air.shape, BF16)],
        [updated, tiles, cell, slot_of, sea_heat_imprint],
        2 * latitude_rows * longitudes * channels * 256,
        held([updated, cell, slot_of, air])
        + [
            pltpu.SemaphoreType.DMA((latitude_rows + 2,)),
            pltpu.SemaphoreType.DMA((latitude_rows,)),
        ],
        specs=[FAR, WHOLE, FAR, FAR, WHOLE],
        out_specs=FAR,
    )
    mean = call(
        mean_kernel,
        [shape((latitude_rows, longitudes), F32)],
        [everyone, cell, slot_rows],
        2 * 3 * SLOTS * CELLS * latitude_rows * longitudes,
        limit=32,
    )
    return (out[None], mean)


def solution(mesh):
    in_specs = (
        P("member", "space", None, None),
        P("space", None),
        P(),
        P(),
        P(),
        P(),
        P(),
        P(),
        P("member", "space", None, None),
        P(),
        P(),
        P("space", None),
        P("space", None),
        P("space", None),
        P("space"),
    )
    out_specs = (P("member", "space", None, None), P("space", None))
    return jax.shard_map(shards, mesh=mesh, in_specs=in_specs, out_specs=out_specs, check_vma=False)
```

```python
import functools
import math

import jax
import jax.numpy as jnp
import numpy as np
from jax import lax
from jax.experimental import pallas as pl
from jax.experimental.pallas import tpu as pltpu
from jax.sharding import PartitionSpec as P

MERIDIAN_TOTAL = 360
MMAX = 128
LMAX = 128
FC = 8
LEV = 19
CAP = 2
NEAR = 8
HOME_DEV = 14
SLOTS = NEAR * CAP
CELLS = 128
SPAN = SLOTS * CELLS
OCH = 76
OCH_PAD = 80
TAPS = [(row, col) for row in (-1, 0, 1) for col in (-1, 0, 1)]
EARLY = 3
SMALL = 1024
BF16 = jnp.bfloat16
F32 = jnp.float32
WHOLE = pl.BlockSpec(memory_space=pltpu.VMEM)
FAR = pl.BlockSpec(memory_space=pltpu.HBM)


def passed_along(value, axis, by):
    devices = lax.axis_size(axis)
    return lax.ppermute(value, axis, [(i, (i + by) % devices) for i in range(devices)])


def fourier_tables():
    product = np.arange(MMAX)[:, None] * np.arange(MERIDIAN_TOTAL)[None, :] % MERIDIAN_TOTAL
    angles = 2.0 * np.pi / MERIDIAN_TOTAL * product
    analysis = np.stack([np.cos(angles), -np.sin(angles)], axis=1) / MERIDIAN_TOTAL
    weights = np.where(np.arange(MMAX) == 0, 1.0, 2.0)[:, None]
    synthesis = np.stack([weights * np.cos(angles), -weights * np.sin(angles)], axis=1)
    return (
        analysis.reshape(2 * MMAX, MERIDIAN_TOTAL).astype(BF16),
        synthesis.reshape(2 * MMAX, MERIDIAN_TOTAL).T.astype(BF16),
    )


def legendre_tables(latitudes):
    theta = np.pi / latitudes * (np.arange(latitudes) + 0.5)
    cosine = np.cos(theta)[None, :]
    sine = np.sin(theta)
    counter = np.arange(1, MMAX)
    totals = np.concatenate([[0.0], np.cumsum(np.log((2.0 * counter - 1.0) / (2.0 * counter)))])
    order = np.arange(MMAX, dtype=np.float64)[:, None]
    diagonal = np.exp(
        0.5 * (np.log((2.0 * order + 1.0) / (4.0 * np.pi)) + totals[:, None])
        + order * np.log(sine)[None, :]
    )
    values = np.zeros((MMAX, LMAX, latitudes))
    latest = np.zeros((MMAX, latitudes))
    before = np.zeros((MMAX, latitudes))
    for degree in range(LMAX):
        lowered = (degree - 1.0) ** 2
        upward = np.sqrt(
            max(4.0 * degree * degree - 1.0, 0.0) / np.maximum(degree * degree - order * order, 1.0)
        )
        damping = np.sqrt(
            np.maximum(lowered - order * order, 0.0) / max(4.0 * lowered - 1.0, 1.0)
        )
        current = upward * (cosine * latest - damping * before)
        current = np.where(degree == order, diagonal, current)
        current = np.where(degree < order, 0.0, current)
        values[:, degree, :] = current
        latest, before = current, latest
    quadrature = 2.0 * np.pi * np.pi / latitudes * sine
    forward = (values * quadrature[None, None, :]).astype(BF16)
    backward = np.transpose(values, (0, 2, 1)).astype(BF16)
    return forward, backward


def gelu(x):
    inner = math.sqrt(2.0 / math.pi) * (x + 0.044715 * (x * x * x))
    return 0.5 * x * (1.0 + jnp.tanh(inner))


def tap_masks(width):
    lane = lax.broadcasted_iota(jnp.int32, (1, width), 1) % CELLS
    row, col = lane // 16, lane % 16
    masks = []
    for down, right in TAPS:
        inside = (row + down >= 0) & (row + down < 8) & (col + right >= 0) & (col + right < 16)
        masks.append(inside)
    return masks


def shifted(x, tap, mask):
    by = 16 * tap[0] + tap[1]
    if by == 0:
        return x
    rolled = pltpu.roll(x, (-by) % x.shape[1], 1)
    return jnp.where(mask, rolled, 0.0)


def in_three(x):
    high = x.astype(BF16)
    rest = x - high.astype(F32)
    middle = rest.astype(BF16)
    return high, middle, (rest - middle.astype(F32)).astype(BF16)


def begin(copies, sems):
    started = [
        pltpu.make_async_copy(source, target, sems.at[i])
        for i, (source, target) in enumerate(copies)
    ]
    for one in started:
        one.start()
    return started


def normalised(x, scale):
    centered = x - jnp.mean(x, axis=-1, keepdims=True)
    spread = jnp.mean(centered * centered, axis=-1, keepdims=True)
    return (centered * lax.rsqrt(spread + 1e-05) * scale).astype(BF16)


def analysis_kernel(
    air_any, scale_ref, table_any, spectra_any, air_ref, table_ref, spectra_ref, sems, out_sems
):
    rows = air_ref.shape[0]
    leaving = []
    groups = spectra_ref.shape[0]
    copies = begin(
        [(air_any.at[j], air_ref.at[j]) for j in range(rows)] + [(table_any, table_ref)], sems
    )
    scale = scale_ref[...].reshape(1, scale_ref.shape[0])
    for pair in range(rows // 2):
        both = []
        for j in (2 * pair, 2 * pair + 1):
            copies[j].wait()
            normed = normalised(air_ref[j].astype(F32), scale)
            if j == 0:
                copies[rows].wait()
            out = jnp.dot(table_ref[...], normed, preferred_element_type=F32)
            both.append(out.reshape(groups, 8, out.shape[1]))
        block = jnp.concatenate(both, axis=1)
        rows_16 = slice(16 * pair, 16 * (pair + 1))
        spectra_ref[:, rows_16, :] = block.astype(BF16)
        leave = pltpu.make_async_copy(
            spectra_ref.at[:, rows_16], spectra_any.at[:, rows_16], out_sems.at[pair]
        )
        leave.start()
        leaving.append(leave)
    for one in leaving:
        one.wait()


def local_kernel(
    air_any, scale_ref, bypass_ref, exit_ref, exchange_ref, synthesis_ref, place_ref,
    skip_ref, pack_ref, air_ref, sems,
):
    rows = air_ref.shape[0]
    copies = begin([(air_any.at[j], air_ref.at[j]) for j in range(rows)], sems)
    scale = scale_ref[...].reshape(1, scale_ref.shape[0])
    channels = exit_ref.shape[0]
    dims = (((1,), (1,)), ((), ()))
    through = lax.dot_general(
        exit_ref[...], exchange_ref[...], dims, preferred_element_type=F32
    )
    high = through.astype(BF16)
    low = (through - high.astype(F32)).astype(BF16)
    pack_ref[:384, :channels] = exit_ref[...]
    pack_ref[:384, channels:] = jnp.concatenate(
        [high.astype(F32), low.astype(F32), jnp.zeros((channels, 128 - 2 * FC), F32)], axis=1
    ).astype(BF16)
    pack_ref[384:768, :] = jnp.zeros((384, 512), BF16)
    longitudes, orders = synthesis_ref.shape
    pack_ref[384 : 384 + longitudes, :orders] = synthesis_ref[...]
    for block in range(SPAN // 512):
        pack_ref[768 + 128 * block : 896 + 128 * block, :] = place_ref[
            :, 512 * block : 512 * (block + 1)
        ]
    for j in range(rows):
        copies[j].wait()
        own = air_ref[j]
        normed = normalised(own.astype(F32), scale)
        skip_ref[j] = jnp.dot(normed, bypass_ref[...], preferred_element_type=F32)
        skip_ref[rows, FC * j : FC * (j + 1), :longitudes] = lax.dot_general(
            exchange_ref[...], own, dims, preferred_element_type=F32
        )


def legendre_kernel(x_ref, forward_ref, backward_ref, gains_ref, out_ref, work):
    groups, chunk, channels = x_ref.shape
    total = groups * chunk
    latitudes = total // 8
    for third in range(channels // 128):
        lanes = slice(128 * third, 128 * (third + 1))
        work[third] = x_ref[:, :, lanes].astype(F32).reshape(total, 128)
        gains = gains_ref[:, lanes]
        gains = jnp.concatenate([gains, gains], axis=1)
        for m in range(4):
            real, imaginary = (pl.ds(2 * m + r, latitudes, stride=8) for r in (0, 1))
            own = jnp.concatenate(
                [work[third, real, :], work[third, imaginary, :]], axis=1
            ).astype(BF16)
            coefficients = jnp.dot(forward_ref[m], own, preferred_element_type=F32)
            shaped = (coefficients * gains).astype(BF16)
            back = jnp.dot(backward_ref[m], shaped, preferred_element_type=F32)
            work[third, real, :] = back[:, :128]
            work[third, imaginary, :] = back[:, 128:]
        out_ref[:, :, lanes] = work[third].reshape(groups, chunk, 128).astype(BF16)


def ocean_kernel(first, depth_ref, *refs):
    pieces, (weight_ref, out_ref, columns) = refs[:-3], refs[-3:]
    masks = tap_masks(CELLS)
    level = lax.broadcasted_iota(jnp.int32, (OCH, CELLS), 0) % LEV
    hidden_channels = weight_ref.shape[0]
    for slot in range(CAP * len(pieces)):
        lanes = slice(CELLS * slot, CELLS * (slot + 1))
        state = pieces[slot // CAP][slot % CAP].astype(F32)
        out_ref[hidden_channels:, lanes] = jnp.broadcast_to(state[0:1], (8, CELLS))
        state = jnp.where(level < depth_ref[first + slot], state, 0.0)
        state = jnp.concatenate([state, jnp.zeros((OCH_PAD - OCH, CELLS), F32)], axis=0)
        for q, tap in enumerate(TAPS):
            moved = shifted(state, tap, masks[q]).astype(BF16)
            columns[OCH_PAD * q : OCH_PAD * (q + 1), lanes] = moved
    for at in range(0, out_ref.shape[1], 512):
        out_ref[:hidden_channels, at : at + 512] = jnp.dot(
            weight_ref[...], columns[:, at : at + 512], preferred_element_type=F32
        )


def surface_kernel(rows_ref, *refs):
    count = 8
    sources, (updated_any, tiles_ref), held, (updated_ref, flux, sst, sems, out_sems) = (
        refs[:count], refs[count : count + 2], refs[count + 2 : 2 * count + 2],
        refs[2 * count + 2 :],
    )
    leaving = []
    (
        pack_ref, skip_ref, air_ref, group_ref, forcing_weight_ref, decode_ref, far_ref, near_ref,
    ) = held
    pack_any, skip_any, air_any = sources[:3]
    rows = air_ref.shape[0]
    tables, places, fluxes = pl.ds(0, 768), pl.ds(768, 512), pl.ds(0, FC * rows)
    ordered = [
        (pack_any.at[tables], pack_ref.at[tables]),
        (skip_any.at[rows, fluxes], skip_ref.at[rows, fluxes]),
    ]
    for j in range(rows):
        ordered += [(skip_any.at[j], skip_ref.at[j]), (air_any.at[j], air_ref.at[j])]
    ordered.append((pack_any.at[places], pack_ref.at[places]))
    copies = begin(ordered + list(zip(sources, held))[3:], sems)
    after = 2 + 2 * rows
    latitude_rows, longitudes, channels = air_ref.shape
    groups = rows_ref.shape[0]
    pairs = []
    for pair in range(latitude_rows // 2):
        both = rows_ref[:, 16 * pair : 16 * (pair + 1), :].astype(F32)
        pairs.extend([both[:, :8], both[:, 8:]])
    for one in copies[:2]:
        one.wait()
    for j in range(latitude_rows):
        own = pairs[j].reshape(8 * groups, channels).astype(BF16)
        spectral = jnp.dot(pack_ref[384 : 384 + longitudes, : 8 * groups], own, preferred_element_type=F32)
        for one in copies[2 + 2 * j : 4 + 2 * j]:
            one.wait()
        mixed = gelu(spectral + skip_ref[j]).astype(BF16)
        wide = jnp.dot(mixed, pack_ref[:384, :], preferred_element_type=F32)
        updated_ref[j] = air_ref[j].astype(F32) + wide[:, :channels]
        leave = pltpu.make_async_copy(updated_ref.at[j], updated_any.at[j], out_sems.at[j])
        leave.start()
        leaving.append(leave)
        narrow = jnp.concatenate(
            [wide[:, channels:], jnp.zeros((384 - longitudes, 128), F32)], axis=0
        )
        turned = jnp.transpose(narrow)
        extra = jnp.concatenate(
            [
                skip_ref[latitude_rows, FC * j : FC * (j + 1), :longitudes],
                jnp.zeros((FC, 384 - longitudes), F32),
            ],
            axis=1,
        )
        total = turned[:FC] + turned[FC : 2 * FC] + extra
        for part in range(3):
            at = FC * (part * latitude_rows + j)
            flux[at : at + FC, :] = total[:, 128 * part : 128 * (part + 1)]
    for one in copies[after:]:
        one.wait()
    points = flux[...].astype(BF16)
    spread = jnp.concatenate(
        [
            jnp.dot(
                points, pack_ref[768 + at : 896 + at, :], preferred_element_type=F32
            )
            for at in range(0, SPAN // 4, 128)
        ],
        axis=1,
    )
    group = group_ref[...]
    forcing = jnp.zeros((FC, SPAN), F32)
    for at in range(3 * latitude_rows):
        forcing = forcing + jnp.where(group == at, spread[FC * at : FC * (at + 1), :], 0.0)
    masks = tap_masks(SPAN)
    columns = jnp.concatenate(
        [shifted(forcing, tap, masks[q]) for q, tap in enumerate(TAPS)], axis=0
    ).astype(BF16)
    hidden_channels = forcing_weight_ref.shape[0]
    split = far_ref.shape[1]
    partials = []
    for wet_ref, lanes in ((far_ref, slice(0, split)), (near_ref, slice(split, SPAN))):
        hidden = gelu(
            wet_ref[:hidden_channels, :]
            + jnp.dot(forcing_weight_ref[...], columns[:, lanes], preferred_element_type=F32)
        ).astype(BF16)
        partials.append(jnp.dot(decode_ref[...], hidden, preferred_element_type=F32))
    partial = jnp.concatenate(partials, axis=1)
    surface = jnp.concatenate(
        [ref[hidden_channels : hidden_channels + 1, :] for ref in (far_ref, near_ref)], axis=1
    )
    change = jnp.zeros((1, SPAN), F32)
    for q, tap in enumerate(TAPS):
        change = change + shifted(partial[q : q + 1, :], tap, masks[q])
    surface = surface + change
    for slot in range(SLOTS):
        sst[slot : slot + 1, :] = surface[:, CELLS * slot : CELLS * (slot + 1)]
    tiles = sst[...].astype(BF16)
    for member in range(tiles_ref.shape[0]):
        tiles_ref[member] = tiles
    for one in leaving:
        one.wait()


def imprint_kernel(
    updated_any, tiles_ref, cell_any, slot_any, imprint_ref, out_any,
    updated_ref, cell_ref, slot_ref, out_ref, sems, out_sems,
):
    rows, _, channels = updated_ref.shape
    copies = begin(
        [(cell_any, cell_ref), (slot_any, slot_ref)]
        + [(updated_any.at[j], updated_ref.at[j]) for j in range(rows)],
        sems,
    )
    tiles = tiles_ref[0]
    tripled = jnp.concatenate([tiles, tiles, tiles], axis=0)
    pieces = in_three(imprint_ref[...].reshape(1, channels))
    imprint = jnp.concatenate(
        [jnp.broadcast_to(piece, (SLOTS, channels)) for piece in pieces], axis=0
    )
    copies[0].wait()
    copies[1].wait()
    leaving = []
    for j in range(rows):
        picked = lax.dot_general(
            cell_ref[j], tripled, (((1,), (1,)), ((), ())), preferred_element_type=F32
        )
        chosen = picked.astype(BF16) * slot_ref[j]
        warmth = jnp.dot(chosen, imprint, preferred_element_type=F32)
        copies[2 + j].wait()
        out_ref[j] = (updated_ref[j] + warmth).astype(BF16)
        leave = pltpu.make_async_copy(out_ref.at[j], out_any.at[j], out_sems.at[j])
        leave.start()
        leaving.append(leave)
    for one in leaving:
        one.wait()


def mean_kernel(tiles_ref, cell_ref, slot_ref, out_ref):
    members = tiles_ref.shape[0]
    total = jnp.zeros(tiles_ref.shape[1:], F32)
    for member in range(members):
        total = total + tiles_ref[member].astype(F32)
    pieces = jnp.concatenate(in_three(total), axis=0)
    for j in range(cell_ref.shape[0]):
        picked = lax.dot_general(
            pieces, cell_ref[j], (((1,), (1,)), ((), ())), preferred_element_type=F32
        )
        joined = picked[:SLOTS] + picked[SLOTS : 2 * SLOTS] + picked[2 * SLOTS :]
        kept = jnp.where(slot_ref[j] > 0, joined, 0.0)
        out_ref[j : j + 1, :] = jnp.sum(kept, axis=0, keepdims=True) / members


def call(kernel, outs, operands, flops, scratch=(), limit=56, specs=None, out_specs=None):
    size = sum(math.prod(o.shape) * o.dtype.itemsize for o in list(outs) + list(operands))
    return pl.pallas_call(
        kernel,
        out_shape=outs if len(outs) > 1 else outs[0],
        in_specs=specs or [WHOLE] * len(operands),
        out_specs=out_specs or ([WHOLE] * len(outs) if len(outs) > 1 else WHOLE),
        scratch_shapes=list(scratch),
        compiler_params=pltpu.CompilerParams(vmem_limit_bytes=limit * 1024 * 1024),
        cost_estimate=pl.CostEstimate(
            flops=flops, bytes_accessed=min(size, flops), transcendentals=0
        ),
    )(*operands)


def held(operands):
    return [pltpu.VMEM(o.shape, o.dtype) for o in operands]


def shards(
    air_ensemble,
    sea_indicator,
    layernorm_scaling,
    harmonic_damping_factor,
    bypass_factor,
    core_exit_factor,
    air_to_exchange_factor,
    sea_heat_imprint,
    sea_ensemble_arrays,
    input_to_hidden_kernel,
    hidden_to_change_kernel,
    patch_exchange_pick,
    node_sea_pick,
    patch_holder_shift,
    wet_depth_layers,
):
    bands = lax.axis_size("space")
    members = lax.axis_size("member")
    air = air_ensemble[0]
    latitude_rows, longitudes, channels = air.shape
    latitudes = latitude_rows * bands
    hidden_channels = input_to_hidden_kernel.shape[1]
    per_device = MMAX // bands
    chunk = 2 * per_device * latitude_rows
    shape = jax.ShapeDtypeStruct

    analysis, synthesis = (jnp.asarray(t) for t in fourier_tables())
    spectra = call(
        analysis_kernel,
        [shape((bands, chunk, channels), BF16)],
        [air, layernorm_scaling, analysis],
        2 * 2 * MMAX * latitude_rows * longitudes * channels,
        held([air, analysis])
        + [
            pltpu.VMEM((bands, chunk, channels), BF16),
            pltpu.SemaphoreType.DMA((latitude_rows + 1,)),
            pltpu.SemaphoreType.DMA((latitude_rows // 2,)),
        ],
        specs=[FAR, WHOLE, FAR],
        out_specs=FAR,
    )
    gathered = lax.all_to_all(spectra, "space", split_axis=0, concat_axis=0, tiled=True)

    slots = sea_ensemble_arrays[0]
    far = [
        passed_along(slots[offset * CAP : (offset + 1) * CAP], "space", -offset)
        for offset in range(EARLY, NEAR)
    ]
    forward, backward = (jnp.asarray(t) for t in legendre_tables(latitudes))
    first = lax.axis_index("space") * per_device
    forward = lax.dynamic_slice_in_dim(forward, first, per_device, 0)
    backward = lax.dynamic_slice_in_dim(backward, first, per_device, 0)
    offsets = patch_holder_shift[:, 0]
    earlier = jnp.tril(jnp.ones((HOME_DEV, HOME_DEV), jnp.int32), -1)
    positions = jnp.sum((offsets[:, None] == offsets[None, :]).astype(jnp.int32) * earlier, axis=1)
    places = jnp.where(offsets >= EARLY, offsets - EARLY + 1, offsets + NEAR - EARLY)
    targets = jnp.where(offsets == 0, 0, places) * CAP + positions
    selected = targets[None, :] == jnp.arange(SLOTS, dtype=jnp.int32)[:, None]
    depths = jnp.sum(jnp.where(selected, wet_depth_layers[None, :], 0), axis=1)
    kernel = jnp.transpose(input_to_hidden_kernel, (1, 0, 2))
    state_weight = jnp.pad(kernel[:, :, :OCH], ((0, 0), (0, 0), (0, OCH_PAD - OCH))).reshape(
        hidden_channels, -1
    )
    forcing_weight = kernel[:, :, OCH:].reshape(hidden_channels, -1)
    decode_weight = jnp.pad(hidden_to_change_kernel, ((0, 16 - len(TAPS)), (0, 0)))
    picks = jnp.sum(jnp.where(selected[:, :, None], patch_exchange_pick[None], 0), axis=1)
    picks = picks.reshape(1, SPAN)
    line, column = picks // longitudes, picks % longitudes
    group = column // 128 * latitude_rows + line
    place = (column % 128 == jnp.arange(128, dtype=jnp.int32)[:, None]).astype(BF16)
    skip, pack = call(
        local_kernel,
        [shape((latitude_rows + 1, longitudes, channels), F32), shape((1280, 512), BF16)],
        [
            air, layernorm_scaling, bypass_factor, core_exit_factor, air_to_exchange_factor.T,
            synthesis, place,
        ],
        SMALL,
        held([air]) + [pltpu.SemaphoreType.DMA((latitude_rows,))],
        specs=[FAR] + [WHOLE] * 6,
    )
    tile = node_sea_pick // CELLS
    holder = jnp.sum(
        jnp.where(
            tile[:, :, None] == jnp.arange(HOME_DEV, dtype=jnp.int32), targets[None, None, :], 0
        ),
        axis=2,
    )
    holder = jnp.where(sea_indicator > 0, holder, -1)
    cell = (
        (node_sea_pick % CELLS)[:, :, None] == jnp.arange(CELLS, dtype=jnp.int32)
    ).astype(BF16)
    slot_of = (
        holder[:, :, None] == jnp.arange(3 * SLOTS, dtype=jnp.int32) % SLOTS
    ).astype(BF16)
    slot_rows = (
        holder[:, None, :] == jnp.arange(SLOTS, dtype=jnp.int32)[None, :, None]
    ).astype(F32)
    filtered = call(
        legendre_kernel,
        [shape((bands, chunk, channels), BF16)],
        [gathered, forward, backward, harmonic_damping_factor],
        2 * 2 * 2 * per_device * LMAX * latitudes * channels,
        [pltpu.VMEM((channels // 128, bands * chunk, 128), F32)],
        limit=32,
    )
    filtered, late = lax.optimization_barrier((filtered, slots[CAP : EARLY * CAP]))
    returned = lax.all_to_all(filtered, "space", split_axis=0, concat_axis=0, tiled=True)
    near = [
        passed_along(late[at : at + CAP], "space", -(1 + at // CAP))
        for at in range(0, late.shape[0], CAP)
    ]
    def wet(first, parts):
        width = CAP * CELLS * len(parts)
        return call(
            functools.partial(ocean_kernel, first),
            [shape((hidden_channels + 8, width), F32)],
            [depths, *parts, state_weight],
            SMALL,
            [pltpu.VMEM((len(TAPS) * OCH_PAD, width), BF16)],
            limit=32,
            specs=[pl.BlockSpec(memory_space=pltpu.SMEM)] + [WHOLE] * (len(parts) + 1),
        )

    wet_far = wet(0, [slots[:CAP], *far])
    wet_near = wet(CAP * (len(far) + 1), near)
    operands = [pack, skip, air, group, forcing_weight, decode_weight, wet_far, wet_near]
    updated, tiles = call(
        surface_kernel,
        [shape(air.shape, F32), shape((members, SLOTS, CELLS), BF16)],
        [returned] + operands,
        2 * latitude_rows * longitudes * channels * (channels + 2 * MMAX),
        held(operands)
        + [
            pltpu.VMEM(air.shape, F32),
            pltpu.VMEM((3 * FC * latitude_rows, 128), F32),
            pltpu.VMEM((SLOTS, CELLS), F32),
            pltpu.SemaphoreType.DMA((len(operands) + 2 * latitude_rows + 1,)),
            pltpu.SemaphoreType.DMA((latitude_rows,)),
        ],
        limit=52,
        specs=[WHOLE] + [FAR] * len(operands),
        out_specs=[FAR, WHOLE],
    )
    everyone = lax.all_to_all(tiles, "member", split_axis=0, concat_axis=0, tiled=True)
    out = call(
        imprint_kernel,
        [shape(air.shape, BF16)],
        [updated, tiles, cell, slot_of, sea_heat_imprint],
        2 * latitude_rows * longitudes * channels * 256,
        held([updated, cell, slot_of, air])
        + [
            pltpu.SemaphoreType.DMA((latitude_rows + 2,)),
            pltpu.SemaphoreType.DMA((latitude_rows,)),
        ],
        specs=[FAR, WHOLE, FAR, FAR, WHOLE],
        out_specs=FAR,
    )
    mean = call(
        mean_kernel,
        [shape((latitude_rows, longitudes), F32)],
        [everyone, cell, slot_rows],
        2 * 3 * SLOTS * CELLS * latitude_rows * longitudes,
        limit=32,
    )
    return (out[None], mean)


def solution(mesh):
    in_specs = (
        P("member", "space", None, None),
        P("space", None),
        P(),
        P(),
        P(),
        P(),
        P(),
        P(),
        P("member", "space", None, None),
        P(),
        P(),
        P("space", None),
        P("space", None),
        P("space", None),
        P("space"),
    )
    out_specs = (P("member", "space", None, None), P("space", None))
    return jax.shard_map(shards, mesh=mesh, in_specs=in_specs, out_specs=out_specs, check_vma=False)
```

```python
import functools
import math

import jax
import jax.numpy as jnp
import numpy as np
from jax import lax
from jax.experimental import pallas as pl
from jax.experimental.pallas import tpu as pltpu
from jax.sharding import PartitionSpec as P

MERIDIAN_TOTAL = 360
MMAX = 128
LMAX = 128
FC = 8
LEV = 19
CAP = 2
NEAR = 8
HOME_DEV = 14
SLOTS = NEAR * CAP
CELLS = 128
SPAN = SLOTS * CELLS
OCH = 76
OCH_PAD = 80
TAPS = [(row, col) for row in (-1, 0, 1) for col in (-1, 0, 1)]
EARLY = 3
SMALL = 1024
BF16 = jnp.bfloat16
F32 = jnp.float32
WHOLE = pl.BlockSpec(memory_space=pltpu.VMEM)
FAR = pl.BlockSpec(memory_space=pltpu.HBM)


def passed_along(value, axis, by):
    devices = lax.axis_size(axis)
    return lax.ppermute(value, axis, [(i, (i + by) % devices) for i in range(devices)])


def fourier_tables():
    product = np.arange(MMAX)[:, None] * np.arange(MERIDIAN_TOTAL)[None, :] % MERIDIAN_TOTAL
    angles = 2.0 * np.pi / MERIDIAN_TOTAL * product
    analysis = np.stack([np.cos(angles), -np.sin(angles)], axis=1) / MERIDIAN_TOTAL
    weights = np.where(np.arange(MMAX) == 0, 1.0, 2.0)[:, None]
    synthesis = np.stack([weights * np.cos(angles), -weights * np.sin(angles)], axis=1)
    return (
        analysis.reshape(2 * MMAX, MERIDIAN_TOTAL).astype(BF16),
        synthesis.reshape(2 * MMAX, MERIDIAN_TOTAL).T.astype(BF16),
    )


def legendre_tables(latitudes):
    theta = np.pi / latitudes * (np.arange(latitudes) + 0.5)
    cosine = np.cos(theta)[None, :]
    sine = np.sin(theta)
    counter = np.arange(1, MMAX)
    totals = np.concatenate([[0.0], np.cumsum(np.log((2.0 * counter - 1.0) / (2.0 * counter)))])
    order = np.arange(MMAX, dtype=np.float64)[:, None]
    diagonal = np.exp(
        0.5 * (np.log((2.0 * order + 1.0) / (4.0 * np.pi)) + totals[:, None])
        + order * np.log(sine)[None, :]
    )
    values = np.zeros((MMAX, LMAX, latitudes))
    latest = np.zeros((MMAX, latitudes))
    before = np.zeros((MMAX, latitudes))
    for degree in range(LMAX):
        lowered = (degree - 1.0) ** 2
        upward = np.sqrt(
            max(4.0 * degree * degree - 1.0, 0.0) / np.maximum(degree * degree - order * order, 1.0)
        )
        damping = np.sqrt(
            np.maximum(lowered - order * order, 0.0) / max(4.0 * lowered - 1.0, 1.0)
        )
        current = upward * (cosine * latest - damping * before)
        current = np.where(degree == order, diagonal, current)
        current = np.where(degree < order, 0.0, current)
        values[:, degree, :] = current
        latest, before = current, latest
    quadrature = 2.0 * np.pi * np.pi / latitudes * sine
    forward = (values * quadrature[None, None, :]).astype(BF16)
    backward = np.transpose(values, (0, 2, 1)).astype(BF16)
    return forward, backward


def gelu(x):
    scale = math.sqrt(2.0 / math.pi)
    inner = x * (scale + (0.044715 * scale) * (x * x))
    half = 0.5 * x
    return half * jnp.tanh(inner) + half


def tap_masks(width):
    lane = lax.broadcasted_iota(jnp.int32, (1, width), 1) % CELLS
    row, col = lane // 16, lane % 16
    masks = []
    for down, right in TAPS:
        inside = (row + down >= 0) & (row + down < 8) & (col + right >= 0) & (col + right < 16)
        masks.append(inside)
    return masks


def shifted(x, tap, mask):
    by = 16 * tap[0] + tap[1]
    if by == 0:
        return x
    rolled = pltpu.roll(x, (-by) % x.shape[1], 1)
    return jnp.where(mask, rolled, 0.0)


def in_three(x):
    high = x.astype(BF16)
    rest = x - high.astype(F32)
    middle = rest.astype(BF16)
    return high, middle, (rest - middle.astype(F32)).astype(BF16)


def begin(copies, sems):
    started = [
        pltpu.make_async_copy(source, target, sems.at[i])
        for i, (source, target) in enumerate(copies)
    ]
    for one in started:
        one.start()
    return started


def normalised(x, scale):
    centered = x - jnp.mean(x, axis=-1, keepdims=True)
    spread = jnp.mean(centered * centered, axis=-1, keepdims=True)
    return (centered * lax.rsqrt(spread + 1e-05) * scale).astype(BF16)


def analysis_kernel(
    air_any, scale_ref, table_any, spectra_any, air_ref, table_ref, spectra_ref, sems, out_sems
):
    rows = air_ref.shape[0]
    leaving = []
    groups = spectra_ref.shape[0]
    copies = begin(
        [(air_any.at[j], air_ref.at[j]) for j in range(rows)] + [(table_any, table_ref)], sems
    )
    scale = scale_ref[...].reshape(1, scale_ref.shape[0])
    for pair in range(rows // 2):
        both = []
        for j in (2 * pair, 2 * pair + 1):
            copies[j].wait()
            normed = normalised(air_ref[j].astype(F32), scale)
            if j == 0:
                copies[rows].wait()
            out = jnp.dot(table_ref[...], normed, preferred_element_type=F32)
            both.append(out.reshape(groups, 8, out.shape[1]))
        block = jnp.concatenate(both, axis=1)
        rows_16 = slice(16 * pair, 16 * (pair + 1))
        spectra_ref[:, rows_16, :] = block.astype(BF16)
        leave = pltpu.make_async_copy(
            spectra_ref.at[:, rows_16], spectra_any.at[:, rows_16], out_sems.at[pair]
        )
        leave.start()
        leaving.append(leave)
    for one in leaving:
        one.wait()


def local_kernel(
    air_any, scale_ref, bypass_ref, exit_ref, exchange_ref, synthesis_ref, place_ref,
    skip_ref, pack_ref, air_ref, sems,
):
    rows = air_ref.shape[0]
    copies = begin([(air_any.at[j], air_ref.at[j]) for j in range(rows)], sems)
    scale = scale_ref[...].reshape(1, scale_ref.shape[0])
    channels = exit_ref.shape[0]
    dims = (((1,), (1,)), ((), ()))
    through = lax.dot_general(
        exit_ref[...], exchange_ref[...], dims, preferred_element_type=F32
    )
    high = through.astype(BF16)
    low = (through - high.astype(F32)).astype(BF16)
    pack_ref[:384, :channels] = exit_ref[...]
    pack_ref[:384, channels:] = jnp.concatenate(
        [high.astype(F32), low.astype(F32), jnp.zeros((channels, 128 - 2 * FC), F32)], axis=1
    ).astype(BF16)
    pack_ref[384:768, :] = jnp.zeros((384, 512), BF16)
    longitudes, orders = synthesis_ref.shape
    pack_ref[384 : 384 + longitudes, :orders] = synthesis_ref[...]
    for block in range(SPAN // 512):
        pack_ref[768 + 128 * block : 896 + 128 * block, :] = place_ref[
            :, 512 * block : 512 * (block + 1)
        ]
    for j in range(rows):
        copies[j].wait()
        own = air_ref[j]
        normed = normalised(own.astype(F32), scale)
        skip_ref[j] = jnp.dot(normed, bypass_ref[...], preferred_element_type=F32)
        skip_ref[rows, FC * j : FC * (j + 1), :longitudes] = lax.dot_general(
            exchange_ref[...], own, dims, preferred_element_type=F32
        )


def legendre_kernel(
    x_ref, forward_ref, backward_ref, gains_ref, out_any, work, out_ref, out_sems
):
    groups, chunk, channels = x_ref.shape
    leaving = []
    total = groups * chunk
    latitudes = total // 8
    for third in range(channels // 128):
        lanes = slice(128 * third, 128 * (third + 1))
        work[third] = x_ref[:, :, lanes].astype(F32).reshape(total, 128)
        gains = gains_ref[:, lanes]
        gains = jnp.concatenate([gains, gains], axis=1)
        for m in range(4):
            real, imaginary = (pl.ds(2 * m + r, latitudes, stride=8) for r in (0, 1))
            own = jnp.concatenate(
                [work[third, real, :], work[third, imaginary, :]], axis=1
            ).astype(BF16)
            coefficients = jnp.dot(forward_ref[m], own, preferred_element_type=F32)
            shaped = (coefficients * gains).astype(BF16)
            back = jnp.dot(backward_ref[m], shaped, preferred_element_type=F32)
            work[third, real, :] = back[:, :128]
            work[third, imaginary, :] = back[:, 128:]
        out_ref[:, :, lanes] = work[third].reshape(groups, chunk, 128).astype(BF16)
        leave = pltpu.make_async_copy(
            out_ref.at[:, :, lanes], out_any.at[:, :, lanes], out_sems.at[third]
        )
        leave.start()
        leaving.append(leave)
    for one in leaving:
        one.wait()


def ocean_kernel(first, depth_ref, *refs):
    pieces, (weight_ref, out_ref, columns) = refs[:-3], refs[-3:]
    masks = tap_masks(CELLS)
    level = lax.broadcasted_iota(jnp.int32, (OCH, CELLS), 0) % LEV
    hidden_channels = weight_ref.shape[0]
    for slot in range(CAP * len(pieces)):
        lanes = slice(CELLS * slot, CELLS * (slot + 1))
        state = pieces[slot // CAP][slot % CAP].astype(F32)
        out_ref[hidden_channels:, lanes] = jnp.broadcast_to(state[0:1], (8, CELLS))
        state = jnp.where(level < depth_ref[first + slot], state, 0.0)
        state = jnp.concatenate([state, jnp.zeros((OCH_PAD - OCH, CELLS), F32)], axis=0)
        for q, tap in enumerate(TAPS):
            moved = shifted(state, tap, masks[q]).astype(BF16)
            columns[OCH_PAD * q : OCH_PAD * (q + 1), lanes] = moved
    for at in range(0, out_ref.shape[1], 512):
        out_ref[:hidden_channels, at : at + 512] = jnp.dot(
            weight_ref[...], columns[:, at : at + 512], preferred_element_type=F32
        )


def surface_kernel(rows_ref, *refs):
    count = 8
    sources, (updated_any, tiles_ref), held, (updated_ref, flux, sst, sems, out_sems) = (
        refs[:count], refs[count : count + 2], refs[count + 2 : 2 * count + 2],
        refs[2 * count + 2 :],
    )
    leaving = []
    (
        pack_ref, skip_ref, air_ref, group_ref, forcing_weight_ref, decode_ref, far_ref, near_ref,
    ) = held
    pack_any, skip_any, air_any = sources[:3]
    rows = air_ref.shape[0]
    places, fluxes = pl.ds(768, 512), pl.ds(0, FC * rows)
    leaves, enters = pl.ds(0, 384), pl.ds(384, 384)
    ordered = [(pack_any.at[enters], pack_ref.at[enters])]
    for j in range(rows):
        ordered += [(skip_any.at[j], skip_ref.at[j]), (air_any.at[j], air_ref.at[j])]
        if j == 0:
            ordered += [
                (pack_any.at[leaves], pack_ref.at[leaves]),
                (skip_any.at[rows, fluxes], skip_ref.at[rows, fluxes]),
            ]
    ordered.append((pack_any.at[places], pack_ref.at[places]))
    copies = begin(ordered + list(zip(sources, held))[3:], sems)
    after = 3 + 2 * rows
    latitude_rows, longitudes, channels = air_ref.shape
    groups = rows_ref.shape[0]
    pairs = []
    for pair in range(latitude_rows // 2):
        both = rows_ref[:, 16 * pair : 16 * (pair + 1), :].astype(F32)
        pairs.extend([both[:, :8], both[:, 8:]])
    copies[0].wait()
    for j in range(latitude_rows):
        own = pairs[j].reshape(8 * groups, channels).astype(BF16)
        spectral = jnp.dot(pack_ref[384 : 384 + longitudes, : 8 * groups], own, preferred_element_type=F32)
        for one in copies[1:5] if j == 0 else copies[3 + 2 * j : 5 + 2 * j]:
            one.wait()
        mixed = gelu(spectral + skip_ref[j]).astype(BF16)
        wide = jnp.dot(mixed, pack_ref[:384, :], preferred_element_type=F32)
        updated_ref[j] = air_ref[j].astype(F32) + wide[:, :channels]
        leave = pltpu.make_async_copy(updated_ref.at[j], updated_any.at[j], out_sems.at[j])
        leave.start()
        leaving.append(leave)
        narrow = jnp.concatenate(
            [wide[:, channels:], jnp.zeros((384 - longitudes, 128), F32)], axis=0
        )
        turned = jnp.transpose(narrow)
        extra = jnp.concatenate(
            [
                skip_ref[latitude_rows, FC * j : FC * (j + 1), :longitudes],
                jnp.zeros((FC, 384 - longitudes), F32),
            ],
            axis=1,
        )
        total = turned[:FC] + turned[FC : 2 * FC] + extra
        for part in range(3):
            at = FC * (part * latitude_rows + j)
            flux[at : at + FC, :] = total[:, 128 * part : 128 * (part + 1)]
    for one in copies[after:]:
        one.wait()
    points = flux[...].astype(BF16)
    spread = jnp.concatenate(
        [
            jnp.dot(
                points, pack_ref[768 + at : 896 + at, :], preferred_element_type=F32
            )
            for at in range(0, SPAN // 4, 128)
        ],
        axis=1,
    )
    group = group_ref[...]
    forcing = jnp.zeros((FC, SPAN), F32)
    for at in range(3 * latitude_rows):
        forcing = forcing + jnp.where(group == at, spread[FC * at : FC * (at + 1), :], 0.0)
    masks = tap_masks(SPAN)
    columns = jnp.concatenate(
        [shifted(forcing, tap, masks[q]) for q, tap in enumerate(TAPS)], axis=0
    ).astype(BF16)
    hidden_channels = forcing_weight_ref.shape[0]
    split = far_ref.shape[1]
    partials = []
    for wet_ref, lanes in ((far_ref, slice(0, split)), (near_ref, slice(split, SPAN))):
        hidden = gelu(
            wet_ref[:hidden_channels, :]
            + jnp.dot(forcing_weight_ref[...], columns[:, lanes], preferred_element_type=F32)
        ).astype(BF16)
        partials.append(jnp.dot(decode_ref[...], hidden, preferred_element_type=F32))
    partial = jnp.concatenate(partials, axis=1)
    surface = jnp.concatenate(
        [ref[hidden_channels : hidden_channels + 1, :] for ref in (far_ref, near_ref)], axis=1
    )
    change = jnp.zeros((1, SPAN), F32)
    for q, tap in enumerate(TAPS):
        change = change + shifted(partial[q : q + 1, :], tap, masks[q])
    surface = surface + change
    for slot in range(SLOTS):
        sst[slot : slot + 1, :] = surface[:, CELLS * slot : CELLS * (slot + 1)]
    tiles = sst[...].astype(BF16)
    for member in range(tiles_ref.shape[0]):
        tiles_ref[member] = tiles
    for one in leaving:
        one.wait()


def imprint_kernel(
    updated_any, tiles_ref, cell_any, slot_any, imprint_ref, out_any,
    updated_ref, cell_ref, slot_ref, out_ref, sems, out_sems,
):
    rows, _, channels = updated_ref.shape
    copies = begin(
        [(cell_any, cell_ref), (slot_any, slot_ref)]
        + [(updated_any.at[j], updated_ref.at[j]) for j in range(rows)],
        sems,
    )
    tiles = tiles_ref[0]
    tripled = jnp.concatenate([tiles, tiles, tiles], axis=0)
    pieces = in_three(imprint_ref[...].reshape(1, channels))
    imprint = jnp.concatenate(
        [jnp.broadcast_to(piece, (SLOTS, channels)) for piece in pieces], axis=0
    )
    copies[0].wait()
    copies[1].wait()
    leaving = []
    for j in range(rows):
        picked = lax.dot_general(
            cell_ref[j], tripled, (((1,), (1,)), ((), ())), preferred_element_type=F32
        )
        chosen = picked.astype(BF16) * slot_ref[j]
        warmth = jnp.dot(chosen, imprint, preferred_element_type=F32)
        copies[2 + j].wait()
        out_ref[j] = (updated_ref[j] + warmth).astype(BF16)
        leave = pltpu.make_async_copy(out_ref.at[j], out_any.at[j], out_sems.at[j])
        leave.start()
        leaving.append(leave)
    for one in leaving:
        one.wait()


def mean_kernel(tiles_ref, cell_ref, slot_ref, out_ref):
    members = tiles_ref.shape[0]
    total = jnp.zeros(tiles_ref.shape[1:], F32)
    for member in range(members):
        total = total + tiles_ref[member].astype(F32)
    pieces = jnp.concatenate(in_three(total), axis=0)
    for j in range(cell_ref.shape[0]):
        picked = lax.dot_general(
            pieces, cell_ref[j], (((1,), (1,)), ((), ())), preferred_element_type=F32
        )
        joined = picked[:SLOTS] + picked[SLOTS : 2 * SLOTS] + picked[2 * SLOTS :]
        kept = jnp.where(slot_ref[j] > 0, joined, 0.0)
        out_ref[j : j + 1, :] = jnp.sum(kept, axis=0, keepdims=True) / members


def call(kernel, outs, operands, flops, scratch=(), limit=56, specs=None, out_specs=None):
    size = sum(math.prod(o.shape) * o.dtype.itemsize for o in list(outs) + list(operands))
    return pl.pallas_call(
        kernel,
        out_shape=outs if len(outs) > 1 else outs[0],
        in_specs=specs or [WHOLE] * len(operands),
        out_specs=out_specs or ([WHOLE] * len(outs) if len(outs) > 1 else WHOLE),
        scratch_shapes=list(scratch),
        compiler_params=pltpu.CompilerParams(vmem_limit_bytes=limit * 1024 * 1024),
        cost_estimate=pl.CostEstimate(
            flops=flops, bytes_accessed=min(size, flops), transcendentals=0
        ),
    )(*operands)


def held(operands):
    return [pltpu.VMEM(o.shape, o.dtype) for o in operands]


def shards(
    air_ensemble,
    sea_indicator,
    layernorm_scaling,
    harmonic_damping_factor,
    bypass_factor,
    core_exit_factor,
    air_to_exchange_factor,
    sea_heat_imprint,
    sea_ensemble_arrays,
    input_to_hidden_kernel,
    hidden_to_change_kernel,
    patch_exchange_pick,
    node_sea_pick,
    patch_holder_shift,
    wet_depth_layers,
):
    bands = lax.axis_size("space")
    members = lax.axis_size("member")
    air = air_ensemble[0]
    latitude_rows, longitudes, channels = air.shape
    latitudes = latitude_rows * bands
    hidden_channels = input_to_hidden_kernel.shape[1]
    per_device = MMAX // bands
    chunk = 2 * per_device * latitude_rows
    shape = jax.ShapeDtypeStruct

    analysis, synthesis = (jnp.asarray(t) for t in fourier_tables())
    spectra = call(
        analysis_kernel,
        [shape((bands, chunk, channels), BF16)],
        [air, layernorm_scaling, analysis],
        2 * 2 * MMAX * latitude_rows * longitudes * channels,
        held([air, analysis])
        + [
            pltpu.VMEM((bands, chunk, channels), BF16),
            pltpu.SemaphoreType.DMA((latitude_rows + 1,)),
            pltpu.SemaphoreType.DMA((latitude_rows // 2,)),
        ],
        specs=[FAR, WHOLE, FAR],
        out_specs=FAR,
    )
    gathered = lax.all_to_all(spectra, "space", split_axis=0, concat_axis=0, tiled=True)

    slots = sea_ensemble_arrays[0]
    far = [
        passed_along(slots[offset * CAP : (offset + 1) * CAP], "space", -offset)
        for offset in range(EARLY, NEAR)
    ]
    forward, backward = (jnp.asarray(t) for t in legendre_tables(latitudes))
    first = lax.axis_index("space") * per_device
    forward = lax.dynamic_slice_in_dim(forward, first, per_device, 0)
    backward = lax.dynamic_slice_in_dim(backward, first, per_device, 0)
    offsets = patch_holder_shift[:, 0]
    earlier = jnp.tril(jnp.ones((HOME_DEV, HOME_DEV), jnp.int32), -1)
    positions = jnp.sum((offsets[:, None] == offsets[None, :]).astype(jnp.int32) * earlier, axis=1)
    places = jnp.where(offsets >= EARLY, offsets - EARLY + 1, offsets + NEAR - EARLY)
    targets = jnp.where(offsets == 0, 0, places) * CAP + positions
    selected = targets[None, :] == jnp.arange(SLOTS, dtype=jnp.int32)[:, None]
    depths = jnp.sum(jnp.where(selected, wet_depth_layers[None, :], 0), axis=1)
    kernel = jnp.transpose(input_to_hidden_kernel, (1, 0, 2))
    state_weight = jnp.pad(kernel[:, :, :OCH], ((0, 0), (0, 0), (0, OCH_PAD - OCH))).reshape(
        hidden_channels, -1
    )
    forcing_weight = kernel[:, :, OCH:].reshape(hidden_channels, -1)
    decode_weight = jnp.pad(hidden_to_change_kernel, ((0, 16 - len(TAPS)), (0, 0)))
    picks = jnp.sum(jnp.where(selected[:, :, None], patch_exchange_pick[None], 0), axis=1)
    picks = picks.reshape(1, SPAN)
    line, column = picks // longitudes, picks % longitudes
    group = column // 128 * latitude_rows + line
    place = (column % 128 == jnp.arange(128, dtype=jnp.int32)[:, None]).astype(BF16)
    skip, pack = call(
        local_kernel,
        [shape((latitude_rows + 1, longitudes, channels), F32), shape((1280, 512), BF16)],
        [
            air, layernorm_scaling, bypass_factor, core_exit_factor, air_to_exchange_factor.T,
            synthesis, place,
        ],
        SMALL,
        held([air]) + [pltpu.SemaphoreType.DMA((latitude_rows,))],
        specs=[FAR] + [WHOLE] * 6,
    )
    tile = node_sea_pick // CELLS
    holder = jnp.sum(
        jnp.where(
            tile[:, :, None] == jnp.arange(HOME_DEV, dtype=jnp.int32), targets[None, None, :], 0
        ),
        axis=2,
    )
    holder = jnp.where(sea_indicator > 0, holder, -1)
    cell = (
        (node_sea_pick % CELLS)[:, :, None] == jnp.arange(CELLS, dtype=jnp.int32)
    ).astype(BF16)
    slot_of = (
        holder[:, :, None] == jnp.arange(3 * SLOTS, dtype=jnp.int32) % SLOTS
    ).astype(BF16)
    slot_rows = (
        holder[:, None, :] == jnp.arange(SLOTS, dtype=jnp.int32)[None, :, None]
    ).astype(F32)
    filtered = call(
        legendre_kernel,
        [shape((bands, chunk, channels), BF16)],
        [gathered, forward, backward, harmonic_damping_factor],
        2 * 2 * 2 * per_device * LMAX * latitudes * channels,
        [
            pltpu.VMEM((channels // 128, bands * chunk, 128), F32),
            pltpu.VMEM((bands, chunk, channels), BF16),
            pltpu.SemaphoreType.DMA((channels // 128,)),
        ],
        limit=32,
        out_specs=FAR,
    )
    filtered, late = lax.optimization_barrier((filtered, slots[CAP : EARLY * CAP]))
    returned = lax.all_to_all(filtered, "space", split_axis=0, concat_axis=0, tiled=True)
    near = [
        passed_along(late[at : at + CAP], "space", -(1 + at // CAP))
        for at in range(0, late.shape[0], CAP)
    ]
    def wet(first, parts):
        width = CAP * CELLS * len(parts)
        return call(
            functools.partial(ocean_kernel, first),
            [shape((hidden_channels + 8, width), F32)],
            [depths, *parts, state_weight],
            SMALL,
            [pltpu.VMEM((len(TAPS) * OCH_PAD, width), BF16)],
            limit=32,
            specs=[pl.BlockSpec(memory_space=pltpu.SMEM)] + [WHOLE] * (len(parts) + 1),
        )

    wet_far = wet(0, [slots[:CAP], *far])
    wet_near = wet(CAP * (len(far) + 1), near)
    operands = [pack, skip, air, group, forcing_weight, decode_weight, wet_far, wet_near]
    updated, tiles = call(
        surface_kernel,
        [shape(air.shape, F32), shape((members, SLOTS, CELLS), BF16)],
        [returned] + operands,
        2 * latitude_rows * longitudes * channels * (channels + 2 * MMAX),
        held(operands)
        + [
            pltpu.VMEM(air.shape, F32),
            pltpu.VMEM((3 * FC * latitude_rows, 128), F32),
            pltpu.VMEM((SLOTS, CELLS), F32),
            pltpu.SemaphoreType.DMA((len(operands) + 2 * latitude_rows + 1,)),
            pltpu.SemaphoreType.DMA((latitude_rows,)),
        ],
        limit=52,
        specs=[WHOLE] + [FAR] * len(operands),
        out_specs=[FAR, WHOLE],
    )
    everyone = lax.all_to_all(tiles, "member", split_axis=0, concat_axis=0, tiled=True)
    out = call(
        imprint_kernel,
        [shape(air.shape, BF16)],
        [updated, tiles, cell, slot_of, sea_heat_imprint],
        2 * latitude_rows * longitudes * channels * 256,
        held([updated, cell, slot_of, air])
        + [
            pltpu.SemaphoreType.DMA((latitude_rows + 2,)),
            pltpu.SemaphoreType.DMA((latitude_rows,)),
        ],
        specs=[FAR, WHOLE, FAR, FAR, WHOLE],
        out_specs=FAR,
    )
    mean = call(
        mean_kernel,
        [shape((latitude_rows, longitudes), F32)],
        [everyone, cell, slot_rows],
        2 * 3 * SLOTS * CELLS * latitude_rows * longitudes,
        limit=32,
    )
    return (out[None], mean)


def solution(mesh):
    in_specs = (
        P("member", "space", None, None),
        P("space", None),
        P(),
        P(),
        P(),
        P(),
        P(),
        P(),
        P("member", "space", None, None),
        P(),
        P(),
        P("space", None),
        P("space", None),
        P("space", None),
        P("space"),
    )
    out_specs = (P("member", "space", None, None), P("space", None))
    return jax.shard_map(shards, mesh=mesh, in_specs=in_specs, out_specs=out_specs, check_vma=False)
```

```python
import functools
import math

import jax
import jax.numpy as jnp
import numpy as np
from jax import lax
from jax.experimental import pallas as pl
from jax.experimental.pallas import tpu as pltpu
from jax.sharding import PartitionSpec as P

MERIDIAN_TOTAL = 360
MMAX = 128
LMAX = 128
FC = 8
LEV = 19
CAP = 2
NEAR = 8
HOME_DEV = 14
SLOTS = NEAR * CAP
CELLS = 128
SPAN = SLOTS * CELLS
OCH = 76
OCH_PAD = 80
TAPS = [(row, col) for row in (-1, 0, 1) for col in (-1, 0, 1)]
EARLY = 4
SMALL = 1024
BF16 = jnp.bfloat16
F32 = jnp.float32
WHOLE = pl.BlockSpec(memory_space=pltpu.VMEM)
FAR = pl.BlockSpec(memory_space=pltpu.HBM)


def passed_along(value, axis, by):
    devices = lax.axis_size(axis)
    return lax.ppermute(value, axis, [(i, (i + by) % devices) for i in range(devices)])


def fourier_tables():
    product = np.arange(MMAX)[:, None] * np.arange(MERIDIAN_TOTAL)[None, :] % MERIDIAN_TOTAL
    angles = 2.0 * np.pi / MERIDIAN_TOTAL * product
    analysis = np.stack([np.cos(angles), -np.sin(angles)], axis=1) / MERIDIAN_TOTAL
    weights = np.where(np.arange(MMAX) == 0, 1.0, 2.0)[:, None]
    synthesis = np.stack([weights * np.cos(angles), -weights * np.sin(angles)], axis=1)
    return (
        analysis.reshape(2 * MMAX, MERIDIAN_TOTAL).astype(BF16),
        synthesis.reshape(2 * MMAX, MERIDIAN_TOTAL).T.astype(BF16),
    )


def legendre_tables(latitudes):
    theta = np.pi / latitudes * (np.arange(latitudes) + 0.5)
    cosine = np.cos(theta)[None, :]
    sine = np.sin(theta)
    counter = np.arange(1, MMAX)
    totals = np.concatenate([[0.0], np.cumsum(np.log((2.0 * counter - 1.0) / (2.0 * counter)))])
    order = np.arange(MMAX, dtype=np.float64)[:, None]
    diagonal = np.exp(
        0.5 * (np.log((2.0 * order + 1.0) / (4.0 * np.pi)) + totals[:, None])
        + order * np.log(sine)[None, :]
    )
    values = np.zeros((MMAX, LMAX, latitudes))
    latest = np.zeros((MMAX, latitudes))
    before = np.zeros((MMAX, latitudes))
    for degree in range(LMAX):
        lowered = (degree - 1.0) ** 2
        upward = np.sqrt(
            max(4.0 * degree * degree - 1.0, 0.0) / np.maximum(degree * degree - order * order, 1.0)
        )
        damping = np.sqrt(
            np.maximum(lowered - order * order, 0.0) / max(4.0 * lowered - 1.0, 1.0)
        )
        current = upward * (cosine * latest - damping * before)
        current = np.where(degree == order, diagonal, current)
        current = np.where(degree < order, 0.0, current)
        values[:, degree, :] = current
        latest, before = current, latest
    quadrature = 2.0 * np.pi * np.pi / latitudes * sine
    forward = (values * quadrature[None, None, :]).astype(BF16)
    backward = np.transpose(values, (0, 2, 1)).astype(BF16)
    return forward, backward


def gelu(x):
    inner = math.sqrt(2.0 / math.pi) * (x + 0.044715 * (x * x * x))
    return 0.5 * x * (1.0 + jnp.tanh(inner))


def tap_masks(width):
    lane = lax.broadcasted_iota(jnp.int32, (1, width), 1) % CELLS
    row, col = lane // 16, lane % 16
    masks = []
    for down, right in TAPS:
        inside = (row + down >= 0) & (row + down < 8) & (col + right >= 0) & (col + right < 16)
        masks.append(inside)
    return masks


def shifted(x, tap, mask):
    by = 16 * tap[0] + tap[1]
    if by == 0:
        return x
    rolled = pltpu.roll(x, (-by) % x.shape[1], 1)
    return jnp.where(mask, rolled, 0.0)


def in_three(x):
    high = x.astype(BF16)
    rest = x - high.astype(F32)
    middle = rest.astype(BF16)
    return high, middle, (rest - middle.astype(F32)).astype(BF16)


def begin(copies, sems):
    started = [
        pltpu.make_async_copy(source, target, sems.at[i])
        for i, (source, target) in enumerate(copies)
    ]
    for one in started:
        one.start()
    return started


def normalised(x, scale):
    centered = x - jnp.mean(x, axis=-1, keepdims=True)
    spread = jnp.mean(centered * centered, axis=-1, keepdims=True)
    return (centered * lax.rsqrt(spread + 1e-05) * scale).astype(BF16)


def analysis_kernel(
    air_any, scale_ref, table_any, spectra_any, air_ref, table_ref, spectra_ref, sems, out_sems
):
    rows = air_ref.shape[0]
    leaving = []
    groups = spectra_ref.shape[0]
    copies = begin(
        [(air_any.at[j], air_ref.at[j]) for j in range(rows)] + [(table_any, table_ref)], sems
    )
    scale = scale_ref[...].reshape(1, scale_ref.shape[0])
    for pair in range(rows // 2):
        both = []
        for j in (2 * pair, 2 * pair + 1):
            copies[j].wait()
            normed = normalised(air_ref[j].astype(F32), scale)
            if j == 0:
                copies[rows].wait()
            out = jnp.dot(table_ref[...], normed, preferred_element_type=F32)
            both.append(out.reshape(groups, 8, out.shape[1]))
        block = jnp.concatenate(both, axis=1)
        rows_16 = slice(16 * pair, 16 * (pair + 1))
        spectra_ref[:, rows_16, :] = block.astype(BF16)
        leave = pltpu.make_async_copy(
            spectra_ref.at[:, rows_16], spectra_any.at[:, rows_16], out_sems.at[pair]
        )
        leave.start()
        leaving.append(leave)
    for one in leaving:
        one.wait()


def local_kernel(
    air_any, scale_ref, bypass_ref, exit_ref, exchange_ref, synthesis_ref, place_ref,
    skip_ref, pack_ref, air_ref, sems,
):
    rows = air_ref.shape[0]
    copies = begin([(air_any.at[j], air_ref.at[j]) for j in range(rows)], sems)
    scale = scale_ref[...].reshape(1, scale_ref.shape[0])
    channels = exit_ref.shape[0]
    dims = (((1,), (1,)), ((), ()))
    through = lax.dot_general(
        exit_ref[...], exchange_ref[...], dims, preferred_element_type=F32
    )
    high = through.astype(BF16)
    low = (through - high.astype(F32)).astype(BF16)
    pack_ref[:384, :channels] = exit_ref[...]
    pack_ref[:384, channels:] = jnp.concatenate(
        [high.astype(F32), low.astype(F32), jnp.zeros((channels, 128 - 2 * FC), F32)], axis=1
    ).astype(BF16)
    pack_ref[384:768, :] = jnp.zeros((384, 512), BF16)
    longitudes, orders = synthesis_ref.shape
    pack_ref[384 : 384 + longitudes, :orders] = synthesis_ref[...]
    for block in range(SPAN // 512):
        pack_ref[768 + 128 * block : 896 + 128 * block, :] = place_ref[
            :, 512 * block : 512 * (block + 1)
        ]
    for j in range(rows):
        copies[j].wait()
        own = air_ref[j]
        normed = normalised(own.astype(F32), scale)
        skip_ref[j] = jnp.dot(normed, bypass_ref[...], preferred_element_type=F32)
        skip_ref[rows, FC * j : FC * (j + 1), :longitudes] = lax.dot_general(
            exchange_ref[...], own, dims, preferred_element_type=F32
        )


def legendre_kernel(x_ref, forward_ref, backward_ref, gains_ref, out_ref, work):
    groups, chunk, channels = x_ref.shape
    total = groups * chunk
    latitudes = total // 8
    for third in range(channels // 128):
        lanes = slice(128 * third, 128 * (third + 1))
        work[third] = x_ref[:, :, lanes].astype(F32).reshape(total, 128)
        gains = gains_ref[:, lanes]
        gains = jnp.concatenate([gains, gains], axis=1)
        for m in range(4):
            real, imaginary = (pl.ds(2 * m + r, latitudes, stride=8) for r in (0, 1))
            own = jnp.concatenate(
                [work[third, real, :], work[third, imaginary, :]], axis=1
            ).astype(BF16)
            coefficients = jnp.dot(forward_ref[m], own, preferred_element_type=F32)
            shaped = (coefficients * gains).astype(BF16)
            back = jnp.dot(backward_ref[m], shaped, preferred_element_type=F32)
            work[third, real, :] = back[:, :128]
            work[third, imaginary, :] = back[:, 128:]
        out_ref[:, :, lanes] = work[third].reshape(groups, chunk, 128).astype(BF16)


def ocean_kernel(first, depth_ref, *refs):
    pieces, (weight_ref, out_ref, columns) = refs[:-3], refs[-3:]
    masks = tap_masks(CELLS)
    level = lax.broadcasted_iota(jnp.int32, (OCH, CELLS), 0) % LEV
    hidden_channels = weight_ref.shape[0]
    for slot in range(CAP * len(pieces)):
        lanes = slice(CELLS * slot, CELLS * (slot + 1))
        state = pieces[slot // CAP][slot % CAP].astype(F32)
        out_ref[hidden_channels:, lanes] = jnp.broadcast_to(state[0:1], (8, CELLS))
        state = jnp.where(level < depth_ref[first + slot], state, 0.0)
        state = jnp.concatenate([state, jnp.zeros((OCH_PAD - OCH, CELLS), F32)], axis=0)
        for q, tap in enumerate(TAPS):
            moved = shifted(state, tap, masks[q]).astype(BF16)
            columns[OCH_PAD * q : OCH_PAD * (q + 1), lanes] = moved
    for at in range(0, out_ref.shape[1], 256):
        out_ref[:hidden_channels, at : at + 256] = jnp.dot(
            weight_ref[...], columns[:, at : at + 256], preferred_element_type=F32
        )


def surface_kernel(rows_ref, *refs):
    count = 8
    sources, (updated_any, tiles_ref), held, (updated_ref, flux, sst, sems, out_sems) = (
        refs[:count], refs[count : count + 2], refs[count + 2 : 2 * count + 2],
        refs[2 * count + 2 :],
    )
    leaving = []
    (
        pack_ref, skip_ref, air_ref, group_ref, forcing_weight_ref, decode_ref, far_ref, near_ref,
    ) = held
    pack_any, skip_any, air_any = sources[:3]
    rows = air_ref.shape[0]
    tables, places, fluxes = pl.ds(0, 768), pl.ds(768, 512), pl.ds(0, FC * rows)
    ordered = [
        (pack_any.at[tables], pack_ref.at[tables]),
        (skip_any.at[rows, fluxes], skip_ref.at[rows, fluxes]),
    ]
    for j in range(rows):
        ordered += [(skip_any.at[j], skip_ref.at[j]), (air_any.at[j], air_ref.at[j])]
    ordered.append((pack_any.at[places], pack_ref.at[places]))
    copies = begin(ordered + list(zip(sources, held))[3:], sems)
    after = 2 + 2 * rows
    latitude_rows, longitudes, channels = air_ref.shape
    groups = rows_ref.shape[0]
    pairs = []
    for pair in range(latitude_rows // 2):
        both = rows_ref[:, 16 * pair : 16 * (pair + 1), :].astype(F32)
        pairs.extend([both[:, :8], both[:, 8:]])
    for one in copies[:2]:
        one.wait()
    for j in range(latitude_rows):
        own = pairs[j].reshape(8 * groups, channels).astype(BF16)
        spectral = jnp.dot(pack_ref[384 : 384 + longitudes, : 8 * groups], own, preferred_element_type=F32)
        for one in copies[2 + 2 * j : 4 + 2 * j]:
            one.wait()
        mixed = gelu(spectral + skip_ref[j]).astype(BF16)
        wide = jnp.dot(mixed, pack_ref[:384, :], preferred_element_type=F32)
        updated_ref[j] = air_ref[j].astype(F32) + wide[:, :channels]
        leave = pltpu.make_async_copy(updated_ref.at[j], updated_any.at[j], out_sems.at[j])
        leave.start()
        leaving.append(leave)
        narrow = jnp.concatenate(
            [wide[:, channels:], jnp.zeros((384 - longitudes, 128), F32)], axis=0
        )
        turned = jnp.transpose(narrow)
        extra = jnp.concatenate(
            [
                skip_ref[latitude_rows, FC * j : FC * (j + 1), :longitudes],
                jnp.zeros((FC, 384 - longitudes), F32),
            ],
            axis=1,
        )
        total = turned[:FC] + turned[FC : 2 * FC] + extra
        for part in range(3):
            at = FC * (part * latitude_rows + j)
            flux[at : at + FC, :] = total[:, 128 * part : 128 * (part + 1)]
    for one in copies[after:]:
        one.wait()
    points = flux[...].astype(BF16)
    spread = jnp.concatenate(
        [
            jnp.dot(
                points, pack_ref[768 + at : 896 + at, :], preferred_element_type=F32
            )
            for at in range(0, SPAN // 4, 128)
        ],
        axis=1,
    )
    group = group_ref[...]
    forcing = jnp.zeros((FC, SPAN), F32)
    for at in range(3 * latitude_rows):
        forcing = forcing + jnp.where(group == at, spread[FC * at : FC * (at + 1), :], 0.0)
    masks = tap_masks(SPAN)
    columns = jnp.concatenate(
        [shifted(forcing, tap, masks[q]) for q, tap in enumerate(TAPS)], axis=0
    ).astype(BF16)
    hidden_channels = forcing_weight_ref.shape[0]
    split = far_ref.shape[1]
    partials = []
    for wet_ref, lanes in ((far_ref, slice(0, split)), (near_ref, slice(split, SPAN))):
        hidden = gelu(
            wet_ref[:hidden_channels, :]
            + jnp.dot(forcing_weight_ref[...], columns[:, lanes], preferred_element_type=F32)
        ).astype(BF16)
        partials.append(jnp.dot(decode_ref[...], hidden, preferred_element_type=F32))
    partial = jnp.concatenate(partials, axis=1)
    surface = jnp.concatenate(
        [ref[hidden_channels : hidden_channels + 1, :] for ref in (far_ref, near_ref)], axis=1
    )
    change = jnp.zeros((1, SPAN), F32)
    for q, tap in enumerate(TAPS):
        change = change + shifted(partial[q : q + 1, :], tap, masks[q])
    surface = surface + change
    for slot in range(SLOTS):
        sst[slot : slot + 1, :] = surface[:, CELLS * slot : CELLS * (slot + 1)]
    tiles = sst[...].astype(BF16)
    for member in range(tiles_ref.shape[0]):
        tiles_ref[member] = tiles
    for one in leaving:
        one.wait()


def imprint_kernel(
    updated_any, tiles_ref, cell_any, slot_any, imprint_ref, out_any,
    updated_ref, cell_ref, slot_ref, out_ref, sems, out_sems,
):
    rows, _, channels = updated_ref.shape
    copies = begin(
        [(cell_any, cell_ref), (slot_any, slot_ref)]
        + [(updated_any.at[j], updated_ref.at[j]) for j in range(rows)],
        sems,
    )
    tiles = tiles_ref[0]
    tripled = jnp.concatenate([tiles, tiles, tiles], axis=0)
    pieces = in_three(imprint_ref[...].reshape(1, channels))
    imprint = jnp.concatenate(
        [jnp.broadcast_to(piece, (SLOTS, channels)) for piece in pieces], axis=0
    )
    copies[0].wait()
    copies[1].wait()
    leaving = []
    for j in range(rows):
        picked = lax.dot_general(
            cell_ref[j], tripled, (((1,), (1,)), ((), ())), preferred_element_type=F32
        )
        chosen = picked.astype(BF16) * slot_ref[j]
        warmth = jnp.dot(chosen, imprint, preferred_element_type=F32)
        copies[2 + j].wait()
        out_ref[j] = (updated_ref[j] + warmth).astype(BF16)
        leave = pltpu.make_async_copy(out_ref.at[j], out_any.at[j], out_sems.at[j])
        leave.start()
        leaving.append(leave)
    for one in leaving:
        one.wait()


def mean_kernel(tiles_ref, cell_ref, slot_ref, out_ref):
    members = tiles_ref.shape[0]
    total = jnp.zeros(tiles_ref.shape[1:], F32)
    for member in range(members):
        total = total + tiles_ref[member].astype(F32)
    pieces = jnp.concatenate(in_three(total), axis=0)
    for j in range(cell_ref.shape[0]):
        picked = lax.dot_general(
            pieces, cell_ref[j], (((1,), (1,)), ((), ())), preferred_element_type=F32
        )
        joined = picked[:SLOTS] + picked[SLOTS : 2 * SLOTS] + picked[2 * SLOTS :]
        kept = jnp.where(slot_ref[j] > 0, joined, 0.0)
        out_ref[j : j + 1, :] = jnp.sum(kept, axis=0, keepdims=True) / members


def call(kernel, outs, operands, flops, scratch=(), limit=56, specs=None, out_specs=None):
    size = sum(math.prod(o.shape) * o.dtype.itemsize for o in list(outs) + list(operands))
    return pl.pallas_call(
        kernel,
        out_shape=outs if len(outs) > 1 else outs[0],
        in_specs=specs or [WHOLE] * len(operands),
        out_specs=out_specs or ([WHOLE] * len(outs) if len(outs) > 1 else WHOLE),
        scratch_shapes=list(scratch),
        compiler_params=pltpu.CompilerParams(vmem_limit_bytes=limit * 1024 * 1024),
        cost_estimate=pl.CostEstimate(
            flops=flops, bytes_accessed=min(size, flops), transcendentals=0
        ),
    )(*operands)


def held(operands):
    return [pltpu.VMEM(o.shape, o.dtype) for o in operands]


def shards(
    air_ensemble,
    sea_indicator,
    layernorm_scaling,
    harmonic_damping_factor,
    bypass_factor,
    core_exit_factor,
    air_to_exchange_factor,
    sea_heat_imprint,
    sea_ensemble_arrays,
    input_to_hidden_kernel,
    hidden_to_change_kernel,
    patch_exchange_pick,
    node_sea_pick,
    patch_holder_shift,
    wet_depth_layers,
):
    bands = lax.axis_size("space")
    members = lax.axis_size("member")
    air = air_ensemble[0]
    latitude_rows, longitudes, channels = air.shape
    latitudes = latitude_rows * bands
    hidden_channels = input_to_hidden_kernel.shape[1]
    per_device = MMAX // bands
    chunk = 2 * per_device * latitude_rows
    shape = jax.ShapeDtypeStruct

    analysis, synthesis = (jnp.asarray(t) for t in fourier_tables())
    spectra = call(
        analysis_kernel,
        [shape((bands, chunk, channels), BF16)],
        [air, layernorm_scaling, analysis],
        2 * 2 * MMAX * latitude_rows * longitudes * channels,
        held([air, analysis])
        + [
            pltpu.VMEM((bands, chunk, channels), BF16),
            pltpu.SemaphoreType.DMA((latitude_rows + 1,)),
            pltpu.SemaphoreType.DMA((latitude_rows // 2,)),
        ],
        specs=[FAR, WHOLE, FAR],
        out_specs=FAR,
    )
    gathered = lax.all_to_all(spectra, "space", split_axis=0, concat_axis=0, tiled=True)

    slots = sea_ensemble_arrays[0]
    far = [
        passed_along(slots[offset * CAP : (offset + 1) * CAP], "space", -offset)
        for offset in range(EARLY, NEAR)
    ]
    forward, backward = (jnp.asarray(t) for t in legendre_tables(latitudes))
    first = lax.axis_index("space") * per_device
    forward = lax.dynamic_slice_in_dim(forward, first, per_device, 0)
    backward = lax.dynamic_slice_in_dim(backward, first, per_device, 0)
    offsets = patch_holder_shift[:, 0]
    earlier = jnp.tril(jnp.ones((HOME_DEV, HOME_DEV), jnp.int32), -1)
    positions = jnp.sum((offsets[:, None] == offsets[None, :]).astype(jnp.int32) * earlier, axis=1)
    places = jnp.where(offsets >= EARLY, offsets - EARLY + 1, offsets + NEAR - EARLY)
    targets = jnp.where(offsets == 0, 0, places) * CAP + positions
    selected = targets[None, :] == jnp.arange(SLOTS, dtype=jnp.int32)[:, None]
    depths = jnp.sum(jnp.where(selected, wet_depth_layers[None, :], 0), axis=1)
    kernel = jnp.transpose(input_to_hidden_kernel, (1, 0, 2))
    state_weight = jnp.pad(kernel[:, :, :OCH], ((0, 0), (0, 0), (0, OCH_PAD - OCH))).reshape(
        hidden_channels, -1
    )
    forcing_weight = kernel[:, :, OCH:].reshape(hidden_channels, -1)
    decode_weight = jnp.pad(hidden_to_change_kernel, ((0, 16 - len(TAPS)), (0, 0)))
    picks = jnp.sum(jnp.where(selected[:, :, None], patch_exchange_pick[None], 0), axis=1)
    picks = picks.reshape(1, SPAN)
    line, column = picks // longitudes, picks % longitudes
    group = column // 128 * latitude_rows + line
    place = (column % 128 == jnp.arange(128, dtype=jnp.int32)[:, None]).astype(BF16)
    skip, pack = call(
        local_kernel,
        [shape((latitude_rows + 1, longitudes, channels), F32), shape((1280, 512), BF16)],
        [
            air, layernorm_scaling, bypass_factor, core_exit_factor, air_to_exchange_factor.T,
            synthesis, place,
        ],
        SMALL,
        held([air]) + [pltpu.SemaphoreType.DMA((latitude_rows,))],
        specs=[FAR] + [WHOLE] * 6,
    )
    tile = node_sea_pick // CELLS
    holder = jnp.sum(
        jnp.where(
            tile[:, :, None] == jnp.arange(HOME_DEV, dtype=jnp.int32), targets[None, None, :], 0
        ),
        axis=2,
    )
    holder = jnp.where(sea_indicator > 0, holder, -1)
    cell = (
        (node_sea_pick % CELLS)[:, :, None] == jnp.arange(CELLS, dtype=jnp.int32)
    ).astype(BF16)
    slot_of = (
        holder[:, :, None] == jnp.arange(3 * SLOTS, dtype=jnp.int32) % SLOTS
    ).astype(BF16)
    slot_rows = (
        holder[:, None, :] == jnp.arange(SLOTS, dtype=jnp.int32)[None, :, None]
    ).astype(F32)
    filtered = call(
        legendre_kernel,
        [shape((bands, chunk, channels), BF16)],
        [gathered, forward, backward, harmonic_damping_factor],
        2 * 2 * 2 * per_device * LMAX * latitudes * channels,
        [pltpu.VMEM((channels // 128, bands * chunk, 128), F32)],
        limit=32,
    )
    filtered, late = lax.optimization_barrier((filtered, slots[CAP : EARLY * CAP]))
    returned = lax.all_to_all(filtered, "space", split_axis=0, concat_axis=0, tiled=True)
    near = [
        passed_along(late[at : at + CAP], "space", -(1 + at // CAP))
        for at in range(0, late.shape[0], CAP)
    ]
    def wet(first, parts):
        width = CAP * CELLS * len(parts)
        return call(
            functools.partial(ocean_kernel, first),
            [shape((hidden_channels + 8, width), F32)],
            [depths, *parts, state_weight],
            SMALL,
            [pltpu.VMEM((len(TAPS) * OCH_PAD, width), BF16)],
            limit=32,
            specs=[pl.BlockSpec(memory_space=pltpu.SMEM)] + [WHOLE] * (len(parts) + 1),
        )

    wet_far = wet(0, [slots[:CAP], *far])
    wet_near = wet(CAP * (len(far) + 1), near)
    operands = [pack, skip, air, group, forcing_weight, decode_weight, wet_far, wet_near]
    updated, tiles = call(
        surface_kernel,
        [shape(air.shape, F32), shape((members, SLOTS, CELLS), BF16)],
        [returned] + operands,
        2 * latitude_rows * longitudes * channels * (channels + 2 * MMAX),
        held(operands)
        + [
            pltpu.VMEM(air.shape, F32),
            pltpu.VMEM((3 * FC * latitude_rows, 128), F32),
            pltpu.VMEM((SLOTS, CELLS), F32),
            pltpu.SemaphoreType.DMA((len(operands) + 2 * latitude_rows + 1,)),
            pltpu.SemaphoreType.DMA((latitude_rows,)),
        ],
        limit=52,
        specs=[WHOLE] + [FAR] * len(operands),
        out_specs=[FAR, WHOLE],
    )
    everyone = lax.all_to_all(tiles, "member", split_axis=0, concat_axis=0, tiled=True)
    out = call(
        imprint_kernel,
        [shape(air.shape, BF16)],
        [updated, tiles, cell, slot_of, sea_heat_imprint],
        2 * latitude_rows * longitudes * channels * 256,
        held([updated, cell, slot_of, air])
        + [
            pltpu.SemaphoreType.DMA((latitude_rows + 2,)),
            pltpu.SemaphoreType.DMA((latitude_rows,)),
        ],
        specs=[FAR, WHOLE, FAR, FAR, WHOLE],
        out_specs=FAR,
    )
    mean = call(
        mean_kernel,
        [shape((latitude_rows, longitudes), F32)],
        [everyone, cell, slot_rows],
        2 * 3 * SLOTS * CELLS * latitude_rows * longitudes,
        limit=32,
    )
    return (out[None], mean)


def solution(mesh):
    in_specs = (
        P("member", "space", None, None),
        P("space", None),
        P(),
        P(),
        P(),
        P(),
        P(),
        P(),
        P("member", "space", None, None),
        P(),
        P(),
        P("space", None),
        P("space", None),
        P("space", None),
        P("space"),
    )
    out_specs = (P("member", "space", None, None), P("space", None))
    return jax.shard_map(shards, mesh=mesh, in_specs=in_specs, out_specs=out_specs, check_vma=False)
```
